256 devices in a mesh: clip: 2 (over x_hi), frame: 4 (over y), row: 32 (over x_lo, z, core).
Axes of the slice: x: 4 (x_hi: 2, x_lo: 2; x = x_hi * 2 + x_lo), y: 4, z: 8, core: 2. Of those that a mesh axis runs over, the one named last changes fastest.
Arguments:
- x_input: bfloat16 [2, 4, 256, 120, 128], P('clip', 'frame', 'row'), may hold values from -12 to 12
- d_output: bfloat16 [2, 4, 256, 120, 128], P('clip', 'frame', 'row'), may hold values from -8 to 8
- gain_one: float32 [120], replicated, may hold values from 0.1 to 1.9
- w_self: bfloat16 [120, 360], replicated, may hold values from -0.5 to 0.5
- w_mutual: bfloat16 [120, 360], replicated, may hold values from -0.5 to 0.5
- w_proj: bfloat16 [240, 120], replicated, may hold values from -0.375 to 0.375
- gain_two: float32 [120], replicated, may hold values from 0.1 to 1.9
- w_fc_one: bfloat16 [120, 240], replicated, may hold values from -0.5 to 0.5
- w_fc_two: bfloat16 [120, 240], replicated, may hold values from -0.5 to 0.5
- w_down: bfloat16 [240, 120], replicated, may hold values from -0.375 to 0.375
Outputs:
- grad_input: bfloat16 [2, 4, 256, 120, 128], P('clip', 'frame', 'row')
- grad_gain_one: float32 [120], replicated
- grad_w_self: float32 [120, 360], replicated
- grad_w_mutual: float32 [120, 360], replicated
- grad_w_proj: float32 [240, 120], replicated
- grad_gain_two: float32 [120], replicated
- grad_fc_one: float32 [120, 240], replicated
- grad_fc_two: float32 [120, 240], replicated
- grad_w_down: float32 [240, 120], replicated
The draws below stay inside these ranges and needn't reach their ends.
All inputs are finite; a program needn't handle non-finite values.
Results may differ from the reference program's by a relative error of at most 0.013.
Values may be sent and summed in bfloat16 or wider, within the bound.
A program may use at most 128 MiB of HBM per device.

```python
import jax
import jax.numpy as jnp
from jax import lax

C = 120
HEADS = 6
MLP = 240
W = 128
CLIPS = 2
FRAMES = 4
H = 256


def draw_x_input(key, part):
    key = jax.random.fold_in(key, 11)
    key_noise, key_chan, key_token = jax.random.split(key, 3)
    shape_all = (CLIPS, FRAMES, H, C, W)
    chan_scale = jnp.exp(jax.random.uniform(key_chan, (C, 1), jnp.float32, jnp.log(0.3), jnp.log(3.0)))
    token_scale = jnp.exp(jax.random.uniform(key_token, (CLIPS, FRAMES, H, 1, W), jnp.float32, jnp.log(0.3), jnp.log(3.0)))
    noise = jax.random.normal(key_noise, shape_all, jnp.float32)
    return jnp.clip(noise * chan_scale * token_scale, -12.0, 12.0).astype(jnp.bfloat16)


def draw_d_output(key, part):
    key = jax.random.fold_in(key, 23)
    key_noise = jax.random.fold_in(key, 0)
    shape_all = (CLIPS, FRAMES, H, C, W)
    rising = 0.5 + jnp.arange(H, dtype=jnp.float32)[:, None, None] / H
    noise = jax.random.normal(key_noise, shape_all, jnp.float32)
    return jnp.clip(noise * rising, -8.0, 8.0).astype(jnp.bfloat16)


def centred(rng, extent, scale, bound, kind=jnp.bfloat16):
    result = jax.random.normal(rng, extent, jnp.float32) * scale
    return jnp.minimum(jnp.maximum(result, -bound), bound).astype(kind)


def setup_inputs(seed: int = 0) -> dict:
    seeds = jax.random.split(jax.random.key(seed), 11)
    x_input = draw_x_input(jax.random.fold_in(seeds[10], 71), 0)
    d_output = draw_d_output(jax.random.fold_in(seeds[10], 71), 0)
    gain_one = jnp.clip(1.0 + 0.18 * jax.random.normal(seeds[2], (C,), jnp.float32), 0.1, 1.9)
    w_self = centred(seeds[3], (C, 3 * C), C ** -0.5, 0.5)
    w_mutual = centred(seeds[4], (C, 3 * C), C ** -0.5, 0.5)
    w_proj = centred(seeds[5], (2 * C, C), (2 * C) ** -0.5, 0.375)
    gain_two = jnp.clip(1.0 + 0.18 * jax.random.normal(seeds[6], (C,), jnp.float32), 0.1, 1.9)
    w_fc_one = centred(seeds[7], (C, MLP), C ** -0.5, 0.5)
    w_fc_two = centred(seeds[8], (C, MLP), C ** -0.5, 0.5)
    w_down = centred(seeds[9], (MLP, C), MLP ** -0.5, 0.375)
    return {"x_input": x_input, "d_output": d_output, "gain_one": gain_one, "w_self": w_self, "w_mutual": w_mutual, "w_proj": w_proj, "gain_two": gain_two, "w_fc_one": w_fc_one, "w_fc_two": w_fc_two, "w_down": w_down}


norm_eps = 1e-05

def product(pattern, left_side, right_side):
    left_wide = lax.optimization_barrier(left_side).astype(jnp.float32)
    right_wide = lax.optimization_barrier(right_side).astype(jnp.float32)
    return jnp.einsum(pattern, left_wide, right_wide)

def to_float(tensor):
    return lax.optimization_barrier(tensor).astype(jnp.float32)

def layer_norm(values, gain_vec):
    centre = values - lax.optimization_barrier(jnp.mean(values, axis=-2, keepdims=True))
    spread = lax.optimization_barrier(jnp.mean(centre * centre, axis=-2, keepdims=True))
    return centre * lax.rsqrt(spread + norm_eps) * gain_vec[:, None]

def gelu_exact(inputs_in):
    return jax.nn.gelu(inputs_in, approximate=False)

def to_windows(tensor):
    leading = tensor.shape[:-3]
    row_count, channels, col_count = tensor.shape[-3:]
    lead_dims = len(leading)
    blocked = tensor.reshape(leading + (row_count // 8, 8, HEADS, channels // HEADS, col_count // 8, 8))
    permuted = list(range(lead_dims)) + [lead_dims, lead_dims + 4, lead_dims + 2, lead_dims + 1, lead_dims + 5, lead_dims + 3]
    return blocked.transpose(permuted).reshape(leading + (row_count // 8, col_count // 8, HEADS, 64, channels // HEADS))

def from_windows(tensor, row_count, col_count):
    leading = tensor.shape[:-5]
    lead_dims = len(leading)
    head_size = tensor.shape[-1]
    blocked = tensor.reshape(leading + (row_count // 8, col_count // 8, HEADS, 8, 8, head_size))
    permuted = list(range(lead_dims)) + [lead_dims, lead_dims + 3, lead_dims + 2, lead_dims + 5, lead_dims + 1, lead_dims + 4]
    return blocked.transpose(permuted).reshape(leading + (row_count, HEADS * head_size, col_count))

def softmax_mix(queries, key_rows, value_rows, scale_factor):
    scores = product('...qd,...kd->...qk', queries, key_rows) * scale_factor
    raised = jnp.exp(scores)
    softmaxed = (raised / lax.optimization_barrier(jnp.sum(raised, axis=-1, keepdims=True))).astype(jnp.bfloat16)
    return product('...qk,...kd->...qd', softmaxed, value_rows)

def attend(own_four, part_four):
    channels = own_four.shape[-2] // 4
    row_count = own_four.shape[-3]
    col_count = own_four.shape[-1]
    scale_factor = float(channels // HEADS) ** (-0.5)
    own_parts = [to_windows(own_four[..., block_id * channels:(block_id + 1) * channels, :]) for block_id in range(4)]
    part_parts = [to_windows(part_four[..., block_id * channels:(block_id + 1) * channels, :]) for block_id in range(4)]
    query_self, key_self, value_self, query_cross = own_parts
    key_pair, value_pair, key_cross, value_cross = part_parts
    out_self = softmax_mix(query_self, jnp.concatenate([key_self, key_pair], axis=-2), jnp.concatenate([value_self, value_pair], axis=-2), scale_factor)
    out_cross = softmax_mix(query_cross, key_cross, value_cross, scale_factor)
    joined = jnp.concatenate([from_windows(out_cross, row_count, col_count), from_windows(out_self, row_count, col_count)], axis=-2)
    return joined.astype(jnp.bfloat16)

def attend_back(inputs_in):
    own_band, part_band, grad_band = inputs_in
    _, pullback = jax.vjp(attend, own_band, part_band)
    return pullback(grad_band)

def to_bands(tensor):
    blocked = tensor.reshape((tensor.shape[0], tensor.shape[1] // 8, 8) + tensor.shape[2:])
    return jnp.swapaxes(blocked, 0, 1)

def from_bands(tensor):
    merged = jnp.swapaxes(tensor, 0, 1)
    return merged.reshape((merged.shape[0], merged.shape[1] * 8) + merged.shape[3:])

def assemble_grads(grad_own, grad_part, channels):
    zeros_block = jnp.zeros((channels, channels), jnp.float32)
    grad_self = grad_own[:, :3 * channels] + jnp.concatenate([zeros_block, grad_part[:, :2 * channels]], axis=1)
    grad_mutual = jnp.concatenate([grad_own[:, 3 * channels:], grad_part[:, 2 * channels:]], axis=1)
    return (grad_self, grad_mutual)

def one_pair(x_pair, grad_pair, gain_one, w_self, w_mutual, w_proj, gain_two, w_fc_one, w_fc_two, w_down):
    channels = x_pair.shape[2]
    x_float = x_pair.astype(jnp.float32)
    normed = layer_norm(x_float, gain_one).astype(jnp.bfloat16)
    shifted = jnp.roll(normed, (-4, -4), axis=(1, 3))
    partner = shifted[::-1]
    w_own = jnp.concatenate([w_self, w_mutual[:, :channels]], axis=1)
    w_part = jnp.concatenate([w_self[:, channels:], w_mutual[:, channels:]], axis=1)
    own_four = product('fhcw,cd->fhdw', shifted, w_own).astype(jnp.bfloat16)
    part_four = product('fhcw,cd->fhdw', partner, w_part).astype(jnp.bfloat16)
    own_bands = to_bands(own_four)
    part_bands = to_bands(part_four)
    joined = from_bands(lax.map(lambda pair_in: attend(pair_in[0], pair_in[1]), (own_bands, part_bands)))
    attention = product('fhcw,cd->fhdw', joined, w_proj).astype(jnp.bfloat16)
    attn_back = jnp.roll(attention, (4, 4), axis=(1, 3))
    hidden_in = x_float + to_float(attn_back)
    normed_two = layer_norm(hidden_in, gain_two).astype(jnp.bfloat16)
    up_one = product('fhcw,cd->fhdw', normed_two, w_fc_one)
    up_two = product('fhcw,cd->fhdw', normed_two, w_fc_two)
    gelu_value, gelu_back = jax.vjp(gelu_exact, up_one)
    hidden = (gelu_value * up_two).astype(jnp.bfloat16)
    grad_down = product('fhcw,fhdw->cd', hidden, grad_pair)
    d_hidden = to_float(product('fhdw,cd->fhcw', grad_pair, w_down).astype(jnp.bfloat16))
    d_up_one = gelu_back(d_hidden * up_two)[0].astype(jnp.bfloat16)
    d_up_two = (d_hidden * gelu_value).astype(jnp.bfloat16)
    grad_fc_one = product('fhcw,fhdw->cd', normed_two, d_up_one)
    grad_fc_two = product('fhcw,fhdw->cd', normed_two, d_up_two)
    d_normed_two = (product('fhdw,cd->fhcw', d_up_one, w_fc_one) + product('fhdw,cd->fhcw', d_up_two, w_fc_two)).astype(jnp.bfloat16)
    _, norm_back_two = jax.vjp(layer_norm, hidden_in, gain_two)
    d_hidden_in, grad_gain_two = norm_back_two(to_float(d_normed_two))
    d_resid = grad_pair.astype(jnp.float32) + d_hidden_in
    d_attention = jnp.roll(d_resid.astype(jnp.bfloat16), (-4, -4), axis=(1, 3))
    grad_proj = product('fhcw,fhdw->cd', joined, d_attention)
    d_joined = product('fhdw,cd->fhcw', d_attention, w_proj).astype(jnp.bfloat16)
    d_own_bands, d_part_bands = lax.map(attend_back, (own_bands, part_bands, to_bands(d_joined)))
    d_own = from_bands(d_own_bands)
    d_part = from_bands(d_part_bands)
    grad_own = product('fhcw,fhdw->cd', shifted, d_own)
    grad_part = product('fhcw,fhdw->cd', partner, d_part)
    d_from_own = product('fhdw,cd->fhcw', d_own, w_own).astype(jnp.bfloat16)
    d_from_part = product('fhdw,cd->fhcw', d_part, w_part).astype(jnp.bfloat16)
    d_shifted = (to_float(d_from_own) + to_float(d_from_part[::-1])).astype(jnp.bfloat16)
    d_normed = jnp.roll(d_shifted, (4, 4), axis=(1, 3))
    _, norm_back_one = jax.vjp(layer_norm, x_float, gain_one)
    d_x_norm, grad_gain_one = norm_back_one(to_float(d_normed))
    grad_input = (d_resid + d_x_norm).astype(jnp.bfloat16)
    grad_self, grad_mutual = assemble_grads(grad_own, grad_part, channels)
    return (grad_input, (grad_gain_one, grad_self, grad_mutual, grad_proj, grad_gain_two, grad_fc_one, grad_fc_two, grad_down))

def reference(x_input, d_output, gain_one, w_self, w_mutual, w_proj, gain_two, w_fc_one, w_fc_two, w_down):
    clip_count, frame_count, row_count, channels, col_count = x_input.shape
    pair_shape = (clip_count * frame_count // 2, 2, row_count, channels, col_count)

    def run_pair(inputs_in):
        return one_pair(inputs_in[0], inputs_in[1], gain_one, w_self, w_mutual, w_proj, gain_two, w_fc_one, w_fc_two, w_down)
    grad_pairs, grad_parts = lax.map(run_pair, (x_input.reshape(pair_shape), d_output.reshape(pair_shape)))
    scale_factor = float(clip_count * frame_count * row_count * col_count) ** (-0.5)
    summed = [lax.optimization_barrier(jnp.sum(stacked, axis=0)) * scale_factor for stacked in grad_parts]
    return (grad_pairs.reshape(x_input.shape), summed[0], summed[1], summed[2], summed[3], summed[4], summed[5], summed[6], summed[7])
```

```python
import math

import jax
import jax.numpy as jnp
from jax import lax
from jax.experimental import pallas as pl
from jax.experimental.pallas import tpu as pltpu
from jax.sharding import PartitionSpec as P

F32 = jnp.float32
BF16 = jnp.bfloat16
MESH = pl.DeviceIdType.MESH

C = 120
L = 128
W = 128
HEADS = 6
HD = 20
MLP = 240
M = 256
T = 1024
CH = 256
EPS = 1e-05
EXP_SCALE = float(HD) ** -0.5 * math.log2(math.e)
SCALE = float(HD) ** -0.5

EARLY = 8 * L
LATE = 6 * L
ROWS = 2048


def nn(a, b):
    return lax.dot_general(a, b, (((1,), (0,)), ((), ())), preferred_element_type=F32)


def nt(a, b):
    return lax.dot_general(a, b, (((1,), (1,)), ((), ())), preferred_element_type=F32)


def iota(shape, dim):
    return lax.broadcasted_iota(jnp.int32, shape, dim)


def one_hot(mask):
    return jnp.where(mask, 1.0, 0.0).astype(BF16)


def pad_rows(v):
    return jnp.concatenate([v, jnp.zeros((L - C, v.shape[1]), F32)], axis=0).astype(BF16)


def norm_parts(v):
    mean = jnp.sum(v, axis=0, keepdims=True) * (1.0 / C)
    centre = v - mean
    var = jnp.sum(centre * centre, axis=0, keepdims=True) * (1.0 / C)
    inv = lax.rsqrt(var + EPS)
    return centre * inv, inv


def norm_back(xhat, inv, gain, dy):
    dh = dy * gain
    m1 = jnp.sum(dh, axis=0, keepdims=True) * (1.0 / C)
    m2 = jnp.sum(dh * xhat, axis=0, keepdims=True) * (1.0 / C)
    return inv * (dh - m1 - xhat * m2)


def gain_row(acc):
    full = jnp.concatenate([acc, jnp.zeros((L - C, L), F32)], axis=0)
    row = jnp.sum(jnp.transpose(full), axis=0, keepdims=True)
    return jnp.broadcast_to(row, (8, L))


def fold_lanes(v):
    out = v[:, :L]
    for i in range(1, v.shape[1] // L):
        out = out + v[:, i * L : (i + 1) * L]
    return out


def make_perm(perm):
    o = iota((256, T), 1)
    v, r, j = o >> 6, (o >> 3) & 7, o & 7
    src = r * W + ((v * 8 + j + 4) & (W - 1))
    for i in range(T // 256):
        perm[pl.ds(i * 256, 256), :] = one_hot(iota((256, T), 0) + i * 256 == src)


def make_masks(mask_q, mask_v, mask_x):
    row, lane = iota((2 * L, HEADS * L), 0), iota((2 * L, HEADS * L), 1)
    c, h = row & (L - 1), lane >> 7
    head = (c >= h * HD) & (c < h * HD + HD)
    mask_q[...] = one_hot(head & ((row >> 7) == ((lane >> 6) & 1)))
    mask_v[...] = one_hot(head[:L])
    row, lane = iota((L, HEADS * 64), 0), iota((L, HEADS * 64), 1)
    h = lane >> 6
    mask_x[...] = one_hot((row >= h * HD) & (row < h * HD + HD))


def make_weights(ws, wm, wp, f1, f2, wd, wn, wt, proj, proj_t, fc_n, fc_t, down):
    def rows128(ref):
        return pad_rows(ref[...].astype(F32))

    r, e = iota((3 * L, 3 * C), 0), iota((3 * L, 3 * C), 1)
    pad3 = one_hot((e == (r >> 7) * C + (r & (L - 1))) & ((r & (L - 1)) < C))
    for i, ref in enumerate((ws, wm)):
        w = rows128(ref)
        wt[pl.ds(i * 3 * L, 3 * L), :] = nt(pad3, w).astype(BF16)
        wn[:, pl.ds(i * 3 * L, 3 * L)] = nt(w, pad3).astype(BF16)
    r, e = iota((M, MLP), 0), iota((M, MLP), 1)
    pad_m = one_hot(r == e)
    pad2 = one_hot((e == (r >> 7) * C + (r & (L - 1))) & ((r & (L - 1)) < C))
    pad_l = one_hot(iota((C, L), 0) == iota((C, L), 1))
    eye = one_hot(iota((L, L), 0) == iota((L, L), 1))
    for i, ref in enumerate((f1, f2)):
        w = rows128(ref)
        fc_t[pl.ds(i * M, M), :] = nt(pad_m, w).astype(BF16)
        fc_n[:, pl.ds(i * M, M)] = nt(w, pad_m).astype(BF16)
    down[...] = nn(nn(pad_m, wd[...]).astype(BF16), pad_l).astype(BF16)
    padded = nn(nn(pad2, wp[...]).astype(BF16), pad_l).astype(BF16)
    proj[...] = padded
    proj_t[...] = nt(eye, padded).astype(BF16)


def make_gain(gain, col):
    col[...] = jnp.transpose(jnp.broadcast_to(gain[...], (L, C)))


def wide(col):
    return jnp.concatenate([col[...]] * (CH // L), axis=1)


def to_slab(slab, index, rows_ref, first):
    for i in range(rows_ref.shape[0]):
        slab[pl.ds(index * L, C), pl.ds((first + i) * W, W)] = rows_ref[i]


def norm_one(win, base, gain_col, out_cm, out_tm):
    gain = wide(gain_col)

    def step(i, carry):
        at = pl.ds(pl.multiple_of(i * CH, CH), CH)
        x = win[pl.ds(base, L), at].astype(F32)[:C]
        y = norm_parts(x)[0] * gain
        y = jnp.concatenate([y, jnp.zeros((L - C, CH), F32)], axis=0)
        out_cm[:, at] = y.astype(BF16)
        out_tm[at, :] = jnp.transpose(y).astype(BF16)
        return carry

    lax.fori_loop(0, T // CH, step, 0)


def project_own(wt, wn, cm, tm, own_cm, own_tm):
    own_cm[...] = nn(wt[pl.ds(0, 4 * L), :], cm[...]).astype(BF16)
    own_tm[...] = nn(tm[...], wn[:, pl.ds(L, 2 * L)]).astype(BF16)


def project_part(wt, wn, cm, tm, part_cm, part_tm):
    for i, first in enumerate((L, 4 * L)):
        part_cm[pl.ds(i * 2 * L, 2 * L), :] = nn(wt[pl.ds(first, 2 * L), :], cm[...]).astype(BF16)
        part_tm[:, pl.ds(i * 2 * L, 2 * L)] = nn(tm[...], wn[:, pl.ds(first, 2 * L)]).astype(BF16)


def spread(v, mask_q):
    v6 = jnp.concatenate([v] * HEADS, axis=1)
    return jnp.concatenate([v6, v6], axis=0) * mask_q[...]


def keys_self(own, part):
    top = jnp.concatenate([own[:64], part[64:]], axis=1)
    return jnp.concatenate([top, jnp.concatenate([part[:64], own[64:]], axis=1)], axis=0)


def keys_cross(part):
    return jnp.concatenate([part[:64], part[64:]], axis=1)


def halves(a, b):
    return jnp.where(iota(a.shape, 1) < 64, a, b)


def spread_self(own, part, mask_v):
    own, part = own.astype(F32), pltpu.roll(part.astype(F32), 64, 1)
    both = (halves(own, part).astype(BF16), halves(part, own).astype(BF16))
    return jnp.concatenate(
        [jnp.concatenate([v] * HEADS, axis=1) * mask_v[...] for v in both], axis=0
    )


def spread_cross(part, mask_x):
    part = part.astype(F32)
    moved = pltpu.roll(part, 64, 1)
    both = (halves(part, moved).astype(BF16), halves(moved, part).astype(BF16))
    return jnp.concatenate(
        [jnp.concatenate([v] * (HEADS // 2), axis=1) * mask_x[...] for v in both], axis=0
    )


def stacked(v):
    return jnp.concatenate([v[:, h * L : (h + 1) * L] for h in range(HEADS)], axis=0)


def mix(spread_values, weights):
    both = nn(spread_values, stacked(weights))
    return halves(both[:L], both[L:])


def softmax(scores):
    raised = jnp.exp2(scores * EXP_SCALE)
    return (raised * (1.0 / jnp.sum(raised, axis=0, keepdims=True))).astype(BF16)


def attend(own_cm, own_tm, part_cm, part_tm, mask_q, mask_v, mask_x, probs, joined):
    def step(p, carry):
        at = pl.ds(pl.multiple_of(p * L, L), L)
        q = spread(own_cm[pl.ds(0, L), at], mask_q)
        k = keys_self(own_tm[at, pl.ds(0, L)], part_tm[at, pl.ds(0, L)])
        pr = softmax(nn(k, q))
        probs[p, pl.ds(0, L), :] = pr
        v = spread_self(own_cm[pl.ds(2 * L, L), at], part_cm[pl.ds(L, L), at], mask_v)
        joined[pl.ds(L, L), at] = mix(v, pr).astype(BF16)
        q = spread(own_cm[pl.ds(3 * L, L), at], mask_q)
        pr = softmax(nn(keys_cross(part_tm[at, pl.ds(2 * L, L)]), q))
        probs[p, pl.ds(L, 64), :] = pr
        v = spread_cross(part_cm[pl.ds(3 * L, L), at], mask_x)
        joined[pl.ds(0, L), at] = mix(v, pr).astype(BF16)
        return carry

    lax.fori_loop(0, T // L, step, 0)


def score_back(pr, d_pr):
    pr = pr.astype(F32)
    delta = jnp.sum(pr * d_pr, axis=0, keepdims=True)
    return (pr * (d_pr - delta)).astype(BF16)


def attend_back(
    own_cm, own_tm, part_cm, part_tm, mask_q, mask_v, mask_x, probs, dj, dq, d_own, d_part
):
    def step(p, carry):
        start = pl.multiple_of(p * L, L)
        at = pl.ds(start, L)
        first, second = pl.ds(start, 64), pl.ds(pl.multiple_of(start + 64, 64), 64)
        pr = probs[p, pl.ds(0, L), :]
        do = spread(dj[pl.ds(L, L), at], mask_q)
        v = keys_self(own_tm[at, pl.ds(L, L)], part_tm[at, pl.ds(L, L)])
        ds = score_back(pr, nn(v, do))
        k = spread_self(own_cm[pl.ds(L, L), at], part_cm[pl.ds(0, L), at], mask_v)
        dq[pl.ds(0, L), at] = (mix(k, ds) * SCALE).astype(BF16)
        q = spread(own_cm[pl.ds(0, L), at], mask_q)
        for i, d in enumerate((nt(ds, q) * SCALE, nt(pr, do))):
            d = d.astype(BF16)
            d_own[first, pl.ds(i * L, L)] = d[:64, :L]
            d_own[second, pl.ds(i * L, L)] = d[64:, L:]
            d_part[first, pl.ds(i * L, L)] = d[64:, :L]
            d_part[second, pl.ds(i * L, L)] = d[:64, L:]
        pr = probs[p, pl.ds(L, 64), :]
        do = spread(dj[pl.ds(0, L), at], mask_q)
        v = keys_cross(part_tm[at, pl.ds(3 * L, L)])
        ds = score_back(pr, nn(v, do))
        k = spread_cross(part_cm[pl.ds(2 * L, L), at], mask_x)
        dq[pl.ds(L, L), at] = (mix(k, ds) * SCALE).astype(BF16)
        q = spread(own_cm[pl.ds(3 * L, L), at], mask_q)
        for i, d in enumerate((nt(ds, q) * SCALE, nt(pr, do))):
            d = d.astype(BF16)
            d_part[first, pl.ds((2 + i) * L, L)] = d[:, :L]
            d_part[second, pl.ds((2 + i) * L, L)] = d[:, L:]
        return carry

    lax.fori_loop(0, T // L, step, 0)


def feed_forward(
    win, joined, gain_col, proj, proj_t, fc_n, fc_t, down, hid, dup, n2, datt, dres, dj, acc
):
    gain = wide(gain_col)
    acc[...] = jnp.zeros_like(acc)

    def step(i, carry):
        at = pl.ds(pl.multiple_of(i * CH, CH), CH)
        att = nn(proj_t[...], joined[:, at]).astype(BF16).astype(F32)
        xhat, inv = norm_parts(win[pl.ds(0, L), at].astype(F32)[:C] + att[:C])
        normed = pad_rows(xhat * gain)
        n2[:, at] = normed
        up = nn(fc_t[...], normed)
        up_one, up_two = up[:M], up[M:]
        cdf = 0.5 * (1.0 + lax.erf(up_one * math.sqrt(0.5)))
        gelu = up_one * cdf
        slope = cdf + up_one * (
            jnp.exp2(up_one * up_one * (-0.5 * math.log2(math.e))) * (1.0 / math.sqrt(2.0 * math.pi))
        )
        hid[:, at] = (gelu * up_two).astype(BF16)
        grad = win[pl.ds(L, L), at]
        d_hid = nn(down[...], grad).astype(BF16).astype(F32)
        d_up = jnp.concatenate(
            [(d_hid * up_two * slope).astype(BF16), (d_hid * gelu).astype(BF16)], axis=0
        )
        dup[:, at] = d_up
        dn = nn(fc_n[...], d_up).astype(BF16).astype(F32)[:C]
        acc[...] += fold_lanes(dn * xhat)
        d_resid = grad.astype(F32)[:C] + norm_back(xhat, inv, gain, dn)
        dres[:, at] = d_resid
        da = pad_rows(d_resid)
        datt[:, at] = da
        dj[:, at] = nn(proj[...], da).astype(BF16)
        return carry

    lax.fori_loop(0, T // CH, step, 0)


def early_grads(hid, dup, n2, joined, datt, win, acc, pack):
    g = nt(hid[...], win[pl.ds(L, L), :])
    row = gain_row(acc[...])
    g = jnp.concatenate([g[:MLP], row, row], axis=0)
    pack[pl.ds(0, 2 * L), :] = g.astype(BF16)
    for i in range(2):
        g = nt(n2[...], dup[pl.ds(i * M, M), :]).astype(BF16)
        pack[pl.ds((2 + 2 * i) * L, L), :] = g[:, :L]
        pack[pl.ds((3 + 2 * i) * L, L), :] = g[:, L:]
    pack[pl.ds(6 * L, 2 * L), :] = nt(joined[...], datt[...]).astype(BF16)


def back_part(wn, d_part, out):
    out[...] = (
        nt(wn[:, pl.ds(L, 2 * L)], d_part[:, pl.ds(0, 2 * L)])
        + nt(wn[:, pl.ds(4 * L, 2 * L)], d_part[:, pl.ds(2 * L, 2 * L)])
    ).astype(BF16)


def back_own(wn, dq, d_own, out):
    out[...] = (
        nt(wn[:, pl.ds(L, 2 * L)], d_own[...])
        + nn(wn[:, pl.ds(0, L)], dq[pl.ds(0, L), :])
        + nn(wn[:, pl.ds(3 * L, L)], dq[pl.ds(L, L), :])
    ).astype(BF16)


def late_grads(cm_own, cm_part, dq, d_own, d_part, pack):
    own, part = nn(cm_own[...], d_own[...]), nn(cm_part[...], d_part[...])
    both = (own + part[:, : 2 * L]).astype(BF16)
    part = part.astype(BF16)
    base = EARLY
    pack[pl.ds(base + L, L), :] = both[:, :L]
    pack[pl.ds(base + 2 * L, L), :] = both[:, L:]
    pack[pl.ds(base + 3 * L, L), :] = nt(cm_own[...], dq[pl.ds(L, L), :]).astype(BF16)
    pack[pl.ds(base + 4 * L, L), :] = part[:, 2 * L : 3 * L]
    pack[pl.ds(base + 5 * L, L), :] = part[:, 3 * L :]
    return nt(cm_own[...], dq[pl.ds(0, L), :])


def finish(win, gain_col, from_own, from_part, dres, gi, acc):
    gain = wide(gain_col)
    acc[...] = jnp.zeros_like(acc)

    def step(i, carry):
        at = pl.ds(pl.multiple_of(i * CH, CH), CH)
        xhat, inv = norm_parts(win[pl.ds(0, L), at].astype(F32)[:C])
        d = from_own[:, at].astype(F32) + from_part[:, at].astype(F32)
        d = d.astype(BF16).astype(F32)[:C]
        acc[...] += fold_lanes(d * xhat)
        gi[:, at] = pad_rows(dres[:, at] + norm_back(xhat, inv, gain, d))
        return carry

    lax.fori_loop(0, T // CH, step, 0)


def first_kernel(
    xo, do, xp, g1, g2, ws, wm, wp, f1, f2, wd,
    win, from_part, from_own, dres, pack, g_query,
    perm, slab, mask_q, mask_v, mask_x, wn, wt, proj, proj_t, fc_n, fc_t, down, col1, col2,
    cm_o, tm_o, cm_p, tm_p, own_cm, own_tm, part_cm, part_tm, probs, joined,
    hid, dup, n2, datt, dj, dq, d_own, d_part, acc,
):
    make_perm(perm)
    make_masks(mask_q, mask_v, mask_x)
    make_weights(ws, wm, wp, f1, f2, wd, wn, wt, proj, proj_t, fc_n, fc_t, down)
    make_gain(g1, col1)
    make_gain(g2, col2)
    slab[...] = jnp.zeros_like(slab)
    for i, ref in enumerate((xo, do, xp)):
        to_slab(slab, i, ref, 0)
    win[...] = nn(slab[...], perm[...]).astype(BF16)
    norm_one(win, 0, col1, cm_o, tm_o)
    norm_one(win, 2 * L, col1, cm_p, tm_p)
    project_own(wt, wn, cm_o, tm_o, own_cm, own_tm)
    project_part(wt, wn, cm_p, tm_p, part_cm, part_tm)
    attend(own_cm, own_tm, part_cm, part_tm, mask_q, mask_v, mask_x, probs, joined)
    feed_forward(
        win, joined, col2, proj, proj_t, fc_n, fc_t, down, hid, dup, n2, datt, dres, dj, acc
    )
    early_grads(hid, dup, n2, joined, datt, win, acc, pack)
    attend_back(
        own_cm, own_tm, part_cm, part_tm, mask_q, mask_v, mask_x, probs, dj, dq, d_own, d_part
    )
    back_part(wn, d_part, from_part)
    back_own(wn, dq, d_own, from_own)
    g_query[...] = late_grads(cm_o, cm_p, dq, d_own, d_part, pack)


def second_kernel(
    win, from_part, from_own, dres, g_query, g1, out, block, perm, gi, col1, acc
):
    make_perm(perm)
    make_gain(g1, col1)
    finish(win, col1, from_own, from_part, dres, gi, acc)
    block[...] = jnp.concatenate([g_query[pl.ds(0, C), :], gain_row(acc[...])], axis=0).astype(BF16)
    rows = nt(gi[...], perm[...]).astype(BF16)
    for r in range(8):
        out[r] = rows[:C, r * W : (r + 1) * W]


def place(group, z, sizes):
    clips, frames, xs, zs = sizes
    core = lax.rem(group, 2)
    x = lax.rem(group // 2, xs)
    frame = lax.rem(group // (2 * xs), frames)
    clip = group // (2 * xs * frames)
    return clip, frame, x * (2 * zs) + z * 2 + core


def reduce_kernel(sizes, block, pack, out, got, mine, heights, s1, r1, s2, r2, s3, r3):
    clips, frames, xs, zs = sizes
    n = clips * frames * xs * 2
    row = lax.axis_index("row")
    core, z, x = lax.rem(row, 2), lax.rem(row // 2, zs), row // (2 * zs)
    me = ((lax.axis_index("clip") * frames + lax.axis_index("frame")) * xs + x) * 2 + core

    def member(d):
        return lax.rem(me + d, n)

    def height(d):
        return lax.rem(z + d, zs)

    def rows_of(i):
        return pl.ds(pl.multiple_of(i * block, block), block)

    barrier = pltpu.get_barrier_semaphore()

    def greet(d, carry):
        pl.semaphore_signal(barrier, inc=1, device_id=place(member(d), z, sizes), device_id_type=MESH)
        return carry

    lax.fori_loop(1, n, greet, 0)

    def greet_up(d, carry):
        pl.semaphore_signal(barrier, inc=1, device_id=place(me, height(d), sizes), device_id_type=MESH)
        return carry

    lax.fori_loop(1, zs, greet_up, 0)
    pl.semaphore_wait(barrier, n - 1 + zs - 1)

    def scatter(d):
        to = member(d)
        return pltpu.make_async_remote_copy(
            src_ref=pack.at[rows_of(to)], dst_ref=got.at[d],
            send_sem=s1.at[d], recv_sem=r1.at[d],
            device_id=place(to, z, sizes), device_id_type=MESH,
        )

    def exchange(d):
        return pltpu.make_async_remote_copy(
            src_ref=mine, dst_ref=heights.at[z],
            send_sem=s2.at[d], recv_sem=r2.at[d],
            device_id=place(me, height(d), sizes), device_id_type=MESH,
        )

    def gather(d):
        return pltpu.make_async_remote_copy(
            src_ref=out.at[rows_of(me)], dst_ref=out.at[rows_of(me)],
            send_sem=s3.at[d], recv_sem=r3.at[d],
            device_id=place(member(d), z, sizes), device_id_type=MESH,
        )

    def each(first, last, act):
        def step(d, carry):
            act(d)
            return carry

        lax.fori_loop(first, last, step, 0)

    each(1, n, lambda d: scatter(d).start())

    def add(d, total):
        scatter(d).wait_recv()
        return total + got[d].astype(F32)

    total = lax.fori_loop(1, n, add, pack[rows_of(me), :].astype(F32))
    mine[...] = total.astype(BF16)
    heights[z] = total.astype(BF16)
    each(1, zs, lambda d: exchange(d).start())
    each(1, zs, lambda d: exchange(d).wait_recv())
    total = heights[0].astype(F32)
    for i in range(1, zs):
        total = total + heights[i].astype(F32)
    out[rows_of(me), :] = total.astype(BF16)
    each(1, n, lambda d: gather(d).start())
    each(1, n, lambda d: gather(d).wait_recv())
    each(1, n, lambda d: scatter(d).wait_send())
    each(1, zs, lambda d: exchange(d).wait_send())
    each(1, n, lambda d: gather(d).wait_send())


def unpack_kernel(scale, total, gi, up, out, o1, o_self, o_mut, o_proj, o2, o_f1, o_f2, o_down):
    def block(i):
        return total[pl.ds(i * L, L), :].astype(F32) * scale

    def beside(parts):
        wide_parts = [
            jnp.concatenate([p, jnp.zeros((L, 2 * L), F32)], axis=1) for p in parts
        ]
        joined = wide_parts[0] + pltpu.roll(wide_parts[1], C, 1) + pltpu.roll(wide_parts[2], 2 * C, 1)
        return joined[:C, : 3 * C]

    b = [block(i) for i in range(14)]
    o_down[...] = jnp.concatenate([b[0], b[1]], axis=0)[:MLP, :C]
    o2[...] = b[1][MLP - L : MLP - L + 1, :C]
    o_f1[...] = jnp.concatenate([b[2], b[3]], axis=1)[:C, :MLP]
    o_f2[...] = jnp.concatenate([b[4], b[5]], axis=1)[:C, :MLP]
    o_proj[...] = jnp.concatenate([b[6][:C], b[7][:C]], axis=0)[:, :C]
    o1[...] = b[8][C : C + 1, :C]
    o_self[...] = beside(b[8:11])
    o_mut[...] = beside(b[11:14])
    for r in range(4):
        out[0, 0, r] = up[r]
        out[0, 0, 4 + r] = gi[r]


def vmem(*shape, dtype=BF16):
    return pltpu.VMEM(shape, dtype)


def shape(*dims, dtype=BF16):
    return jax.ShapeDtypeStruct(dims, dtype)


def in_vmem(count):
    return [pl.BlockSpec(memory_space=pltpu.VMEM)] * count


def passed_along(value, axis, steps):
    count = lax.axis_size(axis)
    return lax.ppermute(value, axis, [(i, (i + steps) % count) for i in range(count)])


def to_partner(value):
    return lax.ppermute(value, "frame", [(i, i ^ 1) for i in range(lax.axis_size("frame"))])


def solution(mesh):
    clips, frames, rows = mesh.shape["clip"], mesh.shape["frame"], mesh.shape["row"]
    zs = min(8, rows // 2)
    xs = rows // (2 * zs)
    sizes = (clips, frames, xs, zs)
    n = clips * frames * xs * 2
    block = ROWS // n
    limit = pltpu.CompilerParams(vmem_limit_bytes=56 * 2**20)

    def on_device(x, d_out, g1, w_self, w_mut, w_proj, g2, f1, f2, w_down):
        both = jnp.concatenate([x[0, 0, :4], d_out[0, 0, :4]], axis=0)
        both = passed_along(both, "row", -1)
        xo = jnp.concatenate([x[0, 0, 4:], both[:4]], axis=0)
        do = jnp.concatenate([d_out[0, 0, 4:], both[4:]], axis=0)
        xp = to_partner(xo)
        g1, g2 = g1.reshape(1, C), g2.reshape(1, C)
        win, from_part, from_own, dres, pack, g_query = pl.pallas_call(
            first_kernel,
            out_shape=(
                shape(3 * L, T), shape(L, T), shape(L, T), shape(C, T, dtype=F32),
                shape(ROWS, L), shape(L, L, dtype=F32),
            ),
            in_specs=in_vmem(11),
            out_specs=tuple(in_vmem(6)),
            scratch_shapes=[
                vmem(T, T), vmem(3 * L, T),
                vmem(2 * L, HEADS * L), vmem(L, HEADS * L), vmem(L, HEADS * 64),
                vmem(L, 6 * L), vmem(6 * L, L), vmem(2 * L, L), vmem(L, 2 * L),
                vmem(L, 2 * M), vmem(2 * M, L), vmem(M, L),
                vmem(C, L, dtype=F32), vmem(C, L, dtype=F32),
                vmem(L, T), vmem(T, L), vmem(L, T), vmem(T, L),
                vmem(4 * L, T), vmem(T, 2 * L), vmem(4 * L, T), vmem(T, 4 * L),
                vmem(T // L, L + 64, HEADS * L), vmem(2 * L, T),
                vmem(M, T), vmem(2 * M, T), vmem(L, T), vmem(L, T), vmem(2 * L, T),
                vmem(2 * L, T), vmem(T, 2 * L), vmem(T, 4 * L), vmem(C, L, dtype=F32),
            ],
            compiler_params=limit,
        )(xo, do, xp, g1, g2, w_self, w_mut, w_proj, f1, f2, w_down)
        from_part = to_partner(from_part)
        gi, query = pl.pallas_call(
            second_kernel,
            out_shape=(shape(8, C, W), shape(L, L)),
            in_specs=in_vmem(6),
            out_specs=tuple(in_vmem(2)),
            scratch_shapes=[vmem(T, T), vmem(L, T), vmem(C, L, dtype=F32), vmem(C, L, dtype=F32)],
            compiler_params=limit,
        )(win, from_part, from_own, dres, g_query, g1)
        up = passed_along(gi[4:], "row", 1)
        pack = lax.dynamic_update_slice(pack, query, (EARLY, 0))
        total = pl.pallas_call(
            lambda *refs: reduce_kernel(sizes, block, *refs),
            out_shape=shape(ROWS, L),
            in_specs=in_vmem(1),
            out_specs=in_vmem(1)[0],
            scratch_shapes=[
                vmem(n, block, L), vmem(block, L), vmem(zs, block, L),
                pltpu.SemaphoreType.DMA((n,)), pltpu.SemaphoreType.DMA((n,)),
                pltpu.SemaphoreType.DMA((zs,)), pltpu.SemaphoreType.DMA((zs,)),
                pltpu.SemaphoreType.DMA((n,)), pltpu.SemaphoreType.DMA((n,)),
            ],
            compiler_params=pltpu.CompilerParams(
                collective_id=0, has_side_effects=True, vmem_limit_bytes=56 * 2**20
            ),
        )(pack)
        scale = float(T * rows * frames * clips) ** -0.5
        out = pl.pallas_call(
            lambda *refs: unpack_kernel(scale, *refs),
            out_shape=(
                shape(1, 1, 8, C, W), shape(1, C, dtype=F32), shape(C, 3 * C, dtype=F32),
                shape(C, 3 * C, dtype=F32), shape(2 * C, C, dtype=F32), shape(1, C, dtype=F32),
                shape(C, MLP, dtype=F32), shape(C, MLP, dtype=F32), shape(MLP, C, dtype=F32),
            ),
            in_specs=in_vmem(3),
            out_specs=tuple(in_vmem(9)),
            compiler_params=limit,
        )(total, gi, up)
        out = list(out)
        out[1], out[5] = out[1].reshape(C), out[5].reshape(C)
        return tuple(out)

    whole = P("clip", "frame", "row", None, None)
    return jax.shard_map(
        on_device,
        mesh=mesh,
        in_specs=(whole, whole) + (P(),) * 8,
        out_specs=(whole,) + (P(),) * 8,
        check_vma=False,
    )
```

```python
import math

import jax
import jax.numpy as jnp
from jax import lax
from jax.experimental import pallas as pl
from jax.experimental.pallas import tpu as pltpu
from jax.sharding import PartitionSpec as P

F32 = jnp.float32
BF16 = jnp.bfloat16
MESH = pl.DeviceIdType.MESH

C = 120
L = 128
W = 128
HEADS = 6
HD = 20
MLP = 240
M = 256
T = 1024
HALF = 512
CH = 256
EPS = 1e-05
EXP_SCALE = float(HD) ** -0.5 * math.log2(math.e)
SCALE = float(HD) ** -0.5

EARLY = 8 * L
LATE = 6 * L
ROWS = 2048


def nn(a, b):
    return lax.dot_general(a, b, (((1,), (0,)), ((), ())), preferred_element_type=F32)


def nt(a, b):
    return lax.dot_general(a, b, (((1,), (1,)), ((), ())), preferred_element_type=F32)


def iota(shape, dim):
    return lax.broadcasted_iota(jnp.int32, shape, dim)


def one_hot(mask):
    return jnp.where(mask, 1.0, 0.0).astype(BF16)


def pad_rows(v):
    return jnp.concatenate([v, jnp.zeros((L - C, v.shape[1]), F32)], axis=0).astype(BF16)


def norm_parts(v):
    mean = jnp.sum(v, axis=0, keepdims=True) * (1.0 / C)
    centre = v - mean
    var = jnp.sum(centre * centre, axis=0, keepdims=True) * (1.0 / C)
    inv = lax.rsqrt(var + EPS)
    return centre * inv, inv


def norm_back(xhat, inv, gain, dy):
    dh = dy * gain
    m1 = jnp.sum(dh, axis=0, keepdims=True) * (1.0 / C)
    m2 = jnp.sum(dh * xhat, axis=0, keepdims=True) * (1.0 / C)
    return inv * (dh - m1 - xhat * m2)


def gain_row(acc):
    full = jnp.concatenate([acc, jnp.zeros((L - C, L), F32)], axis=0)
    row = jnp.sum(jnp.transpose(full), axis=0, keepdims=True)
    return jnp.broadcast_to(row, (8, L))


def fold_lanes(v):
    out = v[:, :L]
    for i in range(1, v.shape[1] // L):
        out = out + v[:, i * L : (i + 1) * L]
    return out


def make_perms(split, join):
    o, i = iota((HALF, HALF), 1), iota((HALF, HALF), 0)
    column = (o >> 8) * 64 + ((o >> 5) & 7) * 8 + (o & 7) + 4
    split[...] = one_hot(i == ((o >> 3) & 3) * W + (column & (W - 1)))
    join[...] = one_hot(i == ((o >> 5) & 3) * L + (o >> 7) * 32 + (o & 31))


def make_masks(mask_h, mask_f):
    row, lane = iota((L, HEADS * L), 0), iota((L, HEADS * L), 1)
    h = lane >> 7
    mask_h[...] = one_hot((row >= h * HD) & (row < h * HD + HD))
    mask_f[...] = one_hot((row >> 6) != ((lane >> 6) & 1))


def make_weights(ws, wm, wp, f1, f2, wd, wn, wt, proj, proj_t, fc_n, fc_t, down):
    def rows128(ref):
        return pad_rows(ref[...].astype(F32))

    r, e = iota((3 * L, 3 * C), 0), iota((3 * L, 3 * C), 1)
    pad3 = one_hot((e == (r >> 7) * C + (r & (L - 1))) & ((r & (L - 1)) < C))
    for i, ref in enumerate((ws, wm)):
        w = rows128(ref)
        wt[pl.ds(i * 3 * L, 3 * L), :] = nt(pad3, w).astype(BF16)
        wn[:, pl.ds(i * 3 * L, 3 * L)] = nt(w, pad3).astype(BF16)
    r, e = iota((M, MLP), 0), iota((M, MLP), 1)
    pad_m = one_hot(r == e)
    pad2 = one_hot((e == (r >> 7) * C + (r & (L - 1))) & ((r & (L - 1)) < C))
    pad_l = one_hot(iota((C, L), 0) == iota((C, L), 1))
    eye = one_hot(iota((L, L), 0) == iota((L, L), 1))
    for i, ref in enumerate((f1, f2)):
        w = rows128(ref)
        fc_t[pl.ds(i * M, M), :] = nt(pad_m, w).astype(BF16)
        fc_n[:, pl.ds(i * M, M)] = nt(w, pad_m).astype(BF16)
    down[...] = nn(nn(pad_m, wd[...]).astype(BF16), pad_l).astype(BF16)
    padded = nn(nn(pad2, wp[...]).astype(BF16), pad_l).astype(BF16)
    proj[...] = padded
    proj_t[...] = nt(eye, padded).astype(BF16)


def make_gain(gain, col):
    col[...] = jnp.transpose(jnp.broadcast_to(gain[...], (L, C)))


def wide(col):
    return jnp.concatenate([col[...]] * (CH // L), axis=1)


def to_slab(slab, rows_ref):
    for i in range(8):
        slab[pl.ds((1 - i // 4) * L, C), pl.ds((i % 4) * W, W)] = rows_ref[i]


def split_blocks(slab, split, out):
    blocks = nn(slab[...], split[...]).astype(BF16)
    for part in range(2):
        for half in range(2):
            out[2 * part + half] = blocks[part * L : part * L + L, half * CH : half * CH + CH]


def join_blocks(blocks, join, out):
    for u in range(2):
        beside = jnp.concatenate([blocks[s, :, pl.ds(u * L, L)] for s in range(4)], axis=1)
        out[:, pl.ds(u * HALF, HALF)] = nn(beside, join[...]).astype(BF16)


def norm_one(win, gain_col, out_cm, out_tm):
    gain = wide(gain_col)

    def step(i, carry):
        at = pl.ds(pl.multiple_of(i * CH, CH), CH)
        y = norm_parts(win[:, at].astype(F32)[:C])[0] * gain
        y = jnp.concatenate([y, jnp.zeros((L - C, CH), F32)], axis=0)
        out_cm[:, at] = y.astype(BF16)
        out_tm[at, :] = jnp.transpose(y).astype(BF16)
        return carry

    lax.fori_loop(0, T // CH, step, 0)


def project(wt, wn, n_cm, n_tm, cm, tm):
    cm[...] = nn(wt[...], n_cm[...]).astype(BF16)
    tm[:, pl.ds(0, 2 * L)] = nn(n_tm[...], wn[:, pl.ds(L, 2 * L)]).astype(BF16)
    tm[:, pl.ds(2 * L, 2 * L)] = nn(n_tm[...], wn[:, pl.ds(4 * L, 2 * L)]).astype(BF16)


def spread(v, mask_h):
    return jnp.concatenate([v] * HEADS, axis=1) * mask_h[...]


def stacked(v):
    return jnp.concatenate([v[:, h * L : (h + 1) * L] for h in range(HEADS)], axis=0)


def other_frame(v):
    first = (iota((64, HEADS * L), 1) & 64) == 0
    return jnp.where(first, v[64:], v[:64])


def both_frames(v, mask_f):
    return jnp.concatenate([v, v], axis=0) * mask_f[...]


def softmax(scores):
    raised = jnp.exp2(scores * EXP_SCALE)
    return (raised * (1.0 / jnp.sum(raised, axis=0, keepdims=True))).astype(BF16)


def attend(cm, tm, mask_h, mask_f, probs, joined):
    def step(p, carry):
        at = pl.ds(pl.multiple_of(p * L, L), L)

        def group(i):
            return spread(cm[pl.ds(i * L, L), at], mask_h)

        pr = softmax(nn(tm[at, pl.ds(0, L)], group(0)))
        probs[p, pl.ds(0, L), :] = pr
        joined[pl.ds(L, L), at] = nn(group(2), stacked(pr)).astype(BF16)
        pr = softmax(other_frame(nn(tm[at, pl.ds(2 * L, L)], group(3))))
        pr = both_frames(pr, mask_f)
        probs[p, pl.ds(L, L), :] = pr
        joined[pl.ds(0, L), at] = nn(group(5), stacked(pr)).astype(BF16)
        return carry

    lax.fori_loop(0, T // L, step, 0)


def score_back(pr, d_pr):
    pr = pr.astype(F32)
    delta = jnp.sum(pr * d_pr, axis=0, keepdims=True)
    return (pr * (d_pr - delta)).astype(BF16)


def attend_back(cm, tm, mask_h, mask_f, probs, dj, dq, d_tm, between):
    def step(p, carry):
        at = pl.ds(pl.multiple_of(p * L, L), L)

        def group(i):
            return spread(cm[pl.ds(i * L, L), at], mask_h)

        pr = probs[p, pl.ds(0, L), :]
        do = spread(dj[pl.ds(L, L), at], mask_h)
        ds = score_back(pr, nn(tm[at, pl.ds(L, L)], do))
        dq[pl.ds(0, L), at] = (nn(group(1), stacked(ds)) * SCALE).astype(BF16)
        d_tm[at, pl.ds(0, L)] = (nt(ds, group(0)) * SCALE).astype(BF16)
        d_tm[at, pl.ds(L, L)] = nt(pr, do).astype(BF16)

        pr = probs[p, pl.ds(L, L), :]
        do = spread(dj[pl.ds(0, L), at], mask_h)
        ds = score_back(pr[:64] + pr[64:], other_frame(nn(tm[at, pl.ds(3 * L, L)], do)))
        ds = both_frames(ds, mask_f)
        dq[pl.ds(L, L), at] = (nn(group(4), stacked(ds)) * SCALE).astype(BF16)
        d_tm[at, pl.ds(2 * L, L)] = (nt(ds, group(3)) * SCALE).astype(BF16)
        d_tm[at, pl.ds(3 * L, L)] = nt(pr, do).astype(BF16)
        between(p)
        return carry

    lax.fori_loop(0, T // L, step, 0)


def feed_forward(
    win, d_win, joined, gain_col, proj, proj_t, fc_n, fc_t, down, hid, dup, n2, datt, dres, dj, acc
):
    gain = wide(gain_col)
    acc[...] = jnp.zeros_like(acc)

    def step(i, carry):
        at = pl.ds(pl.multiple_of(i * CH, CH), CH)
        att = nn(proj_t[...], joined[:, at]).astype(BF16).astype(F32)
        xhat, inv = norm_parts(win[:, at].astype(F32)[:C] + att[:C])
        normed = pad_rows(xhat * gain)
        n2[:, at] = normed
        up = nn(fc_t[...], normed)
        up_one, up_two = up[:M], up[M:]
        cdf = 0.5 * (1.0 + lax.erf(up_one * math.sqrt(0.5)))
        gelu = up_one * cdf
        slope = cdf + up_one * (
            jnp.exp2(up_one * up_one * (-0.5 * math.log2(math.e))) * (1.0 / math.sqrt(2.0 * math.pi))
        )
        hid[:, at] = (gelu * up_two).astype(BF16)
        grad = d_win[:, at]
        d_hid = nn(down[...], grad).astype(BF16).astype(F32)
        d_up = jnp.concatenate(
            [(d_hid * up_two * slope).astype(BF16), (d_hid * gelu).astype(BF16)], axis=0
        )
        dup[:, at] = d_up
        dn = nn(fc_n[...], d_up).astype(BF16).astype(F32)[:C]
        acc[...] += fold_lanes(dn * xhat)
        d_resid = grad.astype(F32)[:C] + norm_back(xhat, inv, gain, dn)
        dres[:, at] = d_resid
        da = pad_rows(d_resid)
        datt[:, at] = da
        dj[:, at] = nn(proj[...], da).astype(BF16)
        return carry

    lax.fori_loop(0, T // CH, step, 0)


def early_grads(hid, dup, n2, joined, datt, d_win, acc, pack):
    g = nt(hid[...], d_win[...])
    row = gain_row(acc[...])
    g = jnp.concatenate([g[:MLP], row, row], axis=0)
    pack[pl.ds(0, 2 * L), :] = g.astype(BF16)
    for i in range(2):
        g = nt(n2[...], dup[pl.ds(i * M, M), :]).astype(BF16)
        pack[pl.ds((2 + 2 * i) * L, L), :] = g[:, :L]
        pack[pl.ds((3 + 2 * i) * L, L), :] = g[:, L:]
    pack[pl.ds(6 * L, 2 * L), :] = nt(joined[...], datt[...]).astype(BF16)


def late_grads(n_cm, dq, d_tm, wn, col, pack):
    g = nn(n_cm[...], d_tm[...])
    g_q, g_qm = (nt(n_cm[...], dq[pl.ds(i * L, L), :]) for i in range(2))
    grads = [g_q, g[:, :L], g[:, L : 2 * L], g_qm, g[:, 2 * L : 3 * L], g[:, 3 * L :]]
    acc = jnp.zeros((L, L), F32)
    for i, g in enumerate(grads):
        acc = acc + g * wn[:, pl.ds(i * L, L)].astype(F32)
    grads[0] = jnp.concatenate([grads[0][:C], gain_row(acc[:C] / col[...])], axis=0)
    for i, g in enumerate(grads):
        pack[pl.ds(EARLY + i * L, L), :] = g.astype(BF16)
    pack[pl.ds(EARLY + LATE, ROWS - EARLY - LATE), :] = jnp.zeros((ROWS - EARLY - LATE, L), BF16)


def finish(first, last, win, gain_col, wn, dq, d_tm, dres, gi):
    gain = wide(gain_col)

    def step(i, carry):
        at = pl.ds(pl.multiple_of(i * CH, CH), CH)
        d = (
            nt(wn[:, pl.ds(L, 2 * L)], d_tm[at, pl.ds(0, 2 * L)])
            + nt(wn[:, pl.ds(4 * L, 2 * L)], d_tm[at, pl.ds(2 * L, 2 * L)])
            + nn(wn[:, pl.ds(0, L)], dq[pl.ds(0, L), at])
            + nn(wn[:, pl.ds(3 * L, L)], dq[pl.ds(L, L), at])
        )
        d = d.astype(BF16).astype(F32)[:C]
        xhat, inv = norm_parts(win[:, at].astype(F32)[:C])
        gi[:, at] = pad_rows(dres[:, at] + norm_back(xhat, inv, gain, d))
        return carry

    lax.fori_loop(first, last, step, 0)


class Spot:
    def __init__(self, clips, frames, xs, zs):
        self.frames, self.xs, self.zs = frames, xs, zs
        self.rows = 2 * zs * xs
        self.plane = clips * frames * xs
        self.clip, self.frame, self.row = (lax.axis_index(a) for a in ("clip", "frame", "row"))
        self.core = lax.rem(self.row, 2)
        self.z = lax.rem(self.row // 2, zs)
        self.q = (self.clip * frames + self.frame) * xs + self.row // (2 * zs)

    def beside(self, frame_too, step):
        frame = self.frame + 1 - 2 * lax.rem(self.frame, 2) if frame_too else self.frame
        return self.clip, frame, lax.rem(self.row + step + self.rows, self.rows)

    def other_core(self):
        return self.clip, self.frame, self.row + 1 - 2 * self.core

    def member(self, d):
        return lax.rem(self.q + d, self.plane)

    def behind(self, d):
        return lax.rem(self.q - d + self.plane, self.plane)

    def in_plane(self, d):
        q = self.member(d)
        x = lax.rem(q, self.xs)
        frame = lax.rem(q // self.xs, self.frames)
        return q // (self.xs * self.frames), frame, x * (2 * self.zs) + self.z * 2 + self.core

    def in_column(self, d):
        z = lax.rem(self.z + d, self.zs)
        return self.clip, self.frame, self.row + (z - self.z) * 2


def each(first, last, act):
    def step(d, carry):
        act(d)
        return carry

    lax.fori_loop(first, last, step, 0)


def remote(src, dst, send, recv, to):
    return pltpu.make_async_remote_copy(
        src_ref=src, dst_ref=dst, send_sem=send, recv_sem=recv, device_id=to, device_id_type=MESH
    )


class Stream:
    def __init__(self, s, spot, r):
        self.s, self.at, self.r = s, spot, r
        self.block = HALF // spot.plane

    def half(self, core):
        return pl.ds(pl.multiple_of(self.s * 2 * HALF + core * HALF, HALF), HALF)

    def rows(self, q):
        return pl.ds(pl.multiple_of(q * self.block, self.block), self.block)

    def total_rows(self, q):
        first = self.s * 2 * HALF + self.at.core * HALF + q * self.block
        return pl.ds(pl.multiple_of(first, self.block), self.block)

    def pair(self):
        r, s = self.r, self.s
        src = r["pack"].at[self.half(1 - self.at.core)]
        return remote(src, r["pair_got"].at[s], r["s0"].at[s], r["r0"].at[s], self.at.other_core())

    def scatter(self, d):
        r, s = self.r, self.s
        src = r["chip"].at[s, self.rows(self.at.member(d))]
        to = self.at.in_plane(d)
        return remote(src, r["plane_got"].at[s, d], r["s1"].at[s, d], r["r1"].at[s, d], to)

    def column(self, d):
        r, s = self.r, self.s
        dst = r["column_got"].at[s, self.at.z]
        return remote(r["mine"].at[s], dst, r["s2"].at[s, d], r["r2"].at[s, d], self.at.in_column(d))

    def gather(self, d):
        r, s = self.r, self.s
        ref = r["total"].at[self.total_rows(self.at.q)]
        return remote(ref, ref, r["s3"].at[s, d], r["r3"].at[s, d], self.at.in_plane(d))

    def hand_over(self, d):
        r, s = self.r, self.s
        ref = r["total"].at[self.total_rows(self.at.behind(d))]
        return remote(ref, ref, r["s4"].at[s, d], r["r4"].at[s, d], self.at.other_core())

    def step_pair(self):
        self.pair().start()

    def step_scatter(self):
        r, s = self.r, self.s
        self.pair().wait_recv()
        own = r["pack"][self.half(self.at.core), :].astype(F32)
        r["chip"][s] = (own + r["pair_got"][s].astype(F32)).astype(BF16)
        each(1, self.at.plane, lambda d: self.scatter(d).start())

    def step_column(self):
        r, s = self.r, self.s

        def add(d, total):
            self.scatter(d).wait_recv()
            return total + r["plane_got"][s, d].astype(F32)

        own = r["chip"][s, self.rows(self.at.q), :].astype(F32)
        total = lax.fori_loop(1, self.at.plane, add, own).astype(BF16)
        r["mine"][s] = total
        r["column_got"][s, self.at.z] = total
        each(1, self.at.zs, lambda d: self.column(d).start())

    def step_gather(self):
        r, s = self.r, self.s
        each(1, self.at.zs, lambda d: self.column(d).wait_recv())
        total = r["column_got"][s, 0].astype(F32)
        for i in range(1, self.at.zs):
            total = total + r["column_got"][s, i].astype(F32)
        r["total"][self.total_rows(self.at.q), :] = total.astype(BF16)
        each(1, self.at.plane, lambda d: self.gather(d).start())
        self.hand_over(0).start()

    def step_hand_over(self):
        def act(d):
            self.gather(d).wait_recv()
            self.hand_over(d).start()

        each(1, self.at.plane, act)

    def step_end(self):
        n, zs = self.at.plane, self.at.zs
        each(0, n, lambda d: self.hand_over(d).wait_recv())
        self.pair().wait_send()
        each(1, n, lambda d: self.scatter(d).wait_send())
        each(1, zs, lambda d: self.column(d).wait_send())
        each(1, n, lambda d: self.gather(d).wait_send())
        each(0, n, lambda d: self.hand_over(d).wait_send())


def layer_kernel(sizes, names, *refs):
    r = dict(zip(names, refs, strict=True))
    spot = Spot(*sizes)

    def get(*wanted):
        return [r[name] for name in wanted]

    barrier = pltpu.get_barrier_semaphore()

    def greet(to):
        pl.semaphore_signal(barrier, inc=1, device_id=to, device_id_type=MESH)

    for frame_too in (False, True):
        for step in (-1, 1):
            greet(spot.beside(frame_too, step))
    each(1, spot.plane, lambda d: greet(spot.in_plane(d)))
    each(1, spot.zs, lambda d: greet(spot.in_column(d)))

    bit = lax.rem(spot.frame, 2)
    sh, rh = r["sh"], r["rh"]
    split, join = get("split", "join")

    def outward(kind, src, dst):
        ends = [
            (src.at[1 - bit], dst.at[2 * bit], spot.beside(True, 0)),
            (src.at[2 + bit], dst.at[2 * bit + 1], spot.beside(False, -1)),
            (src.at[3 - bit], dst.at[2 * bit + 1], spot.beside(True, -1)),
        ]
        return [remote(a, b, sh.at[kind, i], rh.at[kind, i], to) for i, (a, b, to) in enumerate(ends)]

    def homeward(src, dst):
        ends = [
            (src.at[2 * (1 - bit)], dst.at[bit], spot.beside(True, 0)),
            (src.at[2 * bit + 1], dst.at[2 + bit], spot.beside(False, 1)),
            (src.at[2 * (1 - bit) + 1], dst.at[2 + bit], spot.beside(True, 1)),
        ]
        return [remote(a, b, sh.at[2, i], rh.at[2, i], to) for i, (a, b, to) in enumerate(ends)]

    x_copies = outward(0, r["x_send"], r["x_got"])
    d_copies = outward(1, r["d_send"], r["d_got"])
    g_copies = homeward(r["g_send"], r["g_got"])
    copies = x_copies + d_copies + g_copies

    make_perms(split, join)
    for name, rows in (("x_slab", "x"), ("d_slab", "d_out")):
        for part in range(2):
            r[name][pl.ds(part * L + C, L - C), :] = jnp.zeros((L - C, HALF), BF16)
        to_slab(r[name], r[rows].at[0, 0])
    split_blocks(r["x_slab"], split, r["x_send"])
    r["x_got"][2 * bit] = r["x_send"][bit]

    pl.semaphore_wait(barrier, 4 + spot.plane - 1 + spot.zs - 1)
    for copy in x_copies:
        copy.start()
    split_blocks(r["d_slab"], split, r["d_send"])
    for copy in d_copies:
        copy.start()
    r["d_got"][2 * bit] = r["d_send"][bit]
    make_masks(*get("mask_h", "mask_f"))
    make_weights(
        *get("w_self", "w_mut", "w_proj", "f1", "f2", "w_down"),
        *get("wn", "wt", "proj", "proj_t", "fc_n", "fc_t", "down"),
    )
    make_gain(r["g1"], r["col1"])
    make_gain(r["g2"], r["col2"])

    for copy in x_copies:
        copy.wait_recv()
    join_blocks(r["x_got"], join, r["win"])
    norm_one(*get("win", "col1", "n_cm", "n_tm"))
    project(*get("wt", "wn", "n_cm", "n_tm", "cm", "tm"))
    attend(*get("cm", "tm", "mask_h", "mask_f", "probs", "joined"))
    for copy in d_copies:
        copy.wait_recv()
    join_blocks(r["d_got"], join, r["d_win"])
    feed_forward(
        *get("win", "d_win", "joined", "col2", "proj", "proj_t", "fc_n", "fc_t", "down"),
        *get("hid", "dup", "n2", "datt", "dres", "dj", "acc"),
    )
    early_grads(*get("hid", "dup", "n2", "joined", "datt", "d_win", "acc", "pack"))
    early, late = Stream(0, spot, r), Stream(1, spot, r)
    early.step_pair()

    def between(p):
        @pl.when(p == 2)
        def _():
            early.step_scatter()

        @pl.when(p == 5)
        def _():
            early.step_column()

    attend_back(*get("cm", "tm", "mask_h", "mask_f", "probs", "dj", "dq", "d_tm"), between)
    late_grads(*get("n_cm", "dq", "d_tm", "wn", "col1", "pack"))
    late.step_pair()
    early.step_gather()
    rest = get("win", "col1", "wn", "dq", "d_tm", "dres", "gi")
    finish(0, 1, *rest)
    late.step_scatter()
    finish(1, 4, *rest)
    gi, g_send, g_got, out = get("gi", "g_send", "g_got", "out")
    for u in range(2):
        blocks = nt(gi[:, pl.ds(u * HALF, HALF)], join[...]).astype(BF16)
        for s in range(4):
            g_send[s, :, pl.ds(u * L, L)] = blocks[:, s * L : (s + 1) * L]
    for copy in g_copies:
        copy.start()
    g_got[bit] = g_send[2 * bit]
    late.step_column()
    early.step_hand_over()
    for copy in g_copies:
        copy.wait_recv()
    for part in range(2):
        both = jnp.concatenate([g_got[2 * part], g_got[2 * part + 1]], axis=1)
        rows = nt(both, split[...]).astype(BF16)
        for i in range(4):
            out[4 * (1 - part) + i] = rows[:C, i * W : (i + 1) * W]
    late.step_gather()
    late.step_hand_over()
    early.step_end()
    late.step_end()
    for copy in copies:
        copy.wait_send()


def unpack_kernel(scale, total, gi, out, o1, o_self, o_mut, o_proj, o2, o_f1, o_f2, o_down):
    def block(i):
        return total[pl.ds(i * L, L), :].astype(F32) * scale

    def beside(parts):
        wide_parts = [
            jnp.concatenate([p, jnp.zeros((L, 2 * L), F32)], axis=1) for p in parts
        ]
        joined = wide_parts[0] + pltpu.roll(wide_parts[1], C, 1) + pltpu.roll(wide_parts[2], 2 * C, 1)
        return joined[:C, : 3 * C]

    b = [block(i) for i in range(14)]
    o_down[...] = jnp.concatenate([b[0], b[1]], axis=0)[:MLP, :C]
    o2[...] = b[1][MLP - L : MLP - L + 1, :C]
    o_f1[...] = jnp.concatenate([b[2], b[3]], axis=1)[:C, :MLP]
    o_f2[...] = jnp.concatenate([b[4], b[5]], axis=1)[:C, :MLP]
    o_proj[...] = jnp.concatenate([b[6][:C], b[7][:C]], axis=0)[:, :C]
    o1[...] = b[8][C : C + 1, :C]
    o_self[...] = beside(b[8:11])
    o_mut[...] = beside(b[11:14])
    out[0, 0] = gi[...]


def vmem(*shape, dtype=BF16):
    return pltpu.VMEM(shape, dtype)


def shape(*dims, dtype=BF16):
    return jax.ShapeDtypeStruct(dims, dtype)


def in_vmem(count):
    return [pl.BlockSpec(memory_space=pltpu.VMEM)] * count


def solution(mesh):
    clips, frames, rows = mesh.shape["clip"], mesh.shape["frame"], mesh.shape["row"]
    zs = min(8, rows // 2)
    xs = rows // (2 * zs)
    sizes = (clips, frames, xs, zs)
    plane = clips * frames * xs
    dma = pltpu.SemaphoreType.DMA
    ins = ["x", "d_out", "g1", "w_self", "w_mut", "w_proj", "g2", "f1", "f2", "w_down"]
    scratch = dict(
        split=vmem(HALF, HALF), join=vmem(HALF, HALF), x_slab=vmem(2 * L, HALF), d_slab=vmem(2 * L, HALF),
        x_send=vmem(4, L, CH), x_got=vmem(4, L, CH), d_send=vmem(4, L, CH), d_got=vmem(4, L, CH),
        g_send=vmem(4, L, CH), g_got=vmem(4, L, CH), win=vmem(L, T), d_win=vmem(L, T),
        mask_h=vmem(L, HEADS * L), mask_f=vmem(L, HEADS * L),
        wn=vmem(L, 6 * L), wt=vmem(6 * L, L), proj=vmem(2 * L, L), proj_t=vmem(L, 2 * L),
        fc_n=vmem(L, 2 * M), fc_t=vmem(2 * M, L), down=vmem(M, L),
        col1=vmem(C, L, dtype=F32), col2=vmem(C, L, dtype=F32), acc=vmem(C, L, dtype=F32),
        n_cm=vmem(L, T), n_tm=vmem(T, L), cm=vmem(6 * L, T), tm=vmem(T, 4 * L),
        probs=vmem(T // L, 2 * L, HEADS * L), joined=vmem(2 * L, T),
        hid=vmem(M, T), dup=vmem(2 * M, T), n2=vmem(L, T), datt=vmem(L, T),
        dres=vmem(C, T, dtype=F32), dj=vmem(2 * L, T),
        dq=vmem(2 * L, T), d_tm=vmem(T, 4 * L), gi=vmem(L, T),
        pack=vmem(ROWS, L), pair_got=vmem(2, HALF, L), chip=vmem(2, HALF, L),
        plane_got=vmem(2, plane, HALF // plane, L), mine=vmem(2, HALF // plane, L),
        column_got=vmem(2, zs, HALF // plane, L),
        sh=dma((3, 3)), rh=dma((3, 3)), s0=dma((2,)), r0=dma((2,)),
        s1=dma((2, plane)), r1=dma((2, plane)), s2=dma((2, zs)), r2=dma((2, zs)),
        s3=dma((2, plane)), r3=dma((2, plane)), s4=dma((2, plane)), r4=dma((2, plane)),
    )
    names = [*ins, "out", "total", *scratch]

    def on_device(x, d_out, g1, w_self, w_mut, w_proj, g2, f1, f2, w_down):
        g1, g2 = g1.reshape(1, C), g2.reshape(1, C)
        gi, total = pl.pallas_call(
            lambda *refs: layer_kernel(sizes, names, *refs),
            out_shape=(shape(8, C, W), shape(ROWS, L)),
            in_specs=in_vmem(10),
            out_specs=tuple(in_vmem(2)),
            scratch_shapes=list(scratch.values()),
            compiler_params=pltpu.CompilerParams(
                collective_id=0, has_side_effects=True, vmem_limit_bytes=56 * 2**20
            ),
        )(x, d_out, g1, w_self, w_mut, w_proj, g2, f1, f2, w_down)
        scale = float(T * rows * frames * clips) ** -0.5
        out = pl.pallas_call(
            lambda *refs: unpack_kernel(scale, *refs),
            out_shape=(
                shape(1, 1, 8, C, W), shape(1, C, dtype=F32), shape(C, 3 * C, dtype=F32),
                shape(C, 3 * C, dtype=F32), shape(2 * C, C, dtype=F32), shape(1, C, dtype=F32),
                shape(C, MLP, dtype=F32), shape(C, MLP, dtype=F32), shape(MLP, C, dtype=F32),
            ),
            in_specs=in_vmem(2),
            out_specs=tuple(in_vmem(9)),
            compiler_params=pltpu.CompilerParams(vmem_limit_bytes=56 * 2**20),
        )(total, gi)
        out = list(out)
        out[1], out[5] = out[1].reshape(C), out[5].reshape(C)
        return tuple(out)

    whole = P("clip", "frame", "row", None, None)
    return jax.shard_map(
        on_device,
        mesh=mesh,
        in_specs=(whole, whole) + (P(),) * 8,
        out_specs=(whole,) + (P(),) * 8,
        check_vma=False,
    )
```

```python
import math

import jax
import jax.numpy as jnp
from jax import lax
from jax.experimental import pallas as pl
from jax.experimental.pallas import tpu as pltpu
from jax.sharding import PartitionSpec as P

F32 = jnp.float32
BF16 = jnp.bfloat16
MESH = pl.DeviceIdType.MESH

C = 120
L = 128
W = 128
HEADS = 6
HD = 20
MLP = 240
M = 256
T = 1024
HALF = 512
CH = 256
EPS = 1e-05
EXP_SCALE = float(HD) ** -0.5 * math.log2(math.e)
SCALE = float(HD) ** -0.5

EARLY = 8 * L
CROSS = EARLY
SELF = CROSS + 4 * L
ROWS = SELF + 4 * L


def nn(a, b):
    return lax.dot_general(a, b, (((1,), (0,)), ((), ())), preferred_element_type=F32)


def nt(a, b):
    return lax.dot_general(a, b, (((1,), (1,)), ((), ())), preferred_element_type=F32)


def iota(shape, dim):
    return lax.broadcasted_iota(jnp.int32, shape, dim)


def one_hot(mask):
    return jnp.where(mask, 1.0, 0.0).astype(BF16)


def pad_rows(v):
    return jnp.concatenate([v, jnp.zeros((L - C, v.shape[1]), F32)], axis=0).astype(BF16)


def norm_parts(v):
    mean = jnp.sum(v, axis=0, keepdims=True) * (1.0 / C)
    centre = v - mean
    var = jnp.sum(centre * centre, axis=0, keepdims=True) * (1.0 / C)
    inv = lax.rsqrt(var + EPS)
    return centre * inv, inv


def norm_back(xhat, inv, gain, dy):
    dh = dy * gain
    m1 = jnp.sum(dh, axis=0, keepdims=True) * (1.0 / C)
    m2 = jnp.sum(dh * xhat, axis=0, keepdims=True) * (1.0 / C)
    return inv * (dh - m1 - xhat * m2)


def gain_row(acc):
    full = jnp.concatenate([acc, jnp.zeros((L - C, L), F32)], axis=0)
    row = jnp.sum(jnp.transpose(full), axis=0, keepdims=True)
    return jnp.broadcast_to(row, (8, L))


def fold_lanes(v):
    out = v[:, :L]
    for i in range(1, v.shape[1] // L):
        out = out + v[:, i * L : (i + 1) * L]
    return out


def make_perms(split, join):
    o, i = iota((HALF, HALF), 1), iota((HALF, HALF), 0)
    column = (o >> 8) * 64 + ((o >> 5) & 7) * 8 + (o & 7) + 4
    split[...] = one_hot(i == ((o >> 3) & 3) * W + (column & (W - 1)))
    join[...] = one_hot(i == ((o >> 5) & 3) * L + (o >> 7) * 32 + (o & 31))


def make_masks(mask_h, mask_f):
    row, lane = iota((L, HEADS * L), 0), iota((L, HEADS * L), 1)
    h = lane >> 7
    mask_h[...] = one_hot((row >= h * HD) & (row < h * HD + HD))
    mask_f[...] = one_hot((row >> 6) != ((lane >> 6) & 1))


def make_weights(ws, wm, wp, f1, f2, wd, wn, wt, proj, proj_t, fc_n, fc_t, down):
    def rows128(ref):
        return pad_rows(ref[...].astype(F32))

    r, e = iota((3 * L, 3 * C), 0), iota((3 * L, 3 * C), 1)
    pad3 = one_hot((e == (r >> 7) * C + (r & (L - 1))) & ((r & (L - 1)) < C))
    for i, ref in enumerate((ws, wm)):
        w = rows128(ref)
        wt[pl.ds(i * 3 * L, 3 * L), :] = nt(pad3, w).astype(BF16)
        wn[:, pl.ds(i * 3 * L, 3 * L)] = nt(w, pad3).astype(BF16)
    r, e = iota((M, MLP), 0), iota((M, MLP), 1)
    pad_m = one_hot(r == e)
    pad2 = one_hot((e == (r >> 7) * C + (r & (L - 1))) & ((r & (L - 1)) < C))
    pad_l = one_hot(iota((C, L), 0) == iota((C, L), 1))
    eye = one_hot(iota((L, L), 0) == iota((L, L), 1))
    for i, ref in enumerate((f1, f2)):
        w = rows128(ref)
        fc_t[pl.ds(i * M, M), :] = nt(pad_m, w).astype(BF16)
        fc_n[:, pl.ds(i * M, M)] = nt(w, pad_m).astype(BF16)
    down[...] = nn(nn(pad_m, wd[...]).astype(BF16), pad_l).astype(BF16)
    padded = nn(nn(pad2, wp[...]).astype(BF16), pad_l).astype(BF16)
    proj[...] = padded
    proj_t[...] = nt(eye, padded).astype(BF16)


def make_gain(gain, col):
    col[...] = jnp.transpose(jnp.broadcast_to(gain[...], (L, C)))


def wide(col):
    return jnp.concatenate([col[...]] * (CH // L), axis=1)


def to_slab(slab, rows_ref):
    for i in range(8):
        slab[pl.ds((1 - i // 4) * L, C), pl.ds((i % 4) * W, W)] = rows_ref[i]


def split_blocks(slab, split, out):
    blocks = nn(slab[...], split[...]).astype(BF16)
    for part in range(2):
        for half in range(2):
            out[2 * part + half] = blocks[part * L : part * L + L, half * CH : half * CH + CH]


def join_blocks(blocks, join, out):
    for u in range(2):
        beside = jnp.concatenate([blocks[s, :, pl.ds(u * L, L)] for s in range(4)], axis=1)
        out[:, pl.ds(u * HALF, HALF)] = nn(beside, join[...]).astype(BF16)


def norm_one(win, gain_col, out_cm, out_tm):
    gain = wide(gain_col)

    def step(i, carry):
        at = pl.ds(pl.multiple_of(i * CH, CH), CH)
        y = norm_parts(win[:, at].astype(F32)[:C])[0] * gain
        y = jnp.concatenate([y, jnp.zeros((L - C, CH), F32)], axis=0)
        out_cm[:, at] = y.astype(BF16)
        out_tm[at, :] = jnp.transpose(y).astype(BF16)
        return carry

    lax.fori_loop(0, T // CH, step, 0)


def project(wt, wn, n_cm, n_tm, cm, tm):
    cm[...] = nn(wt[...], n_cm[...]).astype(BF16)
    tm[:, pl.ds(0, 2 * L)] = nn(n_tm[...], wn[:, pl.ds(L, 2 * L)]).astype(BF16)
    tm[:, pl.ds(2 * L, 2 * L)] = nn(n_tm[...], wn[:, pl.ds(4 * L, 2 * L)]).astype(BF16)


def spread(v, mask_h):
    return jnp.concatenate([v] * HEADS, axis=1) * mask_h[...]


def stacked(v):
    return jnp.concatenate([v[:, h * L : (h + 1) * L] for h in range(HEADS)], axis=0)


def other_frame(v):
    first = (iota((64, HEADS * L), 1) & 64) == 0
    return jnp.where(first, v[64:], v[:64])


def both_frames(v, mask_f):
    return jnp.concatenate([v, v], axis=0) * mask_f[...]


def softmax(scores):
    raised = jnp.exp2(scores * EXP_SCALE)
    return (raised * (1.0 / jnp.sum(raised, axis=0, keepdims=True))).astype(BF16)


def attend(cm, tm, mask_h, mask_f, probs, joined):
    def step(p, carry):
        at = pl.ds(pl.multiple_of(p * L, L), L)

        def group(i):
            return spread(cm[pl.ds(i * L, L), at], mask_h)

        pr = softmax(nn(tm[at, pl.ds(0, L)], group(0)))
        probs[p, pl.ds(0, L), :] = pr
        joined[pl.ds(L, L), at] = nn(group(2), stacked(pr)).astype(BF16)
        pr = softmax(other_frame(nn(tm[at, pl.ds(2 * L, L)], group(3))))
        pr = both_frames(pr, mask_f)
        probs[p, pl.ds(L, L), :] = pr
        joined[pl.ds(0, L), at] = nn(group(5), stacked(pr)).astype(BF16)
        return carry

    lax.fori_loop(0, T // L, step, 0, unroll=2)


def score_back(pr, d_pr):
    pr = pr.astype(F32)
    delta = jnp.sum(pr * d_pr, axis=0, keepdims=True)
    return (pr * (d_pr - delta)).astype(BF16)


def back_self(cm, tm, mask_h, probs, dj, dq, d_tm, between):
    def step(p, carry):
        at = pl.ds(pl.multiple_of(p * L, L), L)

        def group(i):
            return spread(cm[pl.ds(i * L, L), at], mask_h)

        pr = probs[p, pl.ds(0, L), :]
        do = spread(dj[pl.ds(L, L), at], mask_h)
        ds = score_back(pr, nn(tm[at, pl.ds(L, L)], do))
        dq[pl.ds(0, L), at] = (nn(group(1), stacked(ds)) * SCALE).astype(BF16)
        d_tm[at, pl.ds(0, L)] = (nt(ds, group(0)) * SCALE).astype(BF16)
        d_tm[at, pl.ds(L, L)] = nt(pr, do).astype(BF16)
        between(p)
        return carry

    lax.fori_loop(0, T // L, step, 0, unroll=2)


def back_cross(cm, tm, mask_h, probs, dj, dq, d_tm, mask_f, between):
    def step(p, carry):
        at = pl.ds(pl.multiple_of(p * L, L), L)

        def group(i):
            return spread(cm[pl.ds(i * L, L), at], mask_h)

        pr = probs[p, pl.ds(L, L), :]
        do = spread(dj[pl.ds(0, L), at], mask_h)
        ds = score_back(pr[:64] + pr[64:], other_frame(nn(tm[at, pl.ds(3 * L, L)], do)))
        ds = both_frames(ds, mask_f)
        dq[pl.ds(L, L), at] = (nn(group(4), stacked(ds)) * SCALE).astype(BF16)
        d_tm[at, pl.ds(2 * L, L)] = (nt(ds, group(3)) * SCALE).astype(BF16)
        d_tm[at, pl.ds(3 * L, L)] = nt(pr, do).astype(BF16)
        between(p)
        return carry

    lax.fori_loop(0, T // L, step, 0, unroll=2)


def feed_forward(
    win, d_win, joined, gain_col, proj, proj_t, fc_n, fc_t, down, hid, dup, n2, datt, dres, dj, acc
):
    gain = wide(gain_col)
    acc[...] = jnp.zeros_like(acc)

    def step(i, carry):
        at = pl.ds(pl.multiple_of(i * CH, CH), CH)
        att = nn(proj_t[...], joined[:, at]).astype(BF16).astype(F32)
        xhat, inv = norm_parts(win[:, at].astype(F32)[:C] + att[:C])
        normed = pad_rows(xhat * gain)
        n2[:, at] = normed
        up = nn(fc_t[...], normed)
        up_one, up_two = up[:M], up[M:]
        cdf = 0.5 * (1.0 + lax.erf(up_one * math.sqrt(0.5)))
        gelu = up_one * cdf
        slope = cdf + up_one * (
            jnp.exp2(up_one * up_one * (-0.5 * math.log2(math.e))) * (1.0 / math.sqrt(2.0 * math.pi))
        )
        hid[:, at] = (gelu * up_two).astype(BF16)
        grad = d_win[:, at]
        d_hid = nn(down[...], grad).astype(BF16).astype(F32)
        d_up = jnp.concatenate(
            [(d_hid * up_two * slope).astype(BF16), (d_hid * gelu).astype(BF16)], axis=0
        )
        dup[:, at] = d_up
        dn = nn(fc_n[...], d_up).astype(BF16).astype(F32)[:C]
        acc[...] += fold_lanes(dn * xhat)
        d_resid = grad.astype(F32)[:C] + norm_back(xhat, inv, gain, dn)
        dres[:, at] = d_resid
        da = pad_rows(d_resid)
        datt[:, at] = da
        dj[:, at] = nn(proj[...], da).astype(BF16)
        return carry

    lax.fori_loop(0, T // CH, step, 0)


def early_grads(hid, dup, n2, joined, datt, d_win, acc, pack):
    g = nt(hid[...], d_win[...])
    row = gain_row(acc[...])
    g = jnp.concatenate([g[:MLP], row, row], axis=0)
    pack[pl.ds(0, 2 * L), :] = g.astype(BF16)
    for i in range(2):
        g = nt(n2[...], dup[pl.ds(i * M, M), :]).astype(BF16)
        pack[pl.ds((2 + 2 * i) * L, L), :] = g[:, :L]
        pack[pl.ds((3 + 2 * i) * L, L), :] = g[:, L:]
    pack[pl.ds(6 * L, 2 * L), :] = nt(joined[...], datt[...]).astype(BF16)


def put_grads(pack, base, grads):
    for i, g in enumerate(grads):
        pack[pl.ds(base + i * L, L), :] = g.astype(BF16)
    pack[pl.ds(base + 3 * L, L), :] = jnp.zeros((L, L), BF16)


def by_weights(grads, wn, first):
    acc = jnp.zeros((L, L), F32)
    for i, g in enumerate(grads):
        acc = acc + g * wn[:, pl.ds((first + i) * L, L)].astype(F32)
    return acc[:C]


def cross_grads(n_cm, dq, d_tm, wn, pack, acc):
    g = nn(n_cm[...], d_tm[:, pl.ds(2 * L, 2 * L)])
    grads = [nt(n_cm[...], dq[pl.ds(L, L), :]), g[:, :L], g[:, L:]]
    put_grads(pack, CROSS, grads)
    acc[...] = by_weights(grads, wn, 3)


def self_grads(n_cm, dq, d_tm, wn, pack, acc, col):
    g = nn(n_cm[...], d_tm[:, pl.ds(0, 2 * L)])
    grads = [nt(n_cm[...], dq[pl.ds(0, L), :]), g[:, :L], g[:, L:]]
    row = gain_row((by_weights(grads, wn, 0) + acc[...]) / col[...])
    grads[0] = jnp.concatenate([grads[0][:C], row], axis=0)
    put_grads(pack, SELF, grads)


def finish(first, last, win, gain_col, wn, dq, d_tm, dres, gi):
    gain = wide(gain_col)

    def step(i, carry):
        at = pl.ds(pl.multiple_of(i * CH, CH), CH)
        d = (
            nt(wn[:, pl.ds(L, 2 * L)], d_tm[at, pl.ds(0, 2 * L)])
            + nt(wn[:, pl.ds(4 * L, 2 * L)], d_tm[at, pl.ds(2 * L, 2 * L)])
            + nn(wn[:, pl.ds(0, L)], dq[pl.ds(0, L), at])
            + nn(wn[:, pl.ds(3 * L, L)], dq[pl.ds(L, L), at])
        )
        d = d.astype(BF16).astype(F32)[:C]
        xhat, inv = norm_parts(win[:, at].astype(F32)[:C])
        gi[:, at] = pad_rows(dres[:, at] + norm_back(xhat, inv, gain, d))
        return carry

    lax.fori_loop(first, last, step, 0)


def flips(value, count):
    out = [value]
    step = 1
    while step < count:
        bit = lax.rem(value // step, 2)
        out += [v + step - 2 * step * bit for v in out]
        step *= 2
    return out


class Spot:
    def __init__(self, clips, frames, xs, zs):
        self.zs = zs
        self.rows = 2 * zs * xs
        self.plane = clips * frames * xs
        self.clip, self.frame, self.row = (lax.axis_index(a) for a in ("clip", "frame", "row"))
        self.core = lax.rem(self.row, 2)
        self.z = lax.rem(self.row // 2, zs)
        self.q = (self.clip * frames + self.frame) * xs + self.row // (2 * zs)
        self.clips, self.frames = flips(self.clip, clips), flips(self.frame, frames)
        self.xs = [v * 2 * zs + self.z * 2 + self.core for v in flips(self.row // (2 * zs), xs)]
        self.qs = flips(self.q, self.plane)
        self.all = 2 * self.plane
        self.g = self.q * 2 + self.core
        self.gs = flips(self.g, self.all)

    def beside(self, frame_too, step):
        frame = self.frames[1] if frame_too else self.frame
        return self.clip, frame, lax.rem(self.row + step + self.rows, self.rows)

    def other_core(self):
        return self.clip, self.frame, self.row + 1 - 2 * self.core

    def in_plane(self, d):
        n, m = len(self.xs), len(self.frames)
        return self.clips[d // (n * m)], self.frames[d // n % m], self.xs[d % n]

    def in_both(self, d):
        clip, frame, row = self.in_plane(d // 2)
        return clip, frame, row + (d % 2) * (1 - 2 * self.core)

    def in_column(self, d):
        z = lax.rem(self.z + d, self.zs)
        return self.clip, self.frame, self.row + (z - self.z) * 2


def remote(src, dst, send, recv, to):
    return pltpu.make_async_remote_copy(
        src_ref=src, dst_ref=dst, send_sem=send, recv_sem=recv, device_id=to, device_id_type=MESH
    )


class Stream:
    def __init__(self, s, spot, r):
        self.s, self.at, self.r = s, spot, r
        self.block = HALF // spot.plane

    def sems(self, phase):
        return self.r["sem_send"].at[self.s, phase], self.r["sem_got"].at[self.s, phase]

    def half(self, core):
        return pl.ds(pl.multiple_of(self.s * 2 * HALF + core * HALF, HALF), HALF)

    def rows(self, q):
        return pl.ds(pl.multiple_of(q * self.block, self.block), self.block)

    def total_rows(self, q):
        first = self.s * 2 * HALF + self.at.core * HALF + q * self.block
        return pl.ds(pl.multiple_of(first, self.block), self.block)

    def pair(self):
        src = self.r["pack"].at[self.half(1 - self.at.core)]
        return remote(src, self.r["pair_got"].at[self.s], *self.sems(0), self.at.other_core())

    def scatter(self, d):
        r, s = self.r, self.s
        src = r["chip"].at[s, self.at.qs[d]]
        return remote(src, r["plane_got"].at[s, d - 1], *self.sems(1), self.at.in_plane(d))

    def scatters(self):
        r, s, rest = self.r, self.s, pl.ds(0, self.at.plane - 1)
        return remote(
            r["chip"].at[s, rest], r["plane_got"].at[s, rest], *self.sems(1), self.at.other_core()
        )

    def column(self, d):
        r, s = self.r, self.s
        dst = r["column_got"].at[s, self.at.z]
        return remote(r["mine"].at[s], dst, *self.sems(2), self.at.in_column(d))

    def columns(self):
        ref = self.r["column_got"].at[self.s, pl.ds(0, self.at.zs - 1)]
        return remote(ref, ref, *self.sems(2), self.at.other_core())

    def gather(self, d):
        ref = self.r["total"].at[self.total_rows(self.at.q)]
        return remote(ref, ref, *self.sems(3), self.at.in_plane(d))

    def gathers(self):
        rows = (self.at.plane - 1) * self.block
        ref = self.r["total"].at[pl.ds(self.s * 2 * HALF, rows)]
        return remote(ref, ref, *self.sems(3), self.at.other_core())

    def hand_over(self):
        ref = self.r["total"].at[self.half(self.at.core)]
        return remote(ref, ref, *self.sems(4), self.at.other_core())

    def step_pair(self):
        self.pair().start()

    def step_scatter(self):
        r, s = self.r, self.s
        self.pair().wait_recv()
        own = r["pack"][self.half(self.at.core), :].astype(F32)
        own = (own + r["pair_got"][s].astype(F32)).astype(BF16)
        r["chip"][s] = own.reshape(self.at.plane, self.block, L)
        for d in range(1, self.at.plane):
            self.scatter(d).start()

    def step_column(self):
        r, s = self.r, self.s
        self.scatters().wait_recv()
        total = r["chip"][s, self.at.q].astype(F32)
        for d in range(self.at.plane - 1):
            total = total + r["plane_got"][s, d].astype(F32)
        total = total.astype(BF16)
        r["mine"][s] = total
        r["column_got"][s, self.at.z] = total
        for d in range(1, self.at.zs):
            self.column(d).start()

    def step_gather(self):
        r, s = self.r, self.s
        self.columns().wait_recv()
        total = r["column_got"][s, 0].astype(F32)
        for i in range(1, self.at.zs):
            total = total + r["column_got"][s, i].astype(F32)
        r["total"][self.total_rows(self.at.q), :] = total.astype(BF16)
        for d in range(1, self.at.plane):
            self.gather(d).start()

    def step_hand_over(self):
        self.gathers().wait_recv()
        self.hand_over().start()

    def step_end(self):
        self.hand_over().wait_recv()
        self.pair().wait_send()
        self.scatters().wait_send()
        self.columns().wait_send()
        self.gathers().wait_send()
        self.hand_over().wait_send()


class Direct:
    def __init__(self, s, spot, r):
        self.s, self.at, self.r = s, spot, r
        self.block = HALF // spot.all

    def sems(self, phase):
        return self.r["direct_send"].at[self.s, phase], self.r["direct_got"].at[self.s, phase]

    def rows(self, g):
        first = 2 * HALF + self.s * HALF + g * self.block
        return pl.ds(pl.multiple_of(first, self.block), self.block)

    def scatter(self, d):
        r, s = self.r, self.s
        src = r["pack"].at[self.rows(self.at.gs[d])]
        return remote(src, r["all_got"].at[s, d - 1], *self.sems(0), self.at.in_both(d))

    def scatters(self):
        ref = self.r["all_got"].at[self.s]
        return remote(ref, ref, *self.sems(0), self.at.other_core())

    def column(self, d):
        r, s = self.r, self.s
        dst = r["height_got"].at[s, self.at.z]
        return remote(r["part_sum"].at[s], dst, *self.sems(1), self.at.in_column(d))

    def columns(self):
        ref = self.r["height_got"].at[self.s, pl.ds(0, self.at.zs - 1)]
        return remote(ref, ref, *self.sems(1), self.at.other_core())

    def gather(self, d):
        ref = self.r["total"].at[self.rows(self.at.g)]
        return remote(ref, ref, *self.sems(2), self.at.in_both(d))

    def gathers(self):
        rows = (self.at.all - 1) * self.block
        ref = self.r["total"].at[pl.ds(2 * HALF + self.s * HALF, rows)]
        return remote(ref, ref, *self.sems(2), self.at.other_core())

    def step_scatter(self):
        for d in range(1, self.at.all):
            self.scatter(d).start()

    def step_column(self):
        r, s = self.r, self.s
        self.scatters().wait_recv()
        total = r["pack"][self.rows(self.at.g), :].astype(F32)
        for d in range(self.at.all - 1):
            total = total + r["all_got"][s, d].astype(F32)
        total = total.astype(BF16)
        r["part_sum"][s] = total
        r["height_got"][s, self.at.z] = total
        for d in range(1, self.at.zs):
            self.column(d).start()

    def step_gather(self):
        r, s = self.r, self.s
        self.columns().wait_recv()
        total = r["height_got"][s, 0].astype(F32)
        for i in range(1, self.at.zs):
            total = total + r["height_got"][s, i].astype(F32)
        r["total"][self.rows(self.at.g), :] = total.astype(BF16)
        for d in range(1, self.at.all):
            self.gather(d).start()

    def step_end(self):
        self.gathers().wait_recv()
        self.scatters().wait_send()
        self.columns().wait_send()
        self.gathers().wait_send()


def layer_kernel(sizes, names, *refs):
    r = dict(zip(names, refs, strict=True))
    spot = Spot(*sizes)

    def get(*wanted):
        return [r[name] for name in wanted]

    barrier = pltpu.get_barrier_semaphore()

    def greet(to):
        pl.semaphore_signal(barrier, inc=1, device_id=to, device_id_type=MESH)

    for frame_too in (False, True):
        for step in (-1, 1):
            greet(spot.beside(frame_too, step))
    for d in range(1, spot.plane):
        greet(spot.in_plane(d))
    for d in range(1, spot.zs):
        greet(spot.in_column(d))

    bit = lax.rem(spot.frame, 2)
    sh, rh = r["sh"], r["rh"]
    split, join = get("split", "join")

    def outward(kind, src, dst):
        ends = [
            (src.at[1 - bit], dst.at[2 * bit], spot.beside(True, 0)),
            (src.at[2 + bit], dst.at[2 * bit + 1], spot.beside(False, -1)),
            (src.at[3 - bit], dst.at[2 * bit + 1], spot.beside(True, -1)),
        ]
        return [remote(a, b, sh.at[kind, i], rh.at[kind, i], to) for i, (a, b, to) in enumerate(ends)]

    def homeward(src, dst):
        ends = [
            (src.at[2 * (1 - bit)], dst.at[bit], spot.beside(True, 0)),
            (src.at[2 * bit + 1], dst.at[2 + bit], spot.beside(False, 1)),
            (src.at[2 * (1 - bit) + 1], dst.at[2 + bit], spot.beside(True, 1)),
        ]
        return [remote(a, b, sh.at[2, i], rh.at[2, i], to) for i, (a, b, to) in enumerate(ends)]

    x_copies = outward(0, r["x_send"], r["x_got"])
    d_copies = outward(1, r["d_send"], r["d_got"])
    g_copies = homeward(r["g_send"], r["g_got"])
    copies = x_copies + d_copies + g_copies

    make_perms(split, join)
    for name, rows in (("x_slab", "x"), ("d_slab", "d_out")):
        for part in range(2):
            r[name][pl.ds(part * L + C, L - C), :] = jnp.zeros((L - C, HALF), BF16)
        to_slab(r[name], r[rows].at[0, 0])
    split_blocks(r["x_slab"], split, r["x_send"])
    r["x_got"][2 * bit] = r["x_send"][bit]

    make_masks(*get("mask_h", "mask_f"))
    make_weights(
        *get("w_self", "w_mut", "w_proj", "f1", "f2", "w_down"),
        *get("wn", "wt", "proj", "proj_t", "fc_n", "fc_t", "down"),
    )
    make_gain(r["g1"], r["col1"])
    make_gain(r["g2"], r["col2"])
    pl.semaphore_wait(barrier, 4 + spot.plane - 1 + spot.zs - 1)
    for copy in x_copies:
        copy.start()
    split_blocks(r["d_slab"], split, r["d_send"])
    for copy in d_copies:
        copy.start()
    r["d_got"][2 * bit] = r["d_send"][bit]

    for copy in x_copies:
        copy.wait_recv()
    join_blocks(r["x_got"], join, r["win"])
    norm_one(*get("win", "col1", "n_cm", "n_tm"))
    project(*get("wt", "wn", "n_cm", "n_tm", "cm", "tm"))
    attend(*get("cm", "tm", "mask_h", "mask_f", "probs", "joined"))
    for copy in d_copies:
        copy.wait_recv()
    join_blocks(r["d_got"], join, r["d_win"])
    feed_forward(
        *get("win", "d_win", "joined", "col2", "proj", "proj_t", "fc_n", "fc_t", "down"),
        *get("hid", "dup", "n2", "datt", "dres", "dj", "acc"),
    )
    early_grads(*get("hid", "dup", "n2", "joined", "datt", "d_win", "acc", "pack"))
    early, cross, last = Stream(0, spot, r), Direct(0, spot, r), Direct(1, spot, r)
    early.step_pair()

    def in_cross(p):
        @pl.when(p == 3)
        def _():
            early.step_scatter()

    def in_self(p):
        @pl.when(p == 5)
        def _():
            early.step_column()

    back = get("cm", "tm", "mask_h", "probs", "dj", "dq", "d_tm")
    back_cross(*back, r["mask_f"], in_cross)
    cross_grads(*get("n_cm", "dq", "d_tm", "wn", "pack", "acc"))
    cross.step_scatter()
    back_self(*back, in_self)
    self_grads(*get("n_cm", "dq", "d_tm", "wn", "pack", "acc", "col1"))
    last.step_scatter()
    cross.step_column()
    finish(0, 4, *get("win", "col1", "wn", "dq", "d_tm", "dres", "gi"))
    gi, g_send, g_got, out = get("gi", "g_send", "g_got", "out")
    for u in range(2):
        blocks = nt(gi[:, pl.ds(u * HALF, HALF)], join[...]).astype(BF16)
        for s in range(4):
            g_send[s, :, pl.ds(u * L, L)] = blocks[:, s * L : (s + 1) * L]
    for copy in g_copies:
        copy.start()
    g_got[bit] = g_send[2 * bit]
    last.step_column()
    early.step_gather()
    cross.step_gather()
    last.step_gather()
    for copy in g_copies:
        copy.wait_recv()
    for part in range(2):
        both = jnp.concatenate([g_got[2 * part], g_got[2 * part + 1]], axis=1)
        rows = nt(both, split[...]).astype(BF16)
        for i in range(4):
            out[4 * (1 - part) + i] = rows[:C, i * W : (i + 1) * W]
    early.step_hand_over()
    cross.step_end()
    last.step_end()
    early.step_end()
    for copy in copies:
        copy.wait_send()


def unpack_kernel(scale, total, gi, out, o1, o_self, o_mut, o_proj, o2, o_f1, o_f2, o_down):
    def block(i):
        return total[pl.ds(i * L, L), :].astype(F32) * scale

    def beside(parts):
        wide_parts = [
            jnp.concatenate([p, jnp.zeros((L, 2 * L), F32)], axis=1) for p in parts
        ]
        joined = wide_parts[0] + pltpu.roll(wide_parts[1], C, 1) + pltpu.roll(wide_parts[2], 2 * C, 1)
        return joined[:C, : 3 * C]

    b = [block(i) for i in range(8 + 3 + 4)]
    o_down[...] = jnp.concatenate([b[0], b[1]], axis=0)[:MLP, :C]
    o2[...] = b[1][MLP - L : MLP - L + 1, :C]
    o_f1[...] = jnp.concatenate([b[2], b[3]], axis=1)[:C, :MLP]
    o_f2[...] = jnp.concatenate([b[4], b[5]], axis=1)[:C, :MLP]
    o_proj[...] = jnp.concatenate([b[6][:C], b[7][:C]], axis=0)[:, :C]
    o1[...] = b[12][C : C + 1, :C]
    o_mut[...] = beside(b[8:11])
    o_self[...] = beside(b[12:15])
    out[0, 0] = gi[...]


def vmem(*shape, dtype=BF16):
    return pltpu.VMEM(shape, dtype)


def shape(*dims, dtype=BF16):
    return jax.ShapeDtypeStruct(dims, dtype)


def in_vmem(count):
    return [pl.BlockSpec(memory_space=pltpu.VMEM)] * count


def solution(mesh):
    clips, frames, rows = mesh.shape["clip"], mesh.shape["frame"], mesh.shape["row"]
    zs = min(8, rows // 2)
    xs = rows // (2 * zs)
    sizes = (clips, frames, xs, zs)
    plane = clips * frames * xs
    dma = pltpu.SemaphoreType.DMA
    ins = ["x", "d_out", "g1", "w_self", "w_mut", "w_proj", "g2", "f1", "f2", "w_down"]
    scratch = dict(
        split=vmem(HALF, HALF), join=vmem(HALF, HALF), x_slab=vmem(2 * L, HALF), d_slab=vmem(2 * L, HALF),
        x_send=vmem(4, L, CH), x_got=vmem(4, L, CH), d_send=vmem(4, L, CH), d_got=vmem(4, L, CH),
        g_send=vmem(4, L, CH), g_got=vmem(4, L, CH), win=vmem(L, T), d_win=vmem(L, T),
        mask_h=vmem(L, HEADS * L), mask_f=vmem(L, HEADS * L),
        wn=vmem(L, 6 * L), wt=vmem(6 * L, L), proj=vmem(2 * L, L), proj_t=vmem(L, 2 * L),
        fc_n=vmem(L, 2 * M), fc_t=vmem(2 * M, L), down=vmem(M, L),
        col1=vmem(C, L, dtype=F32), col2=vmem(C, L, dtype=F32), acc=vmem(C, L, dtype=F32),
        n_cm=vmem(L, T), n_tm=vmem(T, L), cm=vmem(6 * L, T), tm=vmem(T, 4 * L),
        probs=vmem(T // L, 2 * L, HEADS * L), joined=vmem(2 * L, T),
        hid=vmem(M, T), dup=vmem(2 * M, T), n2=vmem(L, T), datt=vmem(L, T),
        dres=vmem(C, T, dtype=F32), dj=vmem(2 * L, T),
        dq=vmem(2 * L, T), d_tm=vmem(T, 4 * L), gi=vmem(L, T),
        pack=vmem(ROWS, L), pair_got=vmem(1, HALF, L), chip=vmem(1, plane, HALF // plane, L),
        plane_got=vmem(1, plane - 1, HALF // plane, L), mine=vmem(1, HALF // plane, L),
        column_got=vmem(1, zs, HALF // plane, L),
        sh=dma((3, 3)), rh=dma((3, 3)), sem_send=dma((1, 5)), sem_got=dma((1, 5)),
        direct_send=dma((2, 3)), direct_got=dma((2, 3)), all_got=vmem(2, 2 * plane - 1, HALF // (2 * plane), L),
        part_sum=vmem(2, HALF // (2 * plane), L), height_got=vmem(2, zs, HALF // (2 * plane), L),
    )
    names = [*ins, "out", "total", *scratch]

    def on_device(x, d_out, g1, w_self, w_mut, w_proj, g2, f1, f2, w_down):
        g1, g2 = g1.reshape(1, C), g2.reshape(1, C)
        gi, total = pl.pallas_call(
            lambda *refs: layer_kernel(sizes, names, *refs),
            out_shape=(shape(8, C, W), shape(ROWS, L)),
            in_specs=in_vmem(10),
            out_specs=tuple(in_vmem(2)),
            scratch_shapes=list(scratch.values()),
            compiler_params=pltpu.CompilerParams(
                collective_id=0, has_side_effects=True, vmem_limit_bytes=56 * 2**20
            ),
        )(x, d_out, g1, w_self, w_mut, w_proj, g2, f1, f2, w_down)
        scale = float(T * rows * frames * clips) ** -0.5
        out = pl.pallas_call(
            lambda *refs: unpack_kernel(scale, *refs),
            out_shape=(
                shape(1, 1, 8, C, W), shape(1, C, dtype=F32), shape(C, 3 * C, dtype=F32),
                shape(C, 3 * C, dtype=F32), shape(2 * C, C, dtype=F32), shape(1, C, dtype=F32),
                shape(C, MLP, dtype=F32), shape(C, MLP, dtype=F32), shape(MLP, C, dtype=F32),
            ),
            in_specs=in_vmem(2),
            out_specs=tuple(in_vmem(9)),
            compiler_params=pltpu.CompilerParams(vmem_limit_bytes=56 * 2**20),
        )(total, gi)
        out = list(out)
        out[1], out[5] = out[1].reshape(C), out[5].reshape(C)
        return tuple(out)

    whole = P("clip", "frame", "row", None, None)
    return jax.shard_map(
        on_device,
        mesh=mesh,
        in_specs=(whole, whole) + (P(),) * 8,
        out_specs=(whole,) + (P(),) * 8,
        check_vma=False,
    )
```

```python
import math

import jax
import jax.numpy as jnp
from jax import lax
from jax.experimental import pallas as pl
from jax.experimental.pallas import tpu as pltpu
from jax.sharding import PartitionSpec as P

F32 = jnp.float32
BF16 = jnp.bfloat16
MESH = pl.DeviceIdType.MESH

C = 120
L = 128
W = 128
HEADS = 6
HD = 20
MLP = 240
M = 256
T = 1024
HALF = 512
CH = 256
EPS = 1e-05
EXP_SCALE = float(HD) ** -0.5 * math.log2(math.e)
SCALE = float(HD) ** -0.5

EARLY = 8 * L
CROSS = EARLY
SELF = CROSS + 4 * L
ROWS = SELF + 4 * L


def nn(a, b):
    return lax.dot_general(a, b, (((1,), (0,)), ((), ())), preferred_element_type=F32)


def nt(a, b):
    return lax.dot_general(a, b, (((1,), (1,)), ((), ())), preferred_element_type=F32)


def iota(shape, dim):
    return lax.broadcasted_iota(jnp.int32, shape, dim)


def one_hot(mask):
    return jnp.where(mask, 1.0, 0.0).astype(BF16)


def pad_rows(v):
    return jnp.concatenate([v, jnp.zeros((L - C, v.shape[1]), F32)], axis=0).astype(BF16)


def norm_parts(v):
    mean = jnp.sum(v, axis=0, keepdims=True) * (1.0 / C)
    centre = v - mean
    var = jnp.sum(centre * centre, axis=0, keepdims=True) * (1.0 / C)
    inv = lax.rsqrt(var + EPS)
    return centre * inv, inv


def norm_back(xhat, inv, gain, dy):
    dh = dy * gain
    m1 = jnp.sum(dh, axis=0, keepdims=True) * (1.0 / C)
    m2 = jnp.sum(dh * xhat, axis=0, keepdims=True) * (1.0 / C)
    return inv * (dh - m1 - xhat * m2)


def gain_row(acc):
    full = jnp.concatenate([acc, jnp.zeros((L - C, L), F32)], axis=0)
    row = jnp.sum(jnp.transpose(full), axis=0, keepdims=True)
    return jnp.broadcast_to(row, (8, L))


def fold_lanes(v):
    out = v[:, :L]
    for i in range(1, v.shape[1] // L):
        out = out + v[:, i * L : (i + 1) * L]
    return out


def make_perms(split, join):
    o, i = iota((HALF, HALF), 1), iota((HALF, HALF), 0)
    column = (o >> 8) * 64 + ((o >> 5) & 7) * 8 + (o & 7) + 4
    split[...] = one_hot(i == ((o >> 3) & 3) * W + (column & (W - 1)))
    join[...] = one_hot(i == ((o >> 5) & 3) * L + (o >> 7) * 32 + (o & 31))


def make_masks(mask_h, mask_f):
    row, lane = iota((L, HEADS * L), 0), iota((L, HEADS * L), 1)
    h = lane >> 7
    mask_h[...] = one_hot((row >= h * HD) & (row < h * HD + HD))
    mask_f[...] = one_hot((row >> 6) != ((lane >> 6) & 1))


def make_weights(ws, wm, wp, f1, f2, wd, wn, wt, proj, proj_t, fc_n, fc_t, down):
    def rows128(ref):
        return pad_rows(ref[...].astype(F32))

    r, e = iota((3 * L, 3 * C), 0), iota((3 * L, 3 * C), 1)
    pad3 = one_hot((e == (r >> 7) * C + (r & (L - 1))) & ((r & (L - 1)) < C))
    for i, ref in enumerate((ws, wm)):
        w = rows128(ref)
        wt[pl.ds(i * 3 * L, 3 * L), :] = nt(pad3, w).astype(BF16)
        wn[:, pl.ds(i * 3 * L, 3 * L)] = nt(w, pad3).astype(BF16)
    r, e = iota((M, MLP), 0), iota((M, MLP), 1)
    pad_m = one_hot(r == e)
    pad2 = one_hot((e == (r >> 7) * C + (r & (L - 1))) & ((r & (L - 1)) < C))
    pad_l = one_hot(iota((C, L), 0) == iota((C, L), 1))
    eye = one_hot(iota((L, L), 0) == iota((L, L), 1))
    for i, ref in enumerate((f1, f2)):
        w = rows128(ref)
        fc_t[pl.ds(i * M, M), :] = nt(pad_m, w).astype(BF16)
        fc_n[:, pl.ds(i * M, M)] = nt(w, pad_m).astype(BF16)
    down[...] = nn(nn(pad_m, wd[...]).astype(BF16), pad_l).astype(BF16)
    padded = nn(nn(pad2, wp[...]).astype(BF16), pad_l).astype(BF16)
    proj[...] = padded
    proj_t[...] = nt(eye, padded).astype(BF16)


def make_gain(gain, col):
    col[...] = jnp.transpose(jnp.broadcast_to(gain[...], (L, C)))


def wide(col):
    return jnp.concatenate([col[...]] * (CH // L), axis=1)


def to_slab(slab, rows_ref):
    for i in range(8):
        slab[pl.ds((1 - i // 4) * L, C), pl.ds((i % 4) * W, W)] = rows_ref[i]


def split_blocks(slab, split, out):
    blocks = nn(slab[...], split[...]).astype(BF16)
    for part in range(2):
        for half in range(2):
            for u in range(2):
                first = half * CH + u * L
                out[u, 2 * part + half] = blocks[part * L : part * L + L, first : first + L]


def join_blocks(u, blocks, join, out):
    beside = jnp.concatenate([blocks[u, s] for s in range(4)], axis=1)
    out[:, pl.ds(u * HALF, HALF)] = nn(beside, join[...]).astype(BF16)


def norm_one(u, win, gain_col, out_cm, out_tm):
    gain = wide(gain_col)

    def step(i, carry):
        at = pl.ds(pl.multiple_of(i * CH, CH), CH)
        y = norm_parts(win[:, at].astype(F32)[:C])[0] * gain
        y = jnp.concatenate([y, jnp.zeros((L - C, CH), F32)], axis=0)
        out_cm[:, at] = y.astype(BF16)
        out_tm[at, :] = jnp.transpose(y).astype(BF16)
        return carry

    lax.fori_loop(u * 2, u * 2 + 2, step, 0, unroll=2)


def project(u, wt, wn, n_cm, n_tm, cm, tm):
    at = pl.ds(u * HALF, HALF)
    cm[:, at] = nn(wt[...], n_cm[:, at]).astype(BF16)
    tm[at, pl.ds(0, 2 * L)] = nn(n_tm[at, :], wn[:, pl.ds(L, 2 * L)]).astype(BF16)
    tm[at, pl.ds(2 * L, 2 * L)] = nn(n_tm[at, :], wn[:, pl.ds(4 * L, 2 * L)]).astype(BF16)


def spread(v, mask_h):
    return jnp.concatenate([v] * HEADS, axis=1) * mask_h[...]


def stacked(v):
    return jnp.concatenate([v[:, h * L : (h + 1) * L] for h in range(HEADS)], axis=0)


def other_frame(v):
    first = (iota((64, HEADS * L), 1) & 64) == 0
    return jnp.where(first, v[64:], v[:64])


def both_frames(v, mask_f):
    return jnp.concatenate([v, v], axis=0) * mask_f[...]


def softmax(scores):
    raised = jnp.exp2(scores * EXP_SCALE)
    return (raised * (1.0 / jnp.sum(raised, axis=0, keepdims=True))).astype(BF16)


def attend(u, cm, tm, mask_h, mask_f, probs, joined):
    def step(p, carry):
        at = pl.ds(pl.multiple_of(p * L, L), L)

        def group(i):
            return spread(cm[pl.ds(i * L, L), at], mask_h)

        pr = softmax(nn(tm[at, pl.ds(0, L)], group(0)))
        probs[p, pl.ds(0, L), :] = pr
        joined[pl.ds(L, L), at] = nn(group(2), stacked(pr)).astype(BF16)
        pr = softmax(other_frame(nn(tm[at, pl.ds(2 * L, L)], group(3))))
        pr = both_frames(pr, mask_f)
        probs[p, pl.ds(L, L), :] = pr
        joined[pl.ds(0, L), at] = nn(group(5), stacked(pr)).astype(BF16)
        return carry

    lax.fori_loop(u * 4, u * 4 + 4, step, 0, unroll=4)


def score_back(pr, d_pr):
    pr = pr.astype(F32)
    delta = jnp.sum(pr * d_pr, axis=0, keepdims=True)
    return (pr * (d_pr - delta)).astype(BF16)


def back_self(cm, tm, mask_h, probs, dj, dq, d_tm, between):
    def step(p, carry):
        at = pl.ds(pl.multiple_of(p * L, L), L)

        def group(i):
            return spread(cm[pl.ds(i * L, L), at], mask_h)

        pr = probs[p, pl.ds(0, L), :]
        do = spread(dj[pl.ds(L, L), at], mask_h)
        ds = score_back(pr, nn(tm[at, pl.ds(L, L)], do))
        dq[pl.ds(0, L), at] = (nn(group(1), stacked(ds)) * SCALE).astype(BF16)
        d_tm[at, pl.ds(0, L)] = (nt(ds, group(0)) * SCALE).astype(BF16)
        d_tm[at, pl.ds(L, L)] = nt(pr, do).astype(BF16)
        between(p)
        return carry

    lax.fori_loop(0, T // L, step, 0, unroll=8)


def back_cross(cm, tm, mask_h, probs, dj, dq, d_tm, mask_f, between):
    def step(p, carry):
        at = pl.ds(pl.multiple_of(p * L, L), L)

        def group(i):
            return spread(cm[pl.ds(i * L, L), at], mask_h)

        pr = probs[p, pl.ds(L, L), :]
        do = spread(dj[pl.ds(0, L), at], mask_h)
        ds = score_back(pr[:64] + pr[64:], other_frame(nn(tm[at, pl.ds(3 * L, L)], do)))
        ds = both_frames(ds, mask_f)
        dq[pl.ds(L, L), at] = (nn(group(4), stacked(ds)) * SCALE).astype(BF16)
        d_tm[at, pl.ds(2 * L, L)] = (nt(ds, group(3)) * SCALE).astype(BF16)
        d_tm[at, pl.ds(3 * L, L)] = nt(pr, do).astype(BF16)
        between(p)
        return carry

    lax.fori_loop(0, T // L, step, 0, unroll=8)


def feed_forward(
    win, d_win, joined, gain_col, proj, proj_t, fc_n, fc_t, down, hid, dup, n2, datt, dres, dj, acc
):
    gain = wide(gain_col)
    acc[...] = jnp.zeros_like(acc)

    def step(i, carry):
        at = pl.ds(pl.multiple_of(i * CH, CH), CH)
        att = nn(proj_t[...], joined[:, at]).astype(BF16).astype(F32)
        xhat, inv = norm_parts(win[:, at].astype(F32)[:C] + att[:C])
        normed = pad_rows(xhat * gain)
        n2[:, at] = normed
        up = nn(fc_t[...], normed)
        up_one, up_two = up[:M], up[M:]
        cdf = 0.5 * (1.0 + lax.erf(up_one * math.sqrt(0.5)))
        gelu = up_one * cdf
        slope = cdf + up_one * (
            jnp.exp2(up_one * up_one * (-0.5 * math.log2(math.e))) * (1.0 / math.sqrt(2.0 * math.pi))
        )
        hid[:, at] = (gelu * up_two).astype(BF16)
        grad = d_win[:, at]
        d_hid = nn(down[...], grad).astype(BF16).astype(F32)
        d_up = jnp.concatenate(
            [(d_hid * up_two * slope).astype(BF16), (d_hid * gelu).astype(BF16)], axis=0
        )
        dup[:, at] = d_up
        dn = nn(fc_n[...], d_up).astype(BF16).astype(F32)[:C]
        acc[...] += fold_lanes(dn * xhat)
        d_resid = grad.astype(F32)[:C] + norm_back(xhat, inv, gain, dn)
        dres[:, at] = d_resid
        da = pad_rows(d_resid)
        datt[:, at] = da
        dj[:, at] = nn(proj[...], da).astype(BF16)
        return carry

    lax.fori_loop(0, T // CH, step, 0, unroll=4)


def early_grads(hid, dup, n2, joined, datt, d_win, acc, pack):
    g = nt(hid[...], d_win[...])
    row = gain_row(acc[...])
    g = jnp.concatenate([g[:MLP], row, row], axis=0)
    pack[pl.ds(0, 2 * L), :] = g.astype(BF16)
    for i in range(2):
        g = nt(n2[...], dup[pl.ds(i * M, M), :]).astype(BF16)
        pack[pl.ds((2 + 2 * i) * L, L), :] = g[:, :L]
        pack[pl.ds((3 + 2 * i) * L, L), :] = g[:, L:]
    pack[pl.ds(6 * L, 2 * L), :] = nt(joined[...], datt[...]).astype(BF16)


def put_grads(pack, base, grads):
    for i, g in enumerate(grads):
        pack[pl.ds(base + i * L, L), :] = g.astype(BF16)
    pack[pl.ds(base + 3 * L, L), :] = jnp.zeros((L, L), BF16)


def by_weights(grads, wn, first):
    acc = jnp.zeros((L, L), F32)
    for i, g in enumerate(grads):
        acc = acc + g * wn[:, pl.ds((first + i) * L, L)].astype(F32)
    return acc[:C]


def cross_grads(n_cm, dq, d_tm, wn, pack, acc):
    g = nn(n_cm[...], d_tm[:, pl.ds(2 * L, 2 * L)])
    grads = [nt(n_cm[...], dq[pl.ds(L, L), :]), g[:, :L], g[:, L:]]
    put_grads(pack, CROSS, grads)
    acc[...] = by_weights(grads, wn, 3)


def self_grads(n_cm, dq, d_tm, wn, pack, acc, col):
    g = nn(n_cm[...], d_tm[:, pl.ds(0, 2 * L)])
    grads = [nt(n_cm[...], dq[pl.ds(0, L), :]), g[:, :L], g[:, L:]]
    row = gain_row((by_weights(grads, wn, 0) + acc[...]) / col[...])
    grads[0] = jnp.concatenate([grads[0][:C], row], axis=0)
    put_grads(pack, SELF, grads)


def finish(first, last, win, gain_col, wn, dq, d_tm, dres, gi):
    gain = wide(gain_col)

    def step(i, carry):
        at = pl.ds(pl.multiple_of(i * CH, CH), CH)
        d = (
            nt(wn[:, pl.ds(L, 2 * L)], d_tm[at, pl.ds(0, 2 * L)])
            + nt(wn[:, pl.ds(4 * L, 2 * L)], d_tm[at, pl.ds(2 * L, 2 * L)])
            + nn(wn[:, pl.ds(0, L)], dq[pl.ds(0, L), at])
            + nn(wn[:, pl.ds(3 * L, L)], dq[pl.ds(L, L), at])
        )
        d = d.astype(BF16).astype(F32)[:C]
        xhat, inv = norm_parts(win[:, at].astype(F32)[:C])
        gi[:, at] = pad_rows(dres[:, at] + norm_back(xhat, inv, gain, d))
        return carry

    lax.fori_loop(first, last, step, 0, unroll=4)


def flips(value, count):
    out = [value]
    step = 1
    while step < count:
        bit = lax.rem(value // step, 2)
        out += [v + step - 2 * step * bit for v in out]
        step *= 2
    return out


class Spot:
    def __init__(self, clips, frames, xs, zs):
        self.zs = zs
        self.rows = 2 * zs * xs
        self.plane = clips * frames * xs
        self.clip, self.frame, self.row = (lax.axis_index(a) for a in ("clip", "frame", "row"))
        self.core = lax.rem(self.row, 2)
        self.z = lax.rem(self.row // 2, zs)
        self.q = (self.clip * frames + self.frame) * xs + self.row // (2 * zs)
        self.clips, self.frames = flips(self.clip, clips), flips(self.frame, frames)
        self.xs = [v * 2 * zs + self.z * 2 + self.core for v in flips(self.row // (2 * zs), xs)]
        self.qs = flips(self.q, self.plane)
        self.all = 2 * self.plane
        self.g = self.q * 2 + self.core
        self.gs = flips(self.g, self.all)

    def beside(self, frame_too, step):
        frame = self.frames[1] if frame_too else self.frame
        return self.clip, frame, lax.rem(self.row + step + self.rows, self.rows)

    def other_core(self):
        return self.clip, self.frame, self.row + 1 - 2 * self.core

    def in_plane(self, d):
        n, m = len(self.xs), len(self.frames)
        return self.clips[d // (n * m)], self.frames[d // n % m], self.xs[d % n]

    def in_both(self, d):
        clip, frame, row = self.in_plane(d // 2)
        return clip, frame, row + (d % 2) * (1 - 2 * self.core)

    def in_column(self, d):
        z = lax.rem(self.z + d, self.zs)
        return self.clip, self.frame, self.row + (z - self.z) * 2


def remote(src, dst, send, recv, to):
    return pltpu.make_async_remote_copy(
        src_ref=src, dst_ref=dst, send_sem=send, recv_sem=recv, device_id=to, device_id_type=MESH
    )


class Stream:
    def __init__(self, s, spot, r):
        self.s, self.at, self.r = s, spot, r
        self.block = HALF // spot.plane

    def sems(self, phase):
        return self.r["sem_send"].at[self.s, phase], self.r["sem_got"].at[self.s, phase]

    def half(self, core):
        return pl.ds(pl.multiple_of(self.s * 2 * HALF + core * HALF, HALF), HALF)

    def rows(self, q):
        return pl.ds(pl.multiple_of(q * self.block, self.block), self.block)

    def total_rows(self, q):
        first = self.s * 2 * HALF + self.at.core * HALF + q * self.block
        return pl.ds(pl.multiple_of(first, self.block), self.block)

    def pair(self):
        src = self.r["pack"].at[self.half(1 - self.at.core)]
        return remote(src, self.r["pair_got"].at[self.s], *self.sems(0), self.at.other_core())

    def scatter(self, d):
        r, s = self.r, self.s
        src = r["chip"].at[s, self.at.qs[d]]
        return remote(src, r["plane_got"].at[s, d - 1], *self.sems(1), self.at.in_plane(d))

    def scatters(self):
        r, s, rest = self.r, self.s, pl.ds(0, self.at.plane - 1)
        return remote(
            r["chip"].at[s, rest], r["plane_got"].at[s, rest], *self.sems(1), self.at.other_core()
        )

    def column(self, d):
        r, s = self.r, self.s
        dst = r["column_got"].at[s, self.at.z]
        return remote(r["mine"].at[s], dst, *self.sems(2), self.at.in_column(d))

    def columns(self):
        ref = self.r["column_got"].at[self.s, pl.ds(0, self.at.zs - 1)]
        return remote(ref, ref, *self.sems(2), self.at.other_core())

    def gather(self, d):
        ref = self.r["total"].at[self.total_rows(self.at.q)]
        return remote(ref, ref, *self.sems(3), self.at.in_plane(d))

    def gathers(self):
        rows = (self.at.plane - 1) * self.block
        ref = self.r["total"].at[pl.ds(self.s * 2 * HALF, rows)]
        return remote(ref, ref, *self.sems(3), self.at.other_core())

    def hand_over(self):
        ref = self.r["total"].at[self.half(self.at.core)]
        return remote(ref, ref, *self.sems(4), self.at.other_core())

    def step_pair(self):
        self.pair().start()

    def step_scatter(self):
        r, s = self.r, self.s
        self.pair().wait_recv()
        own = r["pack"][self.half(self.at.core), :].astype(F32)
        own = (own + r["pair_got"][s].astype(F32)).astype(BF16)
        r["chip"][s] = own.reshape(self.at.plane, self.block, L)
        for d in range(1, self.at.plane):
            self.scatter(d).start()

    def step_column(self):
        r, s = self.r, self.s
        self.scatters().wait_recv()
        total = r["chip"][s, self.at.q].astype(F32)
        for d in range(self.at.plane - 1):
            total = total + r["plane_got"][s, d].astype(F32)
        total = total.astype(BF16)
        r["mine"][s] = total
        r["column_got"][s, self.at.z] = total
        for d in range(1, self.at.zs):
            self.column(d).start()

    def step_gather(self):
        r, s = self.r, self.s
        self.columns().wait_recv()
        total = r["column_got"][s, 0].astype(F32)
        for i in range(1, self.at.zs):
            total = total + r["column_got"][s, i].astype(F32)
        r["total"][self.total_rows(self.at.q), :] = total.astype(BF16)
        for d in range(1, self.at.plane):
            self.gather(d).start()

    def step_hand_over(self):
        self.gathers().wait_recv()
        self.hand_over().start()

    def step_end(self):
        self.hand_over().wait_recv()
        self.pair().wait_send()
        self.scatters().wait_send()
        self.columns().wait_send()
        self.gathers().wait_send()
        self.hand_over().wait_send()


class Direct:
    def __init__(self, s, spot, r):
        self.s, self.at, self.r = s, spot, r
        self.block = HALF // spot.all

    def sems(self, phase):
        return self.r["direct_send"].at[self.s, phase], self.r["direct_got"].at[self.s, phase]

    def rows(self, g):
        first = 2 * HALF + self.s * HALF + g * self.block
        return pl.ds(pl.multiple_of(first, self.block), self.block)

    def scatter(self, d):
        r, s = self.r, self.s
        src = r["pack"].at[self.rows(self.at.gs[d])]
        return remote(src, r["all_got"].at[s, d - 1], *self.sems(0), self.at.in_both(d))

    def scatters(self):
        ref = self.r["all_got"].at[self.s]
        return remote(ref, ref, *self.sems(0), self.at.other_core())

    def column(self, d):
        r, s = self.r, self.s
        dst = r["height_got"].at[s, self.at.z]
        return remote(r["part_sum"].at[s], dst, *self.sems(1), self.at.in_column(d))

    def columns(self):
        ref = self.r["height_got"].at[self.s, pl.ds(0, self.at.zs - 1)]
        return remote(ref, ref, *self.sems(1), self.at.other_core())

    def gather(self, d):
        ref = self.r["total"].at[self.rows(self.at.g)]
        return remote(ref, ref, *self.sems(2), self.at.in_both(d))

    def gathers(self):
        rows = (self.at.all - 1) * self.block
        ref = self.r["total"].at[pl.ds(2 * HALF + self.s * HALF, rows)]
        return remote(ref, ref, *self.sems(2), self.at.other_core())

    def step_scatter(self):
        for d in range(1, self.at.all):
            self.scatter(d).start()

    def step_column(self):
        r, s = self.r, self.s
        self.scatters().wait_recv()
        total = r["pack"][self.rows(self.at.g), :].astype(F32)
        for d in range(self.at.all - 1):
            total = total + r["all_got"][s, d].astype(F32)
        total = total.astype(BF16)
        r["part_sum"][s] = total
        r["height_got"][s, self.at.z] = total
        for d in range(1, self.at.zs):
            self.column(d).start()

    def step_gather(self):
        r, s = self.r, self.s
        self.columns().wait_recv()
        total = r["height_got"][s, 0].astype(F32)
        for i in range(1, self.at.zs):
            total = total + r["height_got"][s, i].astype(F32)
        r["total"][self.rows(self.at.g), :] = total.astype(BF16)
        for d in range(1, self.at.all):
            self.gather(d).start()

    def step_end(self):
        self.gathers().wait_recv()
        self.scatters().wait_send()
        self.columns().wait_send()
        self.gathers().wait_send()


def layer_kernel(sizes, names, *refs):
    r = dict(zip(names, refs, strict=True))
    spot = Spot(*sizes)

    def get(*wanted):
        return [r[name] for name in wanted]

    barrier = pltpu.get_barrier_semaphore()

    def greet(to):
        pl.semaphore_signal(barrier, inc=1, device_id=to, device_id_type=MESH)

    for frame_too in (False, True):
        for step in (-1, 1):
            greet(spot.beside(frame_too, step))
    for d in range(1, spot.plane):
        greet(spot.in_plane(d))
    for d in range(1, spot.zs):
        greet(spot.in_column(d))

    bit = lax.rem(spot.frame, 2)
    sh, rh = r["sh"], r["rh"]
    split, join = get("split", "join")

    def outward(kind, pick):
        ends = [
            (3 - bit, 2 * bit + 1, spot.beside(True, -1)),
            (1 - bit, 2 * bit, spot.beside(True, 0)),
            (2 + bit, 2 * bit + 1, spot.beside(False, -1)),
        ]
        return [
            remote(*pick(src, dst), sh.at[kind, i], rh.at[kind, i], to)
            for i, (src, dst, to) in enumerate(ends)
        ]

    def homeward(kind, pick):
        ends = [
            (2 * (1 - bit) + 1, 2 + bit, spot.beside(True, 1)),
            (2 * (1 - bit), bit, spot.beside(True, 0)),
            (2 * bit + 1, 2 + bit, spot.beside(False, 1)),
        ]
        return [
            remote(*pick(src, dst), sh.at[kind, i], rh.at[kind, i], to)
            for i, (src, dst, to) in enumerate(ends)
        ]

    x_send, x_got, d_send, d_got = get("x_send", "x_got", "d_send", "d_got")
    g_send, g_got = get("g_send", "g_got")
    x_copies = [
        outward(u, lambda a, b, u=u: (x_send.at[u, a], x_got.at[u, b])) for u in range(2)
    ]
    d_copies = outward(2, lambda a, b: (d_send.at[:, a], d_got.at[:, b]))
    g_copies = homeward(3, lambda a, b: (g_send.at[:, a], g_got.at[:, b]))
    copies = x_copies[0] + x_copies[1] + d_copies + g_copies

    make_perms(split, join)
    for name, rows in (("x_slab", "x"), ("d_slab", "d_out")):
        for part in range(2):
            r[name][pl.ds(part * L + C, L - C), :] = jnp.zeros((L - C, HALF), BF16)
        to_slab(r[name], r[rows].at[0, 0])
    split_blocks(r["x_slab"], split, x_send)
    for u in range(2):
        x_got[u, 2 * bit] = x_send[u, bit]
    split_blocks(r["d_slab"], split, d_send)
    for u in range(2):
        d_got[u, 2 * bit] = d_send[u, bit]
    make_masks(*get("mask_h", "mask_f"))
    make_weights(
        *get("w_self", "w_mut", "w_proj", "f1", "f2", "w_down"),
        *get("wn", "wt", "proj", "proj_t", "fc_n", "fc_t", "down"),
    )
    make_gain(r["g1"], r["col1"])
    make_gain(r["g2"], r["col2"])
    pl.semaphore_wait(barrier, 4 + spot.plane - 1 + spot.zs - 1)
    for copy in x_copies[0] + x_copies[1]:
        copy.start()
    for u in range(2):
        for copy in x_copies[u]:
            copy.wait_recv()
        if u == 1:
            for copy in d_copies:
                copy.start()
        join_blocks(u, x_got, join, r["win"])
        norm_one(u, *get("win", "col1", "n_cm", "n_tm"))
        project(u, *get("wt", "wn", "n_cm", "n_tm", "cm", "tm"))
        attend(u, *get("cm", "tm", "mask_h", "mask_f", "probs", "joined"))
    for copy in d_copies:
        copy.wait_recv()
    for u in range(2):
        join_blocks(u, d_got, join, r["d_win"])
    feed_forward(
        *get("win", "d_win", "joined", "col2", "proj", "proj_t", "fc_n", "fc_t", "down"),
        *get("hid", "dup", "n2", "datt", "dres", "dj", "acc"),
    )
    early_grads(*get("hid", "dup", "n2", "joined", "datt", "d_win", "acc", "pack"))
    early, cross, last = Stream(0, spot, r), Direct(0, spot, r), Direct(1, spot, r)
    early.step_pair()

    def in_cross(p):
        @pl.when(p == 3)
        def _():
            early.step_scatter()

    def in_self(p):
        @pl.when(p == 5)
        def _():
            early.step_column()

    back = get("cm", "tm", "mask_h", "probs", "dj", "dq", "d_tm")
    back_cross(*back, r["mask_f"], in_cross)
    cross_grads(*get("n_cm", "dq", "d_tm", "wn", "pack", "acc"))
    cross.step_scatter()
    back_self(*back, in_self)
    self_grads(*get("n_cm", "dq", "d_tm", "wn", "pack", "acc", "col1"))
    last.step_scatter()
    finish(0, 4, *get("win", "col1", "wn", "dq", "d_tm", "dres", "gi"))
    gi, out = get("gi", "out")
    for u in range(2):
        blocks = nt(gi[:, pl.ds(u * HALF, HALF)], join[...]).astype(BF16)
        for s in range(4):
            g_send[u, s] = blocks[:, s * L : (s + 1) * L]
        g_got[u, bit] = g_send[u, 2 * bit]
    cross.step_column()
    early.step_gather()
    last.step_column()
    for copy in g_copies:
        copy.start()
    cross.step_gather()
    last.step_gather()
    for copy in g_copies:
        copy.wait_recv()
    for part in range(2):
        both = [g_got[u, 2 * part + half] for half in range(2) for u in range(2)]
        rows = nt(jnp.concatenate(both, axis=1), split[...]).astype(BF16)
        for i in range(4):
            out[4 * (1 - part) + i] = rows[:C, i * W : (i + 1) * W]
    early.step_hand_over()
    cross.step_end()
    early.step_end()
    last.step_end()
    for copy in copies:
        copy.wait_send()


def unpack_kernel(scale, total, gi, out, o1, o_self, o_mut, o_proj, o2, o_f1, o_f2, o_down):
    def block(i):
        return total[pl.ds(i * L, L), :].astype(F32) * scale

    def beside(parts):
        wide_parts = [
            jnp.concatenate([p, jnp.zeros((L, 2 * L), F32)], axis=1) for p in parts
        ]
        joined = wide_parts[0] + pltpu.roll(wide_parts[1], C, 1) + pltpu.roll(wide_parts[2], 2 * C, 1)
        return joined[:C, : 3 * C]

    b = [block(i) for i in range(8 + 3 + 4)]
    o_down[...] = jnp.concatenate([b[0], b[1]], axis=0)[:MLP, :C]
    o2[...] = b[1][MLP - L : MLP - L + 1, :C]
    o_f1[...] = jnp.concatenate([b[2], b[3]], axis=1)[:C, :MLP]
    o_f2[...] = jnp.concatenate([b[4], b[5]], axis=1)[:C, :MLP]
    o_proj[...] = jnp.concatenate([b[6][:C], b[7][:C]], axis=0)[:, :C]
    o1[...] = b[12][C : C + 1, :C]
    o_mut[...] = beside(b[8:11])
    o_self[...] = beside(b[12:15])
    out[0, 0] = gi[...]


def vmem(*shape, dtype=BF16):
    return pltpu.VMEM(shape, dtype)


def shape(*dims, dtype=BF16):
    return jax.ShapeDtypeStruct(dims, dtype)


def in_vmem(count):
    return [pl.BlockSpec(memory_space=pltpu.VMEM)] * count


def solution(mesh):
    clips, frames, rows = mesh.shape["clip"], mesh.shape["frame"], mesh.shape["row"]
    zs = min(8, rows // 2)
    xs = rows // (2 * zs)
    sizes = (clips, frames, xs, zs)
    plane = clips * frames * xs
    dma = pltpu.SemaphoreType.DMA
    ins = ["x", "d_out", "g1", "w_self", "w_mut", "w_proj", "g2", "f1", "f2", "w_down"]
    scratch = dict(
        split=vmem(HALF, HALF), join=vmem(HALF, HALF), x_slab=vmem(2 * L, HALF), d_slab=vmem(2 * L, HALF),
        x_send=vmem(2, 4, L, L), x_got=vmem(2, 4, L, L), d_send=vmem(2, 4, L, L), d_got=vmem(2, 4, L, L),
        g_send=vmem(2, 4, L, L), g_got=vmem(2, 4, L, L), win=vmem(L, T), d_win=vmem(L, T),
        mask_h=vmem(L, HEADS * L), mask_f=vmem(L, HEADS * L),
        wn=vmem(L, 6 * L), wt=vmem(6 * L, L), proj=vmem(2 * L, L), proj_t=vmem(L, 2 * L),
        fc_n=vmem(L, 2 * M), fc_t=vmem(2 * M, L), down=vmem(M, L),
        col1=vmem(C, L, dtype=F32), col2=vmem(C, L, dtype=F32), acc=vmem(C, L, dtype=F32),
        n_cm=vmem(L, T), n_tm=vmem(T, L), cm=vmem(6 * L, T), tm=vmem(T, 4 * L),
        probs=vmem(T // L, 2 * L, HEADS * L), joined=vmem(2 * L, T),
        hid=vmem(M, T), dup=vmem(2 * M, T), n2=vmem(L, T), datt=vmem(L, T),
        dres=vmem(C, T, dtype=F32), dj=vmem(2 * L, T),
        dq=vmem(2 * L, T), d_tm=vmem(T, 4 * L), gi=vmem(L, T),
        pack=vmem(ROWS, L), pair_got=vmem(1, HALF, L), chip=vmem(1, plane, HALF // plane, L),
        plane_got=vmem(1, plane - 1, HALF // plane, L), mine=vmem(1, HALF // plane, L),
        column_got=vmem(1, zs, HALF // plane, L),
        sh=dma((4, 3)), rh=dma((4, 3)), sem_send=dma((1, 5)), sem_got=dma((1, 5)),
        direct_send=dma((2, 3)), direct_got=dma((2, 3)), all_got=vmem(2, 2 * plane - 1, HALF // (2 * plane), L),
        part_sum=vmem(2, HALF // (2 * plane), L), height_got=vmem(2, zs, HALF // (2 * plane), L),
    )
    names = [*ins, "out", "total", *scratch]

    def on_device(x, d_out, g1, w_self, w_mut, w_proj, g2, f1, f2, w_down):
        g1, g2 = g1.reshape(1, C), g2.reshape(1, C)
        gi, total = pl.pallas_call(
            lambda *refs: layer_kernel(sizes, names, *refs),
            out_shape=(shape(8, C, W), shape(ROWS, L)),
            in_specs=in_vmem(10),
            out_specs=tuple(in_vmem(2)),
            scratch_shapes=list(scratch.values()),
            compiler_params=pltpu.CompilerParams(
                collective_id=0, has_side_effects=True, vmem_limit_bytes=56 * 2**20
            ),
        )(x, d_out, g1, w_self, w_mut, w_proj, g2, f1, f2, w_down)
        scale = float(T * rows * frames * clips) ** -0.5
        out = pl.pallas_call(
            lambda *refs: unpack_kernel(scale, *refs),
            out_shape=(
                shape(1, 1, 8, C, W), shape(1, C, dtype=F32), shape(C, 3 * C, dtype=F32),
                shape(C, 3 * C, dtype=F32), shape(2 * C, C, dtype=F32), shape(1, C, dtype=F32),
                shape(C, MLP, dtype=F32), shape(C, MLP, dtype=F32), shape(MLP, C, dtype=F32),
            ),
            in_specs=in_vmem(2),
            out_specs=tuple(in_vmem(9)),
            compiler_params=pltpu.CompilerParams(vmem_limit_bytes=56 * 2**20),
        )(total, gi)
        out = list(out)
        out[1], out[5] = out[1].reshape(C), out[5].reshape(C)
        return tuple(out)

    whole = P("clip", "frame", "row", None, None)
    return jax.shard_map(
        on_device,
        mesh=mesh,
        in_specs=(whole, whole) + (P(),) * 8,
        out_specs=(whole,) + (P(),) * 8,
        check_vma=False,
    )
```

```python
import math

import jax
import jax.numpy as jnp
from jax import lax
from jax.experimental import pallas as pl
from jax.experimental.pallas import tpu as pltpu
from jax.sharding import PartitionSpec as P

F32 = jnp.float32
BF16 = jnp.bfloat16
MESH = pl.DeviceIdType.MESH

C = 120
L = 128
W = 128
HEADS = 6
HD = 20
MLP = 240
M = 256
T = 1024
HALF = 512
CH = 256
EPS = 1e-05
EXP_SCALE = float(HD) ** -0.5 * math.log2(math.e)
SCALE = float(HD) ** -0.5

EARLY = 8 * L
CROSS = EARLY
SELF = CROSS + 4 * L
ROWS = SELF + 4 * L


def nn(a, b):
    return lax.dot_general(a, b, (((1,), (0,)), ((), ())), preferred_element_type=F32)


def nt(a, b):
    return lax.dot_general(a, b, (((1,), (1,)), ((), ())), preferred_element_type=F32)


def iota(shape, dim):
    return lax.broadcasted_iota(jnp.int32, shape, dim)


def one_hot(mask):
    return jnp.where(mask, 1.0, 0.0).astype(BF16)


def pad_rows(v):
    return jnp.concatenate([v, jnp.zeros((L - C, v.shape[1]), F32)], axis=0).astype(BF16)


def norm_parts(v):
    mean = jnp.sum(v, axis=0, keepdims=True) * (1.0 / C)
    centre = v - mean
    var = jnp.sum(centre * centre, axis=0, keepdims=True) * (1.0 / C)
    inv = lax.rsqrt(var + EPS)
    return centre * inv, inv


def norm_back(xhat, inv, gain, dy):
    dh = dy * gain
    m1 = jnp.sum(dh, axis=0, keepdims=True) * (1.0 / C)
    m2 = jnp.sum(dh * xhat, axis=0, keepdims=True) * (1.0 / C)
    return inv * (dh - m1 - xhat * m2)


def gain_row(acc):
    full = jnp.concatenate([acc, jnp.zeros((L - C, L), F32)], axis=0)
    row = jnp.sum(jnp.transpose(full), axis=0, keepdims=True)
    return jnp.broadcast_to(row, (8, L))


def fold_lanes(v):
    out = v[:, :L]
    for i in range(1, v.shape[1] // L):
        out = out + v[:, i * L : (i + 1) * L]
    return out


def make_perms(split, join):
    o, i = iota((HALF, HALF), 1), iota((HALF, HALF), 0)
    column = (o >> 8) * 64 + ((o >> 5) & 7) * 8 + (o & 7) + 4
    split[...] = one_hot(i == ((o >> 3) & 3) * W + (column & (W - 1)))
    join[...] = one_hot(i == ((o >> 5) & 3) * L + (o >> 7) * 32 + (o & 31))


def make_masks(mask_h, mask_f):
    row, lane = iota((L, HEADS * L), 0), iota((L, HEADS * L), 1)
    h = lane >> 7
    mask_h[...] = one_hot((row >= h * HD) & (row < h * HD + HD))
    mask_f[...] = one_hot((row >> 6) != ((lane >> 6) & 1))


def make_weights(ws, wm, wp, f1, f2, wd, wn, wt, proj, proj_t, fc_n, fc_t, down):
    def rows128(ref):
        return pad_rows(ref[...].astype(F32))

    r, e = iota((3 * L, 3 * C), 0), iota((3 * L, 3 * C), 1)
    pad3 = one_hot((e == (r >> 7) * C + (r & (L - 1))) & ((r & (L - 1)) < C))
    for i, ref in enumerate((ws, wm)):
        w = rows128(ref)
        wt[pl.ds(i * 3 * L, 3 * L), :] = nt(pad3, w).astype(BF16)
        wn[:, pl.ds(i * 3 * L, 3 * L)] = nt(w, pad3).astype(BF16)
    r, e = iota((M, MLP), 0), iota((M, MLP), 1)
    pad_m = one_hot(r == e)
    pad2 = one_hot((e == (r >> 7) * C + (r & (L - 1))) & ((r & (L - 1)) < C))
    pad_l = one_hot(iota((C, L), 0) == iota((C, L), 1))
    eye = one_hot(iota((L, L), 0) == iota((L, L), 1))
    for i, ref in enumerate((f1, f2)):
        w = rows128(ref)
        fc_t[pl.ds(i * M, M), :] = nt(pad_m, w).astype(BF16)
        fc_n[:, pl.ds(i * M, M)] = nt(w, pad_m).astype(BF16)
    down[...] = nn(nn(pad_m, wd[...]).astype(BF16), pad_l).astype(BF16)
    padded = nn(nn(pad2, wp[...]).astype(BF16), pad_l).astype(BF16)
    proj[...] = padded
    proj_t[...] = nt(eye, padded).astype(BF16)


def make_gain(gain, col):
    col[...] = jnp.transpose(jnp.broadcast_to(gain[...], (L, C)))


def wide(col):
    return jnp.concatenate([col[...]] * (CH // L), axis=1)


def to_slab(slab, rows_ref):
    for i in range(8):
        slab[pl.ds((1 - i // 4) * L, C), pl.ds((i % 4) * W, W)] = rows_ref[i]


def split_blocks(slab, split, out):
    blocks = nn(slab[...], split[...]).astype(BF16)
    for part in range(2):
        for half in range(2):
            for u in range(2):
                first = half * CH + u * L
                out[u, 2 * part + half] = blocks[part * L : part * L + L, first : first + L]


def join_blocks(u, blocks, join, out):
    beside = jnp.concatenate([blocks[u, s] for s in range(4)], axis=1)
    out[:, pl.ds(u * HALF, HALF)] = nn(beside, join[...]).astype(BF16)


def norm_one(u, win, gain_col, out_cm, out_tm):
    gain = wide(gain_col)

    def step(i, carry):
        at = pl.ds(pl.multiple_of(i * CH, CH), CH)
        y = norm_parts(win[:, at].astype(F32)[:C])[0] * gain
        y = jnp.concatenate([y, jnp.zeros((L - C, CH), F32)], axis=0)
        out_cm[:, at] = y.astype(BF16)
        out_tm[at, :] = jnp.transpose(y).astype(BF16)
        return carry

    lax.fori_loop(u * 2, u * 2 + 2, step, 0, unroll=2)


def project(u, wt, wn, n_cm, n_tm, cm, tm):
    at = pl.ds(u * HALF, HALF)
    cm[:, at] = nn(wt[...], n_cm[:, at]).astype(BF16)
    tm[at, pl.ds(0, 2 * L)] = nn(n_tm[at, :], wn[:, pl.ds(L, 2 * L)]).astype(BF16)
    tm[at, pl.ds(2 * L, 2 * L)] = nn(n_tm[at, :], wn[:, pl.ds(4 * L, 2 * L)]).astype(BF16)


def spread(v, mask_h):
    return jnp.concatenate([v] * HEADS, axis=1) * mask_h[...]


def stacked(v):
    return jnp.concatenate([v[:, h * L : (h + 1) * L] for h in range(HEADS)], axis=0)


def other_frame(v):
    first = (iota((64, HEADS * L), 1) & 64) == 0
    return jnp.where(first, v[64:], v[:64])


def both_frames(v, mask_f):
    return jnp.concatenate([v, v], axis=0) * mask_f[...]


def softmax(scores):
    raised = jnp.exp2(scores * EXP_SCALE)
    return (raised * (1.0 / jnp.sum(raised, axis=0, keepdims=True))).astype(BF16)


def attend(cm, tm, mask_h, mask_f, probs, joined):
    def step(p, carry):
        at = pl.ds(pl.multiple_of(p * L, L), L)

        def group(i):
            return spread(cm[pl.ds(i * L, L), at], mask_h)

        pr = softmax(nn(tm[at, pl.ds(0, L)], group(0)))
        probs[p, pl.ds(0, L), :] = pr
        joined[pl.ds(L, L), at] = nn(group(2), stacked(pr)).astype(BF16)
        pr = softmax(other_frame(nn(tm[at, pl.ds(2 * L, L)], group(3))))
        pr = both_frames(pr, mask_f)
        probs[p, pl.ds(L, L), :] = pr
        joined[pl.ds(0, L), at] = nn(group(5), stacked(pr)).astype(BF16)
        return carry

    lax.fori_loop(0, T // L, step, 0, unroll=8)


def score_back(pr, d_pr):
    pr = pr.astype(F32)
    delta = jnp.sum(pr * d_pr, axis=0, keepdims=True)
    return (pr * (d_pr - delta)).astype(BF16)


def back_self(cm, tm, mask_h, probs, dj, dq, d_tm, between):
    def step(p, carry):
        at = pl.ds(pl.multiple_of(p * L, L), L)

        def group(i):
            return spread(cm[pl.ds(i * L, L), at], mask_h)

        pr = probs[p, pl.ds(0, L), :]
        do = spread(dj[pl.ds(L, L), at], mask_h)
        ds = score_back(pr, nn(tm[at, pl.ds(L, L)], do))
        dq[pl.ds(0, L), at] = (nn(group(1), stacked(ds)) * SCALE).astype(BF16)
        d_tm[at, pl.ds(0, L)] = (nt(ds, group(0)) * SCALE).astype(BF16)
        d_tm[at, pl.ds(L, L)] = nt(pr, do).astype(BF16)
        between(p)
        return carry

    lax.fori_loop(0, T // L, step, 0, unroll=8)


def back_cross(cm, tm, mask_h, probs, dj, dq, d_tm, mask_f, between):
    def step(p, carry):
        at = pl.ds(pl.multiple_of(p * L, L), L)

        def group(i):
            return spread(cm[pl.ds(i * L, L), at], mask_h)

        pr = probs[p, pl.ds(L, L), :]
        do = spread(dj[pl.ds(0, L), at], mask_h)
        ds = score_back(pr[:64] + pr[64:], other_frame(nn(tm[at, pl.ds(3 * L, L)], do)))
        ds = both_frames(ds, mask_f)
        dq[pl.ds(L, L), at] = (nn(group(4), stacked(ds)) * SCALE).astype(BF16)
        d_tm[at, pl.ds(2 * L, L)] = (nt(ds, group(3)) * SCALE).astype(BF16)
        d_tm[at, pl.ds(3 * L, L)] = nt(pr, do).astype(BF16)
        between(p)
        return carry

    lax.fori_loop(0, T // L, step, 0, unroll=8)


def feed_forward(
    win, d_win, joined, gain_col, proj, proj_t, fc_n, fc_t, down, hid, dup, n2, datt, dres, dj, acc
):
    gain = wide(gain_col)
    acc[...] = jnp.zeros_like(acc)

    def step(i, carry):
        at = pl.ds(pl.multiple_of(i * CH, CH), CH)
        att = nn(proj_t[...], joined[:, at]).astype(BF16).astype(F32)
        xhat, inv = norm_parts(win[:, at].astype(F32)[:C] + att[:C])
        normed = pad_rows(xhat * gain)
        n2[:, at] = normed
        up = nn(fc_t[...], normed)
        up_one, up_two = up[:M], up[M:]
        cdf = 0.5 * (1.0 + lax.erf(up_one * math.sqrt(0.5)))
        gelu = up_one * cdf
        slope = cdf + up_one * (
            jnp.exp2(up_one * up_one * (-0.5 * math.log2(math.e))) * (1.0 / math.sqrt(2.0 * math.pi))
        )
        hid[:, at] = (gelu * up_two).astype(BF16)
        grad = d_win[:, at]
        d_hid = nn(down[...], grad).astype(BF16).astype(F32)
        d_up = jnp.concatenate(
            [(d_hid * up_two * slope).astype(BF16), (d_hid * gelu).astype(BF16)], axis=0
        )
        dup[:, at] = d_up
        dn = nn(fc_n[...], d_up).astype(BF16).astype(F32)[:C]
        acc[...] += fold_lanes(dn * xhat)
        d_resid = grad.astype(F32)[:C] + norm_back(xhat, inv, gain, dn)
        dres[:, at] = d_resid
        da = pad_rows(d_resid)
        datt[:, at] = da
        dj[:, at] = nn(proj[...], da).astype(BF16)
        return carry

    lax.fori_loop(0, T // CH, step, 0, unroll=4)


def early_grads(hid, dup, n2, joined, datt, d_win, acc, pack):
    g = nt(hid[...], d_win[...])
    row = gain_row(acc[...])
    g = jnp.concatenate([g[:MLP], row, row], axis=0)
    pack[pl.ds(0, 2 * L), :] = g.astype(BF16)
    for i in range(2):
        g = nt(n2[...], dup[pl.ds(i * M, M), :]).astype(BF16)
        pack[pl.ds((2 + 2 * i) * L, L), :] = g[:, :L]
        pack[pl.ds((3 + 2 * i) * L, L), :] = g[:, L:]
    pack[pl.ds(6 * L, 2 * L), :] = nt(joined[...], datt[...]).astype(BF16)


def put_grads(pack, base, grads):
    for i, g in enumerate(grads):
        pack[pl.ds(base + i * L, L), :] = g.astype(BF16)
    pack[pl.ds(base + 3 * L, L), :] = jnp.zeros((L, L), BF16)


def by_weights(grads, wn, first):
    acc = jnp.zeros((L, L), F32)
    for i, g in enumerate(grads):
        acc = acc + g * wn[:, pl.ds((first + i) * L, L)].astype(F32)
    return acc[:C]


def cross_grads(n_cm, dq, d_tm, wn, pack, acc):
    g = nn(n_cm[...], d_tm[:, pl.ds(2 * L, 2 * L)])
    grads = [nt(n_cm[...], dq[pl.ds(L, L), :]), g[:, :L], g[:, L:]]
    put_grads(pack, CROSS, grads)
    acc[...] = by_weights(grads, wn, 3)


def self_grads(n_cm, dq, d_tm, wn, pack, acc, col):
    g = nn(n_cm[...], d_tm[:, pl.ds(0, 2 * L)])
    grads = [nt(n_cm[...], dq[pl.ds(0, L), :]), g[:, :L], g[:, L:]]
    row = gain_row((by_weights(grads, wn, 0) + acc[...]) / col[...])
    grads[0] = jnp.concatenate([grads[0][:C], row], axis=0)
    put_grads(pack, SELF, grads)


def finish(first, last, win, gain_col, wn, dq, d_tm, dres, gi):
    gain = wide(gain_col)

    def step(i, carry):
        at = pl.ds(pl.multiple_of(i * CH, CH), CH)
        d = (
            nt(wn[:, pl.ds(L, 2 * L)], d_tm[at, pl.ds(0, 2 * L)])
            + nt(wn[:, pl.ds(4 * L, 2 * L)], d_tm[at, pl.ds(2 * L, 2 * L)])
            + nn(wn[:, pl.ds(0, L)], dq[pl.ds(0, L), at])
            + nn(wn[:, pl.ds(3 * L, L)], dq[pl.ds(L, L), at])
        )
        d = d.astype(BF16).astype(F32)[:C]
        xhat, inv = norm_parts(win[:, at].astype(F32)[:C])
        gi[:, at] = pad_rows(dres[:, at] + norm_back(xhat, inv, gain, d))
        return carry

    lax.fori_loop(first, last, step, 0, unroll=4)


def flips(value, count):
    out = [value]
    step = 1
    while step < count:
        bit = lax.rem(value // step, 2)
        out += [v + step - 2 * step * bit for v in out]
        step *= 2
    return out


class Spot:
    def __init__(self, clips, frames, xs, zs):
        self.zs = zs
        self.rows = 2 * zs * xs
        self.plane = clips * frames * xs
        self.clip, self.frame, self.row = (lax.axis_index(a) for a in ("clip", "frame", "row"))
        self.core = lax.rem(self.row, 2)
        self.z = lax.rem(self.row // 2, zs)
        self.q = (self.clip * frames + self.frame) * xs + self.row // (2 * zs)
        self.clips, self.frames = flips(self.clip, clips), flips(self.frame, frames)
        self.xs = [v * 2 * zs + self.z * 2 + self.core for v in flips(self.row // (2 * zs), xs)]
        self.qs = flips(self.q, self.plane)
        self.all = 2 * self.plane
        self.g = self.q * 2 + self.core
        self.gs = flips(self.g, self.all)

    def beside(self, frame_too, step):
        frame = self.frames[1] if frame_too else self.frame
        return self.clip, frame, lax.rem(self.row + step + self.rows, self.rows)

    def other_core(self):
        return self.clip, self.frame, self.row + 1 - 2 * self.core

    def in_plane(self, d):
        n, m = len(self.xs), len(self.frames)
        return self.clips[d // (n * m)], self.frames[d // n % m], self.xs[d % n]

    def in_both(self, d):
        clip, frame, row = self.in_plane(d // 2)
        return clip, frame, row + (d % 2) * (1 - 2 * self.core)

    def in_column(self, d):
        z = lax.rem(self.z + d, self.zs)
        return self.clip, self.frame, self.row + (z - self.z) * 2


def remote(src, dst, send, recv, to):
    return pltpu.make_async_remote_copy(
        src_ref=src, dst_ref=dst, send_sem=send, recv_sem=recv, device_id=to, device_id_type=MESH
    )


class Stream:
    def __init__(self, s, spot, r):
        self.s, self.at, self.r = s, spot, r
        self.block = HALF // spot.plane

    def sems(self, phase):
        return self.r["sem_send"].at[self.s, phase], self.r["sem_got"].at[self.s, phase]

    def half(self, core):
        return pl.ds(pl.multiple_of(self.s * 2 * HALF + core * HALF, HALF), HALF)

    def rows(self, q):
        return pl.ds(pl.multiple_of(q * self.block, self.block), self.block)

    def total_rows(self, q):
        first = self.s * 2 * HALF + self.at.core * HALF + q * self.block
        return pl.ds(pl.multiple_of(first, self.block), self.block)

    def pair(self):
        src = self.r["pack"].at[self.half(1 - self.at.core)]
        return remote(src, self.r["pair_got"].at[self.s], *self.sems(0), self.at.other_core())

    def scatter(self, d):
        r, s = self.r, self.s
        src = r["chip"].at[s, self.at.qs[d]]
        return remote(src, r["plane_got"].at[s, d - 1], *self.sems(1), self.at.in_plane(d))

    def scatters(self):
        r, s, rest = self.r, self.s, pl.ds(0, self.at.plane - 1)
        return remote(
            r["chip"].at[s, rest], r["plane_got"].at[s, rest], *self.sems(1), self.at.other_core()
        )

    def column(self, d):
        r, s = self.r, self.s
        dst = r["column_got"].at[s, self.at.z]
        return remote(r["mine"].at[s], dst, *self.sems(2), self.at.in_column(d))

    def columns(self):
        ref = self.r["column_got"].at[self.s, pl.ds(0, self.at.zs - 1)]
        return remote(ref, ref, *self.sems(2), self.at.other_core())

    def gather(self, d):
        ref = self.r["total"].at[self.total_rows(self.at.q)]
        return remote(ref, ref, *self.sems(3), self.at.in_plane(d))

    def gathers(self):
        rows = (self.at.plane - 1) * self.block
        ref = self.r["total"].at[pl.ds(self.s * 2 * HALF, rows)]
        return remote(ref, ref, *self.sems(3), self.at.other_core())

    def hand_over(self):
        ref = self.r["total"].at[self.half(self.at.core)]
        return remote(ref, ref, *self.sems(4), self.at.other_core())

    def step_pair(self):
        self.pair().start()

    def step_scatter(self):
        r, s = self.r, self.s
        self.pair().wait_recv()
        own = r["pack"][self.half(self.at.core), :].astype(F32)
        own = (own + r["pair_got"][s].astype(F32)).astype(BF16)
        r["chip"][s] = own.reshape(self.at.plane, self.block, L)
        for d in range(1, self.at.plane):
            self.scatter(d).start()

    def step_column(self):
        r, s = self.r, self.s
        self.scatters().wait_recv()
        total = r["chip"][s, self.at.q].astype(F32)
        for d in range(self.at.plane - 1):
            total = total + r["plane_got"][s, d].astype(F32)
        total = total.astype(BF16)
        r["mine"][s] = total
        r["column_got"][s, self.at.z] = total
        for d in range(1, self.at.zs):
            self.column(d).start()

    def step_gather(self):
        r, s = self.r, self.s
        self.columns().wait_recv()
        total = r["column_got"][s, 0].astype(F32)
        for i in range(1, self.at.zs):
            total = total + r["column_got"][s, i].astype(F32)
        r["total"][self.total_rows(self.at.q), :] = total.astype(BF16)
        for d in range(1, self.at.plane):
            self.gather(d).start()

    def step_hand_over(self):
        self.gathers().wait_recv()
        self.hand_over().start()

    def step_end(self):
        self.hand_over().wait_recv()
        self.pair().wait_send()
        self.scatters().wait_send()
        self.columns().wait_send()
        self.gathers().wait_send()
        self.hand_over().wait_send()


class Direct:
    def __init__(self, s, spot, r):
        self.s, self.at, self.r = s, spot, r
        self.block = HALF // spot.all

    def sems(self, phase):
        return self.r["direct_send"].at[self.s, phase], self.r["direct_got"].at[self.s, phase]

    def rows(self, g):
        first = 2 * HALF + self.s * HALF + g * self.block
        return pl.ds(pl.multiple_of(first, self.block), self.block)

    def scatter(self, d):
        r, s = self.r, self.s
        src = r["pack"].at[self.rows(self.at.gs[d])]
        return remote(src, r["all_got"].at[s, d - 1], *self.sems(0), self.at.in_both(d))

    def scatters(self):
        ref = self.r["all_got"].at[self.s]
        return remote(ref, ref, *self.sems(0), self.at.other_core())

    def column(self, d):
        r, s = self.r, self.s
        dst = r["height_got"].at[s, self.at.z]
        return remote(r["part_sum"].at[s], dst, *self.sems(1), self.at.in_column(d))

    def columns(self):
        ref = self.r["height_got"].at[self.s, pl.ds(0, self.at.zs - 1)]
        return remote(ref, ref, *self.sems(1), self.at.other_core())

    def gather(self, d):
        ref = self.r["total"].at[self.rows(self.at.g)]
        return remote(ref, ref, *self.sems(2), self.at.in_both(d))

    def gathers(self):
        rows = (self.at.all - 1) * self.block
        ref = self.r["total"].at[pl.ds(2 * HALF + self.s * HALF, rows)]
        return remote(ref, ref, *self.sems(2), self.at.other_core())

    def step_scatter(self):
        for d in range(1, self.at.all):
            self.scatter(d).start()

    def step_column(self):
        r, s = self.r, self.s
        self.scatters().wait_recv()
        total = r["pack"][self.rows(self.at.g), :].astype(F32)
        for d in range(self.at.all - 1):
            total = total + r["all_got"][s, d].astype(F32)
        total = total.astype(BF16)
        r["part_sum"][s] = total
        r["height_got"][s, self.at.z] = total
        for d in range(1, self.at.zs):
            self.column(d).start()

    def step_gather(self):
        r, s = self.r, self.s
        self.columns().wait_recv()
        total = r["height_got"][s, 0].astype(F32)
        for i in range(1, self.at.zs):
            total = total + r["height_got"][s, i].astype(F32)
        r["total"][self.rows(self.at.g), :] = total.astype(BF16)
        for d in range(1, self.at.all):
            self.gather(d).start()

    def step_end(self):
        self.gathers().wait_recv()
        self.scatters().wait_send()
        self.columns().wait_send()
        self.gathers().wait_send()


def layer_kernel(sizes, names, *refs):
    r = dict(zip(names, refs, strict=True))
    spot = Spot(*sizes)

    def get(*wanted):
        return [r[name] for name in wanted]

    barrier = pltpu.get_barrier_semaphore()

    def greet(to):
        pl.semaphore_signal(barrier, inc=1, device_id=to, device_id_type=MESH)

    for frame_too in (False, True):
        for step in (-1, 1):
            greet(spot.beside(frame_too, step))
    for d in range(1, spot.plane):
        greet(spot.in_plane(d))
    for d in range(1, spot.zs):
        greet(spot.in_column(d))

    bit = lax.rem(spot.frame, 2)
    sh, rh = r["sh"], r["rh"]
    split, join = get("split", "join")

    def outward(kind, pick):
        ends = [
            (3 - bit, 2 * bit + 1, spot.beside(True, -1)),
            (1 - bit, 2 * bit, spot.beside(True, 0)),
            (2 + bit, 2 * bit + 1, spot.beside(False, -1)),
        ]
        return [
            remote(*pick(src, dst), sh.at[kind, i], rh.at[kind, i], to)
            for i, (src, dst, to) in enumerate(ends)
        ]

    def homeward(kind, pick):
        ends = [
            (2 * (1 - bit) + 1, 2 + bit, spot.beside(True, 1)),
            (2 * (1 - bit), bit, spot.beside(True, 0)),
            (2 * bit + 1, 2 + bit, spot.beside(False, 1)),
        ]
        return [
            remote(*pick(src, dst), sh.at[kind, i], rh.at[kind, i], to)
            for i, (src, dst, to) in enumerate(ends)
        ]

    x_send, x_got, d_send, d_got = get("x_send", "x_got", "d_send", "d_got")
    g_send, g_got = get("g_send", "g_got")
    x_copies = [
        outward(u, lambda a, b, u=u: (x_send.at[u, a], x_got.at[u, b])) for u in range(2)
    ]
    d_copies = outward(2, lambda a, b: (d_send.at[:, a], d_got.at[:, b]))
    g_copies = homeward(3, lambda a, b: (g_send.at[:, a], g_got.at[:, b]))
    copies = x_copies[0] + x_copies[1] + d_copies + g_copies

    make_perms(split, join)
    for name, rows in (("x_slab", "x"), ("d_slab", "d_out")):
        for part in range(2):
            r[name][pl.ds(part * L + C, L - C), :] = jnp.zeros((L - C, HALF), BF16)
        to_slab(r[name], r[rows].at[0, 0])
    split_blocks(r["x_slab"], split, x_send)
    for u in range(2):
        x_got[u, 2 * bit] = x_send[u, bit]
    split_blocks(r["d_slab"], split, d_send)
    for u in range(2):
        d_got[u, 2 * bit] = d_send[u, bit]
    make_masks(*get("mask_h", "mask_f"))
    make_weights(
        *get("w_self", "w_mut", "w_proj", "f1", "f2", "w_down"),
        *get("wn", "wt", "proj", "proj_t", "fc_n", "fc_t", "down"),
    )
    make_gain(r["g1"], r["col1"])
    make_gain(r["g2"], r["col2"])
    pl.semaphore_wait(barrier, 4 + spot.plane - 1 + spot.zs - 1)
    for copy in x_copies[0] + x_copies[1]:
        copy.start()
    for u in range(2):
        for copy in x_copies[u]:
            copy.wait_recv()
        if u == 1:
            for copy in d_copies:
                copy.start()
        join_blocks(u, x_got, join, r["win"])
        norm_one(u, *get("win", "col1", "n_cm", "n_tm"))
        project(u, *get("wt", "wn", "n_cm", "n_tm", "cm", "tm"))
    attend(*get("cm", "tm", "mask_h", "mask_f", "probs", "joined"))
    for copy in d_copies:
        copy.wait_recv()
    for u in range(2):
        join_blocks(u, d_got, join, r["d_win"])
    feed_forward(
        *get("win", "d_win", "joined", "col2", "proj", "proj_t", "fc_n", "fc_t", "down"),
        *get("hid", "dup", "n2", "datt", "dres", "dj", "acc"),
    )
    early_grads(*get("hid", "dup", "n2", "joined", "datt", "d_win", "acc", "pack"))
    early, cross, last = Stream(0, spot, r), Direct(0, spot, r), Direct(1, spot, r)
    early.step_pair()

    def in_cross(p):
        @pl.when(p == 3)
        def _():
            early.step_scatter()

    def in_self(p):
        @pl.when(p == 5)
        def _():
            early.step_column()

    back = get("cm", "tm", "mask_h", "probs", "dj", "dq", "d_tm")
    back_cross(*back, r["mask_f"], in_cross)
    cross_grads(*get("n_cm", "dq", "d_tm", "wn", "pack", "acc"))
    cross.step_scatter()
    back_self(*back, in_self)
    self_grads(*get("n_cm", "dq", "d_tm", "wn", "pack", "acc", "col1"))
    last.step_scatter()
    finish(0, 4, *get("win", "col1", "wn", "dq", "d_tm", "dres", "gi"))
    gi, out = get("gi", "out")
    for u in range(2):
        blocks = nt(gi[:, pl.ds(u * HALF, HALF)], join[...]).astype(BF16)
        for s in range(4):
            g_send[u, s] = blocks[:, s * L : (s + 1) * L]
        g_got[u, bit] = g_send[u, 2 * bit]
    cross.step_column()
    early.step_gather()
    last.step_column()
    for copy in g_copies:
        copy.start()
    cross.step_gather()
    last.step_gather()
    for copy in g_copies:
        copy.wait_recv()
    for part in range(2):
        both = [g_got[u, 2 * part + half] for half in range(2) for u in range(2)]
        rows = nt(jnp.concatenate(both, axis=1), split[...]).astype(BF16)
        for i in range(4):
            out[4 * (1 - part) + i] = rows[:C, i * W : (i + 1) * W]
    early.step_hand_over()
    cross.step_end()
    early.step_end()
    last.step_end()
    for copy in copies:
        copy.wait_send()


def unpack_kernel(scale, total, gi, out, o1, o_self, o_mut, o_proj, o2, o_f1, o_f2, o_down):
    def block(i):
        return total[pl.ds(i * L, L), :].astype(F32) * scale

    def beside(parts):
        wide_parts = [
            jnp.concatenate([p, jnp.zeros((L, 2 * L), F32)], axis=1) for p in parts
        ]
        joined = wide_parts[0] + pltpu.roll(wide_parts[1], C, 1) + pltpu.roll(wide_parts[2], 2 * C, 1)
        return joined[:C, : 3 * C]

    b = [block(i) for i in range(8 + 3 + 4)]
    o_down[...] = jnp.concatenate([b[0], b[1]], axis=0)[:MLP, :C]
    o2[...] = b[1][MLP - L : MLP - L + 1, :C]
    o_f1[...] = jnp.concatenate([b[2], b[3]], axis=1)[:C, :MLP]
    o_f2[...] = jnp.concatenate([b[4], b[5]], axis=1)[:C, :MLP]
    o_proj[...] = jnp.concatenate([b[6][:C], b[7][:C]], axis=0)[:, :C]
    o1[...] = b[12][C : C + 1, :C]
    o_mut[...] = beside(b[8:11])
    o_self[...] = beside(b[12:15])
    out[0, 0] = gi[...]


def vmem(*shape, dtype=BF16):
    return pltpu.VMEM(shape, dtype)


def shape(*dims, dtype=BF16):
    return jax.ShapeDtypeStruct(dims, dtype)


def in_vmem(count):
    return [pl.BlockSpec(memory_space=pltpu.VMEM)] * count


def solution(mesh):
    clips, frames, rows = mesh.shape["clip"], mesh.shape["frame"], mesh.shape["row"]
    zs = min(8, rows // 2)
    xs = rows // (2 * zs)
    sizes = (clips, frames, xs, zs)
    plane = clips * frames * xs
    dma = pltpu.SemaphoreType.DMA
    ins = ["x", "d_out", "g1", "w_self", "w_mut", "w_proj", "g2", "f1", "f2", "w_down"]
    scratch = dict(
        split=vmem(HALF, HALF), join=vmem(HALF, HALF), x_slab=vmem(2 * L, HALF), d_slab=vmem(2 * L, HALF),
        x_send=vmem(2, 4, L, L), x_got=vmem(2, 4, L, L), d_send=vmem(2, 4, L, L), d_got=vmem(2, 4, L, L),
        g_send=vmem(2, 4, L, L), g_got=vmem(2, 4, L, L), win=vmem(L, T), d_win=vmem(L, T),
        mask_h=vmem(L, HEADS * L), mask_f=vmem(L, HEADS * L),
        wn=vmem(L, 6 * L), wt=vmem(6 * L, L), proj=vmem(2 * L, L), proj_t=vmem(L, 2 * L),
        fc_n=vmem(L, 2 * M), fc_t=vmem(2 * M, L), down=vmem(M, L),
        col1=vmem(C, L, dtype=F32), col2=vmem(C, L, dtype=F32), acc=vmem(C, L, dtype=F32),
        n_cm=vmem(L, T), n_tm=vmem(T, L), cm=vmem(6 * L, T), tm=vmem(T, 4 * L),
        probs=vmem(T // L, 2 * L, HEADS * L), joined=vmem(2 * L, T),
        hid=vmem(M, T), dup=vmem(2 * M, T), n2=vmem(L, T), datt=vmem(L, T),
        dres=vmem(C, T, dtype=F32), dj=vmem(2 * L, T),
        dq=vmem(2 * L, T), d_tm=vmem(T, 4 * L), gi=vmem(L, T),
        pack=vmem(ROWS, L), pair_got=vmem(1, HALF, L), chip=vmem(1, plane, HALF // plane, L),
        plane_got=vmem(1, plane - 1, HALF // plane, L), mine=vmem(1, HALF // plane, L),
        column_got=vmem(1, zs, HALF // plane, L),
        sh=dma((4, 3)), rh=dma((4, 3)), sem_send=dma((1, 5)), sem_got=dma((1, 5)),
        direct_send=dma((2, 3)), direct_got=dma((2, 3)), all_got=vmem(2, 2 * plane - 1, HALF // (2 * plane), L),
        part_sum=vmem(2, HALF // (2 * plane), L), height_got=vmem(2, zs, HALF // (2 * plane), L),
    )
    names = [*ins, "out", "total", *scratch]

    def on_device(x, d_out, g1, w_self, w_mut, w_proj, g2, f1, f2, w_down):
        g1, g2 = g1.reshape(1, C), g2.reshape(1, C)
        gi, total = pl.pallas_call(
            lambda *refs: layer_kernel(sizes, names, *refs),
            out_shape=(shape(8, C, W), shape(ROWS, L)),
            in_specs=in_vmem(10),
            out_specs=tuple(in_vmem(2)),
            scratch_shapes=list(scratch.values()),
            compiler_params=pltpu.CompilerParams(
                collective_id=0, has_side_effects=True, vmem_limit_bytes=56 * 2**20
            ),
        )(x, d_out, g1, w_self, w_mut, w_proj, g2, f1, f2, w_down)
        scale = float(T * rows * frames * clips) ** -0.5
        out = pl.pallas_call(
            lambda *refs: unpack_kernel(scale, *refs),
            out_shape=(
                shape(1, 1, 8, C, W), shape(1, C, dtype=F32), shape(C, 3 * C, dtype=F32),
                shape(C, 3 * C, dtype=F32), shape(2 * C, C, dtype=F32), shape(1, C, dtype=F32),
                shape(C, MLP, dtype=F32), shape(C, MLP, dtype=F32), shape(MLP, C, dtype=F32),
            ),
            in_specs=in_vmem(2),
            out_specs=tuple(in_vmem(9)),
            compiler_params=pltpu.CompilerParams(vmem_limit_bytes=56 * 2**20),
        )(total, gi)
        out = list(out)
        out[1], out[5] = out[1].reshape(C), out[5].reshape(C)
        return tuple(out)

    whole = P("clip", "frame", "row", None, None)
    return jax.shard_map(
        on_device,
        mesh=mesh,
        in_specs=(whole, whole) + (P(),) * 8,
        out_specs=(whole,) + (P(),) * 8,
        check_vma=False,
    )
```

```python
import math

import jax
import jax.numpy as jnp
from jax import lax
from jax.experimental import pallas as pl
from jax.experimental.pallas import tpu as pltpu
from jax.sharding import PartitionSpec as P

F32 = jnp.float32
BF16 = jnp.bfloat16
MESH = pl.DeviceIdType.MESH

C = 120
L = 128
W = 128
HEADS = 6
HD = 20
MLP = 240
M = 256
T = 1024
HALF = 512
CH = 256
EPS = 1e-05
EXP_SCALE = float(HD) ** -0.5 * math.log2(math.e)
SCALE = float(HD) ** -0.5

EARLY = 8 * L
CROSS = EARLY
SELF = CROSS + 4 * L
ROWS = SELF + 4 * L


def nn(a, b):
    return lax.dot_general(a, b, (((1,), (0,)), ((), ())), preferred_element_type=F32)


def nt(a, b):
    return lax.dot_general(a, b, (((1,), (1,)), ((), ())), preferred_element_type=F32)


def iota(shape, dim):
    return lax.broadcasted_iota(jnp.int32, shape, dim)


def one_hot(mask):
    return jnp.where(mask, 1.0, 0.0).astype(BF16)


def pad_rows(v):
    return jnp.concatenate([v, jnp.zeros((L - C, v.shape[1]), F32)], axis=0).astype(BF16)


def norm_parts(v):
    mean = jnp.sum(v, axis=0, keepdims=True) * (1.0 / C)
    centre = v - mean
    var = jnp.sum(centre * centre, axis=0, keepdims=True) * (1.0 / C)
    inv = lax.rsqrt(var + EPS)
    return centre * inv, inv


def norm_back(xhat, inv, gain, dy):
    dh = dy * gain
    m1 = jnp.sum(dh, axis=0, keepdims=True) * (1.0 / C)
    m2 = jnp.sum(dh * xhat, axis=0, keepdims=True) * (1.0 / C)
    return inv * (dh - m1 - xhat * m2)


def gain_row(acc):
    full = jnp.concatenate([acc, jnp.zeros((L - C, L), F32)], axis=0)
    row = jnp.sum(jnp.transpose(full), axis=0, keepdims=True)
    return jnp.broadcast_to(row, (8, L))


def fold_lanes(v):
    out = v[:, :L]
    for i in range(1, v.shape[1] // L):
        out = out + v[:, i * L : (i + 1) * L]
    return out


def make_perms(split, join):
    o, i = iota((HALF, HALF), 1), iota((HALF, HALF), 0)
    column = (o >> 8) * 64 + ((o >> 5) & 7) * 8 + (o & 7) + 4
    split[...] = one_hot(i == ((o >> 3) & 3) * W + (column & (W - 1)))
    join[...] = one_hot(i == ((o >> 5) & 3) * L + (o >> 7) * 32 + (o & 31))


def make_masks(mask_h, mask_f):
    row, lane = iota((L, HEADS * L), 0), iota((L, HEADS * L), 1)
    h = lane >> 7
    mask_h[...] = one_hot((row >= h * HD) & (row < h * HD + HD))
    mask_f[...] = one_hot((row >> 6) != ((lane >> 6) & 1))


def make_weights(ws, wm, wp, f1, f2, wd, wn, wt, proj, proj_t, fc_n, fc_t, down):
    def rows128(ref):
        return pad_rows(ref[...].astype(F32))

    r, e = iota((3 * L, 3 * C), 0), iota((3 * L, 3 * C), 1)
    pad3 = one_hot((e == (r >> 7) * C + (r & (L - 1))) & ((r & (L - 1)) < C))
    for i, ref in enumerate((ws, wm)):
        w = rows128(ref)
        wt[pl.ds(i * 3 * L, 3 * L), :] = nt(pad3, w).astype(BF16)
        wn[:, pl.ds(i * 3 * L, 3 * L)] = nt(w, pad3).astype(BF16)
    r, e = iota((M, MLP), 0), iota((M, MLP), 1)
    pad_m = one_hot(r == e)
    pad2 = one_hot((e == (r >> 7) * C + (r & (L - 1))) & ((r & (L - 1)) < C))
    pad_l = one_hot(iota((C, L), 0) == iota((C, L), 1))
    eye = one_hot(iota((L, L), 0) == iota((L, L), 1))
    for i, ref in enumerate((f1, f2)):
        w = rows128(ref)
        fc_t[pl.ds(i * M, M), :] = nt(pad_m, w).astype(BF16)
        fc_n[:, pl.ds(i * M, M)] = nt(w, pad_m).astype(BF16)
    down[...] = nn(nn(pad_m, wd[...]).astype(BF16), pad_l).astype(BF16)
    padded = nn(nn(pad2, wp[...]).astype(BF16), pad_l).astype(BF16)
    proj[...] = padded
    proj_t[...] = nt(eye, padded).astype(BF16)


def make_gain(gain, col):
    col[...] = jnp.transpose(jnp.broadcast_to(gain[...], (L, C)))


def wide(col):
    return jnp.concatenate([col[...]] * (CH // L), axis=1)


def to_slab(slab, rows_ref):
    for i in range(8):
        slab[pl.ds((1 - i // 4) * L, C), pl.ds((i % 4) * W, W)] = rows_ref[i]


def split_blocks(slab, split, out):
    blocks = nn(slab[...], split[...]).astype(BF16)
    for part in range(2):
        for half in range(2):
            for u in range(2):
                first = half * CH + u * L
                out[u, 2 * part + half] = blocks[part * L : part * L + L, first : first + L]


def join_blocks(u, blocks, join, out):
    beside = jnp.concatenate([blocks[u, s] for s in range(4)], axis=1)
    out[:, pl.ds(u * HALF, HALF)] = nn(beside, join[...]).astype(BF16)


def norm_one(u, win, gain_col, out_cm, out_tm):
    gain = wide(gain_col)

    def step(i, carry):
        at = pl.ds(pl.multiple_of(i * CH, CH), CH)
        y = norm_parts(win[:, at].astype(F32)[:C])[0] * gain
        y = jnp.concatenate([y, jnp.zeros((L - C, CH), F32)], axis=0)
        out_cm[:, at] = y.astype(BF16)
        out_tm[at, :] = jnp.transpose(y).astype(BF16)
        return carry

    lax.fori_loop(u * 2, u * 2 + 2, step, 0, unroll=2)


def project(u, wt, wn, n_cm, n_tm, cm, tm):
    at = pl.ds(u * HALF, HALF)
    cm[:, at] = nn(wt[...], n_cm[:, at]).astype(BF16)
    tm[at, pl.ds(0, 2 * L)] = nn(n_tm[at, :], wn[:, pl.ds(L, 2 * L)]).astype(BF16)
    tm[at, pl.ds(2 * L, 2 * L)] = nn(n_tm[at, :], wn[:, pl.ds(4 * L, 2 * L)]).astype(BF16)


def spread(v, mask_h):
    return jnp.concatenate([v] * HEADS, axis=1) * mask_h[...]


def stacked(v):
    return jnp.concatenate([v[:, h * L : (h + 1) * L] for h in range(HEADS)], axis=0)


def other_frame(v):
    first = (iota((64, HEADS * L), 1) & 64) == 0
    return jnp.where(first, v[64:], v[:64])


def both_frames(v, mask_f):
    return jnp.concatenate([v, v], axis=0) * mask_f[...]


def softmax(scores):
    raised = jnp.exp2(scores * EXP_SCALE)
    return (raised * (1.0 / jnp.sum(raised, axis=0, keepdims=True))).astype(BF16)


def attend(cm, tm, mask_h, mask_f, probs, joined):
    def step(p, carry):
        at = pl.ds(pl.multiple_of(p * L, L), L)

        def group(i):
            return spread(cm[pl.ds(i * L, L), at], mask_h)

        pr = softmax(nn(tm[at, pl.ds(0, L)], group(0)))
        probs[p, pl.ds(0, L), :] = pr
        joined[pl.ds(L, L), at] = nn(group(2), stacked(pr)).astype(BF16)
        pr = softmax(other_frame(nn(tm[at, pl.ds(2 * L, L)], group(3))))
        pr = both_frames(pr, mask_f)
        probs[p, pl.ds(L, L), :] = pr
        joined[pl.ds(0, L), at] = nn(group(5), stacked(pr)).astype(BF16)
        return carry

    lax.fori_loop(0, T // L, step, 0, unroll=8)


def score_back(pr, d_pr):
    pr = pr.astype(F32)
    delta = jnp.sum(pr * d_pr, axis=0, keepdims=True)
    return (pr * (d_pr - delta)).astype(BF16)


def back_self(cm, tm, mask_h, probs, dj, dq, d_tm, between):
    def step(p, carry):
        at = pl.ds(pl.multiple_of(p * L, L), L)

        def group(i):
            return spread(cm[pl.ds(i * L, L), at], mask_h)

        pr = probs[p, pl.ds(0, L), :]
        do = spread(dj[pl.ds(L, L), at], mask_h)
        ds = score_back(pr, nn(tm[at, pl.ds(L, L)], do))
        dq[pl.ds(0, L), at] = (nn(group(1), stacked(ds)) * SCALE).astype(BF16)
        d_tm[at, pl.ds(0, L)] = (nt(ds, group(0)) * SCALE).astype(BF16)
        d_tm[at, pl.ds(L, L)] = nt(pr, do).astype(BF16)
        between(p)
        return carry

    lax.fori_loop(0, T // L, step, 0, unroll=8)


def back_cross(cm, tm, mask_h, probs, dj, dq, d_tm, mask_f, between):
    def step(p, carry):
        at = pl.ds(pl.multiple_of(p * L, L), L)

        def group(i):
            return spread(cm[pl.ds(i * L, L), at], mask_h)

        pr = probs[p, pl.ds(L, L), :]
        do = spread(dj[pl.ds(0, L), at], mask_h)
        ds = score_back(pr[:64] + pr[64:], other_frame(nn(tm[at, pl.ds(3 * L, L)], do)))
        ds = both_frames(ds, mask_f)
        dq[pl.ds(L, L), at] = (nn(group(4), stacked(ds)) * SCALE).astype(BF16)
        d_tm[at, pl.ds(2 * L, L)] = (nt(ds, group(3)) * SCALE).astype(BF16)
        d_tm[at, pl.ds(3 * L, L)] = nt(pr, do).astype(BF16)
        between(p)
        return carry

    lax.fori_loop(0, T // L, step, 0, unroll=8)


def feed_forward(
    win, d_win, joined, gain_col, proj, proj_t, fc_n, fc_t, down, hid, dup, n2, datt, dres, dj, acc
):
    gain = wide(gain_col)
    acc[...] = jnp.zeros_like(acc)

    def step(i, carry):
        at = pl.ds(pl.multiple_of(i * CH, CH), CH)
        att = nn(proj_t[...], joined[:, at]).astype(BF16).astype(F32)
        xhat, inv = norm_parts(win[:, at].astype(F32)[:C] + att[:C])
        normed = pad_rows(xhat * gain)
        n2[:, at] = normed
        up = nn(fc_t[...], normed)
        up_one, up_two = up[:M], up[M:]
        cdf = 0.5 * (1.0 + lax.erf(up_one * math.sqrt(0.5)))
        gelu = up_one * cdf
        slope = cdf + up_one * (
            jnp.exp2(up_one * up_one * (-0.5 * math.log2(math.e))) * (1.0 / math.sqrt(2.0 * math.pi))
        )
        hid[:, at] = (gelu * up_two).astype(BF16)
        grad = d_win[:, at]
        d_hid = nn(down[...], grad).astype(BF16).astype(F32)
        d_up = jnp.concatenate(
            [(d_hid * up_two * slope).astype(BF16), (d_hid * gelu).astype(BF16)], axis=0
        )
        dup[:, at] = d_up
        dn = nn(fc_n[...], d_up).astype(BF16).astype(F32)[:C]
        acc[...] += fold_lanes(dn * xhat)
        d_resid = grad.astype(F32)[:C] + norm_back(xhat, inv, gain, dn)
        dres[:, at] = d_resid
        da = pad_rows(d_resid)
        datt[:, at] = da
        dj[:, at] = nn(proj[...], da).astype(BF16)
        return carry

    lax.fori_loop(0, T // CH, step, 0, unroll=4)


def early_grads(hid, dup, n2, joined, datt, d_win, acc, pack):
    g = nt(hid[...], d_win[...])
    row = gain_row(acc[...])
    g = jnp.concatenate([g[:MLP], row, row], axis=0)
    pack[pl.ds(0, 2 * L), :] = g.astype(BF16)
    for i in range(2):
        g = nt(n2[...], dup[pl.ds(i * M, M), :]).astype(BF16)
        pack[pl.ds((2 + 2 * i) * L, L), :] = g[:, :L]
        pack[pl.ds((3 + 2 * i) * L, L), :] = g[:, L:]
    pack[pl.ds(6 * L, 2 * L), :] = nt(joined[...], datt[...]).astype(BF16)


def put_grads(pack, base, grads):
    for i, g in enumerate(grads):
        pack[pl.ds(base + i * L, L), :] = g.astype(BF16)
    pack[pl.ds(base + 3 * L, L), :] = jnp.zeros((L, L), BF16)


def by_weights(grads, wn, first):
    acc = jnp.zeros((L, L), F32)
    for i, g in enumerate(grads):
        acc = acc + g * wn[:, pl.ds((first + i) * L, L)].astype(F32)
    return acc[:C]


def cross_grads(n_cm, dq, d_tm, wn, pack, acc):
    g = nn(n_cm[...], d_tm[:, pl.ds(2 * L, 2 * L)])
    grads = [nt(n_cm[...], dq[pl.ds(L, L), :]), g[:, :L], g[:, L:]]
    put_grads(pack, CROSS, grads)
    acc[...] = by_weights(grads, wn, 3)


def self_grads(n_cm, dq, d_tm, wn, pack, acc, col):
    g = nn(n_cm[...], d_tm[:, pl.ds(0, 2 * L)])
    grads = [nt(n_cm[...], dq[pl.ds(0, L), :]), g[:, :L], g[:, L:]]
    row = gain_row((by_weights(grads, wn, 0) + acc[...]) / col[...])
    grads[0] = jnp.concatenate([grads[0][:C], row], axis=0)
    put_grads(pack, SELF, grads)


def finish(first, last, win, gain_col, wn, dq, d_tm, dres, gi):
    gain = wide(gain_col)

    def step(i, carry):
        at = pl.ds(pl.multiple_of(i * CH, CH), CH)
        d = (
            nt(wn[:, pl.ds(L, 2 * L)], d_tm[at, pl.ds(0, 2 * L)])
            + nt(wn[:, pl.ds(4 * L, 2 * L)], d_tm[at, pl.ds(2 * L, 2 * L)])
            + nn(wn[:, pl.ds(0, L)], dq[pl.ds(0, L), at])
            + nn(wn[:, pl.ds(3 * L, L)], dq[pl.ds(L, L), at])
        )
        d = d.astype(BF16).astype(F32)[:C]
        xhat, inv = norm_parts(win[:, at].astype(F32)[:C])
        gi[:, at] = pad_rows(dres[:, at] + norm_back(xhat, inv, gain, d))
        return carry

    lax.fori_loop(first, last, step, 0, unroll=4)


def flips(value, count):
    out = [value]
    step = 1
    while step < count:
        bit = lax.rem(value // step, 2)
        out += [v + step - 2 * step * bit for v in out]
        step *= 2
    return out


RING = (0, 1, 2, 1)


def farthest(count, hops):
    return sorted(range(1, count), key=hops, reverse=True)


class Spot:
    def __init__(self, clips, frames, xs, zs):
        self.zs = zs
        self.rows = 2 * zs * xs
        self.plane = clips * frames * xs
        self.clip, self.frame, self.row = (lax.axis_index(a) for a in ("clip", "frame", "row"))
        self.core = lax.rem(self.row, 2)
        self.z = lax.rem(self.row // 2, zs)
        self.q = (self.clip * frames + self.frame) * xs + self.row // (2 * zs)
        self.clips, self.frames = flips(self.clip, clips), flips(self.frame, frames)
        self.xs = [v * 2 * zs + self.z * 2 + self.core for v in flips(self.row // (2 * zs), xs)]
        self.qs = flips(self.q, self.plane)
        self.all = 2 * self.plane
        self.g = self.q * 2 + self.core
        self.gs = flips(self.g, self.all)

        n, m = xs, frames

        def hops(d):
            return RING[(d // (n * m) * 2 + d % n) % 4] + RING[d // n % m % 4]

        self.plane_order = farthest(self.plane, hops)
        self.both_order = farthest(self.all, lambda d: hops(d // 2))
        self.column_order = farthest(zs, lambda d: min(d, zs - d))

    def beside(self, frame_too, step):
        frame = self.frames[1] if frame_too else self.frame
        return self.clip, frame, lax.rem(self.row + step + self.rows, self.rows)

    def other_core(self):
        return self.clip, self.frame, self.row + 1 - 2 * self.core

    def in_plane(self, d):
        n, m = len(self.xs), len(self.frames)
        return self.clips[d // (n * m)], self.frames[d // n % m], self.xs[d % n]

    def in_both(self, d):
        clip, frame, row = self.in_plane(d // 2)
        return clip, frame, row + (d % 2) * (1 - 2 * self.core)

    def in_column(self, d):
        z = lax.rem(self.z + d, self.zs)
        return self.clip, self.frame, self.row + (z - self.z) * 2


def remote(src, dst, send, recv, to):
    return pltpu.make_async_remote_copy(
        src_ref=src, dst_ref=dst, send_sem=send, recv_sem=recv, device_id=to, device_id_type=MESH
    )


class Stream:
    def __init__(self, s, spot, r):
        self.s, self.at, self.r = s, spot, r
        self.block = HALF // spot.plane

    def sems(self, phase):
        return self.r["sem_send"].at[self.s, phase], self.r["sem_got"].at[self.s, phase]

    def half(self, core):
        return pl.ds(pl.multiple_of(self.s * 2 * HALF + core * HALF, HALF), HALF)

    def rows(self, q):
        return pl.ds(pl.multiple_of(q * self.block, self.block), self.block)

    def total_rows(self, q):
        first = self.s * 2 * HALF + self.at.core * HALF + q * self.block
        return pl.ds(pl.multiple_of(first, self.block), self.block)

    def pair(self):
        src = self.r["pack"].at[self.half(1 - self.at.core)]
        return remote(src, self.r["pair_got"].at[self.s], *self.sems(0), self.at.other_core())

    def scatter(self, d):
        r, s = self.r, self.s
        src = r["chip"].at[s, self.at.qs[d]]
        return remote(src, r["plane_got"].at[s, d - 1], *self.sems(1), self.at.in_plane(d))

    def scatters(self):
        r, s, rest = self.r, self.s, pl.ds(0, self.at.plane - 1)
        return remote(
            r["chip"].at[s, rest], r["plane_got"].at[s, rest], *self.sems(1), self.at.other_core()
        )

    def column(self, d):
        r, s = self.r, self.s
        dst = r["column_got"].at[s, self.at.z]
        return remote(r["mine"].at[s], dst, *self.sems(2), self.at.in_column(d))

    def columns(self):
        ref = self.r["column_got"].at[self.s, pl.ds(0, self.at.zs - 1)]
        return remote(ref, ref, *self.sems(2), self.at.other_core())

    def gather(self, d):
        ref = self.r["total"].at[self.total_rows(self.at.q)]
        return remote(ref, ref, *self.sems(3), self.at.in_plane(d))

    def gathers(self):
        rows = (self.at.plane - 1) * self.block
        ref = self.r["total"].at[pl.ds(self.s * 2 * HALF, rows)]
        return remote(ref, ref, *self.sems(3), self.at.other_core())

    def hand_over(self):
        ref = self.r["total"].at[self.half(self.at.core)]
        return remote(ref, ref, *self.sems(4), self.at.other_core())

    def step_pair(self):
        self.pair().start()

    def step_scatter(self):
        r, s = self.r, self.s
        self.pair().wait_recv()
        own = r["pack"][self.half(self.at.core), :].astype(F32)
        own = (own + r["pair_got"][s].astype(F32)).astype(BF16)
        r["chip"][s] = own.reshape(self.at.plane, self.block, L)
        for d in self.at.plane_order:
            self.scatter(d).start()

    def step_column(self):
        r, s = self.r, self.s
        self.scatters().wait_recv()
        total = r["chip"][s, self.at.q].astype(F32)
        for d in range(self.at.plane - 1):
            total = total + r["plane_got"][s, d].astype(F32)
        total = total.astype(BF16)
        r["mine"][s] = total
        r["column_got"][s, self.at.z] = total
        for d in self.at.column_order:
            self.column(d).start()

    def step_gather(self):
        r, s = self.r, self.s
        self.columns().wait_recv()
        total = r["column_got"][s, 0].astype(F32)
        for i in range(1, self.at.zs):
            total = total + r["column_got"][s, i].astype(F32)
        r["total"][self.total_rows(self.at.q), :] = total.astype(BF16)
        for d in self.at.plane_order:
            self.gather(d).start()

    def step_hand_over(self):
        self.gathers().wait_recv()
        self.hand_over().start()

    def step_end(self):
        self.hand_over().wait_recv()
        self.pair().wait_send()
        self.scatters().wait_send()
        self.columns().wait_send()
        self.gathers().wait_send()
        self.hand_over().wait_send()


class Direct:
    def __init__(self, s, spot, r):
        self.s, self.at, self.r = s, spot, r
        self.block = HALF // spot.all

    def sems(self, phase):
        return self.r["direct_send"].at[self.s, phase], self.r["direct_got"].at[self.s, phase]

    def rows(self, g):
        first = 2 * HALF + self.s * HALF + g * self.block
        return pl.ds(pl.multiple_of(first, self.block), self.block)

    def scatter(self, d):
        r, s = self.r, self.s
        src = r["pack"].at[self.rows(self.at.gs[d])]
        return remote(src, r["all_got"].at[s, d - 1], *self.sems(0), self.at.in_both(d))

    def scatters(self):
        ref = self.r["all_got"].at[self.s]
        return remote(ref, ref, *self.sems(0), self.at.other_core())

    def column(self, d):
        r, s = self.r, self.s
        dst = r["height_got"].at[s, self.at.z]
        return remote(r["part_sum"].at[s], dst, *self.sems(1), self.at.in_column(d))

    def columns(self):
        ref = self.r["height_got"].at[self.s, pl.ds(0, self.at.zs - 1)]
        return remote(ref, ref, *self.sems(1), self.at.other_core())

    def gather(self, d):
        ref = self.r["total"].at[self.rows(self.at.g)]
        return remote(ref, ref, *self.sems(2), self.at.in_both(d))

    def gathers(self):
        rows = (self.at.all - 1) * self.block
        ref = self.r["total"].at[pl.ds(2 * HALF + self.s * HALF, rows)]
        return remote(ref, ref, *self.sems(2), self.at.other_core())

    def step_scatter(self):
        for d in self.at.both_order:
            self.scatter(d).start()

    def step_column(self):
        r, s = self.r, self.s
        self.scatters().wait_recv()
        total = r["pack"][self.rows(self.at.g), :].astype(F32)
        for d in range(self.at.all - 1):
            total = total + r["all_got"][s, d].astype(F32)
        total = total.astype(BF16)
        r["part_sum"][s] = total
        r["height_got"][s, self.at.z] = total
        for d in self.at.column_order:
            self.column(d).start()

    def step_gather(self):
        r, s = self.r, self.s
        self.columns().wait_recv()
        total = r["height_got"][s, 0].astype(F32)
        for i in range(1, self.at.zs):
            total = total + r["height_got"][s, i].astype(F32)
        r["total"][self.rows(self.at.g), :] = total.astype(BF16)
        for d in self.at.both_order:
            self.gather(d).start()

    def step_end(self):
        self.gathers().wait_recv()
        self.scatters().wait_send()
        self.columns().wait_send()
        self.gathers().wait_send()


def layer_kernel(sizes, names, *refs):
    r = dict(zip(names, refs, strict=True))
    spot = Spot(*sizes)

    def get(*wanted):
        return [r[name] for name in wanted]

    barrier = pltpu.get_barrier_semaphore()

    def greet(to):
        pl.semaphore_signal(barrier, inc=1, device_id=to, device_id_type=MESH)

    for frame_too in (False, True):
        for step in (-1, 1):
            greet(spot.beside(frame_too, step))
    for d in range(1, spot.plane):
        greet(spot.in_plane(d))
    for d in range(1, spot.zs):
        greet(spot.in_column(d))

    bit = lax.rem(spot.frame, 2)
    sh, rh = r["sh"], r["rh"]
    split, join = get("split", "join")

    def outward(kind, pick):
        ends = [
            (3 - bit, 2 * bit + 1, spot.beside(True, -1)),
            (1 - bit, 2 * bit, spot.beside(True, 0)),
            (2 + bit, 2 * bit + 1, spot.beside(False, -1)),
        ]
        return [
            remote(*pick(src, dst), sh.at[kind, i], rh.at[kind, i], to)
            for i, (src, dst, to) in enumerate(ends)
        ]

    def homeward(kind, pick):
        ends = [
            (2 * (1 - bit) + 1, 2 + bit, spot.beside(True, 1)),
            (2 * (1 - bit), bit, spot.beside(True, 0)),
            (2 * bit + 1, 2 + bit, spot.beside(False, 1)),
        ]
        return [
            remote(*pick(src, dst), sh.at[kind, i], rh.at[kind, i], to)
            for i, (src, dst, to) in enumerate(ends)
        ]

    x_send, x_got, d_send, d_got = get("x_send", "x_got", "d_send", "d_got")
    g_send, g_got = get("g_send", "g_got")
    x_copies = [
        outward(u, lambda a, b, u=u: (x_send.at[u, a], x_got.at[u, b])) for u in range(2)
    ]
    d_copies = outward(2, lambda a, b: (d_send.at[:, a], d_got.at[:, b]))
    g_copies = homeward(3, lambda a, b: (g_send.at[:, a], g_got.at[:, b]))
    copies = x_copies[0] + x_copies[1] + d_copies + g_copies

    make_perms(split, join)
    for name, rows in (("x_slab", "x"), ("d_slab", "d_out")):
        for part in range(2):
            r[name][pl.ds(part * L + C, L - C), :] = jnp.zeros((L - C, HALF), BF16)
        to_slab(r[name], r[rows].at[0, 0])
    split_blocks(r["x_slab"], split, x_send)
    for u in range(2):
        x_got[u, 2 * bit] = x_send[u, bit]
    split_blocks(r["d_slab"], split, d_send)
    for u in range(2):
        d_got[u, 2 * bit] = d_send[u, bit]
    make_masks(*get("mask_h", "mask_f"))
    make_weights(
        *get("w_self", "w_mut", "w_proj", "f1", "f2", "w_down"),
        *get("wn", "wt", "proj", "proj_t", "fc_n", "fc_t", "down"),
    )
    make_gain(r["g1"], r["col1"])
    make_gain(r["g2"], r["col2"])
    pl.semaphore_wait(barrier, 4 + spot.plane - 1 + spot.zs - 1)
    for copy in x_copies[0] + x_copies[1]:
        copy.start()
    for u in range(2):
        for copy in x_copies[u]:
            copy.wait_recv()
        if u == 1:
            for copy in d_copies:
                copy.start()
        join_blocks(u, x_got, join, r["win"])
        norm_one(u, *get("win", "col1", "n_cm", "n_tm"))
        project(u, *get("wt", "wn", "n_cm", "n_tm", "cm", "tm"))
    attend(*get("cm", "tm", "mask_h", "mask_f", "probs", "joined"))
    for copy in d_copies:
        copy.wait_recv()
    for u in range(2):
        join_blocks(u, d_got, join, r["d_win"])
    feed_forward(
        *get("win", "d_win", "joined", "col2", "proj", "proj_t", "fc_n", "fc_t", "down"),
        *get("hid", "dup", "n2", "datt", "dres", "dj", "acc"),
    )
    early_grads(*get("hid", "dup", "n2", "joined", "datt", "d_win", "acc", "pack"))
    early, cross, last = Stream(0, spot, r), Direct(0, spot, r), Direct(1, spot, r)
    early.step_pair()

    def in_cross(p):
        @pl.when(p == 3)
        def _():
            early.step_scatter()

    def in_self(p):
        @pl.when(p == 5)
        def _():
            early.step_column()

    back = get("cm", "tm", "mask_h", "probs", "dj", "dq", "d_tm")
    back_cross(*back, r["mask_f"], in_cross)
    cross_grads(*get("n_cm", "dq", "d_tm", "wn", "pack", "acc"))
    cross.step_scatter()
    back_self(*back, in_self)
    self_grads(*get("n_cm", "dq", "d_tm", "wn", "pack", "acc", "col1"))
    last.step_scatter()
    finish(0, 4, *get("win", "col1", "wn", "dq", "d_tm", "dres", "gi"))
    gi, out = get("gi", "out")
    for u in range(2):
        blocks = nt(gi[:, pl.ds(u * HALF, HALF)], join[...]).astype(BF16)
        for s in range(4):
            g_send[u, s] = blocks[:, s * L : (s + 1) * L]
        g_got[u, bit] = g_send[u, 2 * bit]
    cross.step_column()
    early.step_gather()
    last.step_column()
    for copy in g_copies:
        copy.start()
    cross.step_gather()
    last.step_gather()
    for copy in g_copies:
        copy.wait_recv()
    for part in range(2):
        both = [g_got[u, 2 * part + half] for half in range(2) for u in range(2)]
        rows = nt(jnp.concatenate(both, axis=1), split[...]).astype(BF16)
        for i in range(4):
            out[4 * (1 - part) + i] = rows[:C, i * W : (i + 1) * W]
    early.step_hand_over()
    cross.step_end()
    early.step_end()
    last.step_end()
    for copy in copies:
        copy.wait_send()


def unpack_kernel(scale, total, gi, out, o1, o_self, o_mut, o_proj, o2, o_f1, o_f2, o_down):
    def block(i):
        return total[pl.ds(i * L, L), :].astype(F32) * scale

    def beside(parts):
        wide_parts = [
            jnp.concatenate([p, jnp.zeros((L, 2 * L), F32)], axis=1) for p in parts
        ]
        joined = wide_parts[0] + pltpu.roll(wide_parts[1], C, 1) + pltpu.roll(wide_parts[2], 2 * C, 1)
        return joined[:C, : 3 * C]

    b = [block(i) for i in range(8 + 3 + 4)]
    o_down[...] = jnp.concatenate([b[0], b[1]], axis=0)[:MLP, :C]
    o2[...] = b[1][MLP - L : MLP - L + 1, :C]
    o_f1[...] = jnp.concatenate([b[2], b[3]], axis=1)[:C, :MLP]
    o_f2[...] = jnp.concatenate([b[4], b[5]], axis=1)[:C, :MLP]
    o_proj[...] = jnp.concatenate([b[6][:C], b[7][:C]], axis=0)[:, :C]
    o1[...] = b[12][C : C + 1, :C]
    o_mut[...] = beside(b[8:11])
    o_self[...] = beside(b[12:15])
    out[0, 0] = gi[...]


def vmem(*shape, dtype=BF16):
    return pltpu.VMEM(shape, dtype)


def shape(*dims, dtype=BF16):
    return jax.ShapeDtypeStruct(dims, dtype)


def in_vmem(count):
    return [pl.BlockSpec(memory_space=pltpu.VMEM)] * count


def solution(mesh):
    clips, frames, rows = mesh.shape["clip"], mesh.shape["frame"], mesh.shape["row"]
    zs = min(8, rows // 2)
    xs = rows // (2 * zs)
    sizes = (clips, frames, xs, zs)
    plane = clips * frames * xs
    dma = pltpu.SemaphoreType.DMA
    ins = ["x", "d_out", "g1", "w_self", "w_mut", "w_proj", "g2", "f1", "f2", "w_down"]
    scratch = dict(
        split=vmem(HALF, HALF), join=vmem(HALF, HALF), x_slab=vmem(2 * L, HALF), d_slab=vmem(2 * L, HALF),
        x_send=vmem(2, 4, L, L), x_got=vmem(2, 4, L, L), d_send=vmem(2, 4, L, L), d_got=vmem(2, 4, L, L),
        g_send=vmem(2, 4, L, L), g_got=vmem(2, 4, L, L), win=vmem(L, T), d_win=vmem(L, T),
        mask_h=vmem(L, HEADS * L), mask_f=vmem(L, HEADS * L),
        wn=vmem(L, 6 * L), wt=vmem(6 * L, L), proj=vmem(2 * L, L), proj_t=vmem(L, 2 * L),
        fc_n=vmem(L, 2 * M), fc_t=vmem(2 * M, L), down=vmem(M, L),
        col1=vmem(C, L, dtype=F32), col2=vmem(C, L, dtype=F32), acc=vmem(C, L, dtype=F32),
        n_cm=vmem(L, T), n_tm=vmem(T, L), cm=vmem(6 * L, T), tm=vmem(T, 4 * L),
        probs=vmem(T // L, 2 * L, HEADS * L), joined=vmem(2 * L, T),
        hid=vmem(M, T), dup=vmem(2 * M, T), n2=vmem(L, T), datt=vmem(L, T),
        dres=vmem(C, T, dtype=F32), dj=vmem(2 * L, T),
        dq=vmem(2 * L, T), d_tm=vmem(T, 4 * L), gi=vmem(L, T),
        pack=vmem(ROWS, L), pair_got=vmem(1, HALF, L), chip=vmem(1, plane, HALF // plane, L),
        plane_got=vmem(1, plane - 1, HALF // plane, L), mine=vmem(1, HALF // plane, L),
        column_got=vmem(1, zs, HALF // plane, L),
        sh=dma((4, 3)), rh=dma((4, 3)), sem_send=dma((1, 5)), sem_got=dma((1, 5)),
        direct_send=dma((2, 3)), direct_got=dma((2, 3)), all_got=vmem(2, 2 * plane - 1, HALF // (2 * plane), L),
        part_sum=vmem(2, HALF // (2 * plane), L), height_got=vmem(2, zs, HALF // (2 * plane), L),
    )
    names = [*ins, "out", "total", *scratch]

    def on_device(x, d_out, g1, w_self, w_mut, w_proj, g2, f1, f2, w_down):
        g1, g2 = g1.reshape(1, C), g2.reshape(1, C)
        gi, total = pl.pallas_call(
            lambda *refs: layer_kernel(sizes, names, *refs),
            out_shape=(shape(8, C, W), shape(ROWS, L)),
            in_specs=in_vmem(10),
            out_specs=tuple(in_vmem(2)),
            scratch_shapes=list(scratch.values()),
            compiler_params=pltpu.CompilerParams(
                collective_id=0, has_side_effects=True, vmem_limit_bytes=56 * 2**20
            ),
        )(x, d_out, g1, w_self, w_mut, w_proj, g2, f1, f2, w_down)
        scale = float(T * rows * frames * clips) ** -0.5
        out = pl.pallas_call(
            lambda *refs: unpack_kernel(scale, *refs),
            out_shape=(
                shape(1, 1, 8, C, W), shape(1, C, dtype=F32), shape(C, 3 * C, dtype=F32),
                shape(C, 3 * C, dtype=F32), shape(2 * C, C, dtype=F32), shape(1, C, dtype=F32),
                shape(C, MLP, dtype=F32), shape(C, MLP, dtype=F32), shape(MLP, C, dtype=F32),
            ),
            in_specs=in_vmem(2),
            out_specs=tuple(in_vmem(9)),
            compiler_params=pltpu.CompilerParams(vmem_limit_bytes=56 * 2**20),
        )(total, gi)
        out = list(out)
        out[1], out[5] = out[1].reshape(C), out[5].reshape(C)
        return tuple(out)

    whole = P("clip", "frame", "row", None, None)
    return jax.shard_map(
        on_device,
        mesh=mesh,
        in_specs=(whole, whole) + (P(),) * 8,
        out_specs=(whole,) + (P(),) * 8,
        check_vma=False,
    )
```
